128 devices in a mesh: rows: 16 (over y, x_lo, core), cols: 8 (over z, x_hi).
Axes of the slice: x: 4 (x_hi: 2, x_lo: 2; x = x_hi * 2 + x_lo), y: 4, z: 4, core: 2. Of those that a mesh axis runs over, the one named last changes fastest.
Arguments:
- latents: bfloat16 [1, 256, 256, 192], P(None, 'rows', 'cols'), may hold values from -200 to 200
- actions: int32 [1, 16], replicated, may hold values from 0 to 255
- action_table: bfloat16 [256, 192], replicated, may hold values from -16 to 16
- offsets: int32 [2, 2], replicated, may hold values from 1 to 8, as said below
- fine_gain: float32 [192], replicated, may hold values from 0.1 to 1.9
- fine_qkv: bfloat16 [192, 576], replicated, may hold values from -0.4375 to 0.4375
- fine_bias: float32 [6, 64, 64], replicated, may hold values from -3 to 320
- fine_proj: bfloat16 [192, 192], replicated, may hold values from -0.4375 to 0.4375
- merge_gain: float32 [768], replicated, may hold values from 0.1 to 1.9
- merge_weight: bfloat16 [768, 384], replicated, may hold values from -0.21875 to 0.21875
- coarse_gain: float32 [384], replicated, may hold values from 0.1 to 1.9
- coarse_qkv: bfloat16 [384, 1152], replicated, may hold values from -0.3125 to 0.3125
- coarse_bias: float32 [12, 64, 64], replicated, may hold values from -3 to 320
- coarse_proj: bfloat16 [384, 384], replicated, may hold values from -0.3125 to 0.3125
- head_weight: bfloat16 [384, 768], replicated, may hold values from -0.3125 to 0.3125
- cotangent: bfloat16 [1, 256, 256, 192], P(None, 'rows', 'cols'), may hold values from -0.046875 to 0.046875
Outputs:
- prediction: bfloat16 [1, 256, 256, 192], P(None, 'rows', 'cols')
- grad_fineqkv: float32 [192, 576], replicated
- grad_fineproj: float32 [192, 192], replicated
- grad_merge: float32 [768, 384], replicated
- grad_coarseqkv: float32 [384, 1152], replicated
- grad_coarseproj: float32 [384, 384], replicated
- grad_head: float32 [384, 768], replicated
The draws below stay inside these ranges and needn't reach their ends.
Inputs may be any that keep to these rules, and one draw needn't show every extreme that they name: offsets[0] is the shift of the fine map and offsets[1] that of the merged map, in cells of that map; at least one entry equals 8.
All inputs are finite; a program needn't handle non-finite values.
Results may differ from the reference program's by a relative error of at most 0.02.
Values may be sent and summed in bfloat16 or wider, within the bound.
A program may use at most 128 MiB of HBM per device.

```python
import math
import jax
import jax.numpy as jnp
from jax import lax

P_SIZE = 1
WIN = 8
HEADS1 = 6
ACTS = 16
ACT_VOCAB = 256
C1 = 192
C2 = 384
HEADS2 = 12
NH = 256
NW = 256


def draw_latents(key, part):
    key = jax.random.fold_in(key, 11)
    streams = jax.random.split(key, 3)
    full_shape = (P_SIZE, NH, NW, C1)
    jitter = jnp.clip(jax.random.normal(streams[0], full_shape, jnp.float32), -4.0, 4.0)
    log_top = math.log(10.0)
    row_scale = jnp.exp(jax.random.uniform(streams[1], (P_SIZE, NH, NW, 1), jnp.float32) * log_top)
    channel_scale = jnp.exp(jax.random.uniform(streams[2], (1, 1, 1, C1), jnp.float32) * math.log(10.0))
    return (0.3 * jitter * row_scale * channel_scale).astype(jnp.bfloat16)


def draw_offsets(key, part):
    key = jax.random.fold_in(key, 23)
    pick_key, spot_key = jax.random.split(key)
    values = jax.random.randint(pick_key, (2, 2), 1, WIN + 1)
    chosen = jax.random.randint(spot_key, (), 0, 4)
    places = jnp.arange(4, dtype=jnp.int32).reshape(2, 2)
    return jnp.where(places == chosen, WIN, values).astype(jnp.int32)


def draw_fine_bias(key, part):
    key = jax.random.fold_in(key, 31)
    streams = jax.random.split(key, 1)
    return jnp.clip(jax.random.normal(streams[0], (HEADS1, WIN * WIN, WIN * WIN), jnp.float32), -3.0, 3.0)


def draw_coarse_bias(key, part):
    key = jax.random.fold_in(key, 37)
    streams = jax.random.split(key, 1)
    return jnp.clip(jax.random.normal(streams[0], (HEADS2, WIN * WIN, WIN * WIN), jnp.float32), -3.0, 3.0)


def set_ends(drawn, stream_key, smallest, high):
    extent = drawn.shape
    index_at = [jax.random.randint(jax.random.fold_in(stream_key, axis), (), 0, extent[axis]) for axis in range(len(extent))]
    drawn = drawn.at[tuple(index_at)].set(smallest)
    longest = extent.index(max(extent))
    index_at[longest] = (index_at[longest] + 1) % extent[longest]
    return drawn.at[tuple(index_at)].set(high)


def block_scale(stream_key, shape, shards, least, largest):
    def one(axis_at, shards_of):
        steps = jax.random.uniform(jax.random.fold_in(jax.random.fold_in(stream_key, 6), axis_at), (shards_of,), jnp.float32, least / len(shards), largest / len(shards))
        return jnp.repeat(jnp.exp(steps), shape[axis_at] // shards_of).reshape((-1,) + (1,) * (len(shape) - axis_at - 1))

    level = one(*shards[0])
    for cut in shards[1:]:
        level = level * one(*cut)
    return level


def bell_draw(own_key, extent, width, reach, cuts=(), kind=jnp.bfloat16):
    values = jax.random.normal(own_key, extent, jnp.float32) * width
    if len(cuts) > 0:
        values = block_scale(own_key, extent, cuts, -0.22, 0.18) * values
    return jnp.clip(values, min=-reach, max=reach).astype(kind)


def setup_inputs(seed: int = 0) -> dict:
    keys = jax.random.split(jax.random.key(seed), 17)
    latents = draw_latents(jax.random.fold_in(keys[16], 71), 0)
    actions = set_ends(jax.random.randint(keys[1], (P_SIZE, ACTS), 0, ACT_VOCAB), jax.random.fold_in(keys[1], 1), 0, ACT_VOCAB - 1).astype(jnp.int32)
    action_table = bell_draw(keys[2], (ACT_VOCAB, C1), 4.0, 16.0)
    offsets = draw_offsets(jax.random.fold_in(keys[16], 71), 0)
    fine_gain = jnp.clip(1.0 + 0.18 * jax.random.normal(keys[4], (C1,), jnp.float32), 0.1, 1.9)
    fine_qkv = bell_draw(keys[5], (C1, 3 * C1), C1 ** -0.5, 0.4375)
    fine_bias = draw_fine_bias(jax.random.fold_in(keys[16], 71), 0)
    fine_proj = bell_draw(keys[7], (C1, C1), C1 ** -0.5, 0.4375)
    merge_gain = jnp.clip(1.0 + 0.18 * jax.random.normal(keys[8], (4 * C1,), jnp.float32), 0.1, 1.9)
    merge_weight = bell_draw(keys[9], (4 * C1, C2), (4 * C1) ** -0.5, 0.21875)
    coarse_gain = jnp.clip(1.0 + 0.18 * jax.random.normal(keys[10], (C2,), jnp.float32), 0.1, 1.9)
    coarse_qkv = bell_draw(keys[11], (C2, 3 * C2), C2 ** -0.5, 0.3125)
    coarse_bias = draw_coarse_bias(jax.random.fold_in(keys[16], 71), 0)
    coarse_proj = bell_draw(keys[13], (C2, C2), C2 ** -0.5, 0.3125)
    head_weight = bell_draw(keys[14], (C2, 4 * C1), C2 ** -0.5, 0.3125)
    cotangent = bell_draw(keys[15], (P_SIZE, NH, NW, C1), (2 * (P_SIZE * NH * NW) ** -0.5), 0.046875, ((1, 16), (2, 8)))
    return dict(latents=latents, actions=actions, action_table=action_table, offsets=offsets, fine_gain=fine_gain, fine_qkv=fine_qkv, fine_bias=fine_bias, fine_proj=fine_proj, merge_gain=merge_gain, merge_weight=merge_weight, coarse_gain=coarse_gain, coarse_qkv=coarse_qkv, coarse_bias=coarse_bias, coarse_proj=coarse_proj, head_weight=head_weight, cotangent=cotangent)


epsilon = 1e-05

def product(form, left, right):
    return jnp.einsum(form, left.astype(jnp.float32), right.astype(jnp.float32))

def rounded(value):
    return lax.optimization_barrier(value.astype(jnp.bfloat16))

def normalize(source, gain):
    average = lax.optimization_barrier(jnp.mean(source, axis=-1, keepdims=True))
    centred = source - average
    inverse = lax.rsqrt(lax.optimization_barrier(jnp.mean(centred * centred, axis=-1, keepdims=True)) + epsilon)
    standard = centred * inverse
    return (standard * gain, standard, inverse)

def normalize_back(upstream, standard, inverse, gain):
    scaled = upstream * gain
    return inverse * (scaled - lax.optimization_barrier(jnp.mean(scaled, axis=-1, keepdims=True)) - standard * lax.optimization_barrier(jnp.mean(scaled * standard, axis=-1, keepdims=True)))

def pair_up(source):
    plans, height, breadth, channels = source.shape
    blocks = source.reshape(plans, height // 2, 2, breadth // 2, 2, channels)
    return blocks.transpose(0, 1, 3, 2, 4, 5).reshape(plans, height // 2, breadth // 2, 4 * channels)

def pull_apart(source):
    plans, height, breadth, channels = source.shape
    blocks = source.reshape(plans, height, breadth, 2, 2, channels // 4)
    return blocks.transpose(0, 1, 3, 2, 4, 5).reshape(plans, 2 * height, 2 * breadth, channels // 4)

def roll_ahead(source, shift_pair):
    moved = jnp.roll(source, -shift_pair[0], axis=1)
    return jnp.roll(moved, -shift_pair[1], axis=2)

def roll_behind(source, shift_pair):
    moved = jnp.roll(source, shift_pair[0], axis=1)
    return jnp.roll(moved, shift_pair[1], axis=2)

def attend(rolled, qkv_weight, position_bias, proj_weight):
    plans, height, breadth, channels = rolled.shape
    head_count = position_bias.shape[0]
    head_depth = channels // head_count
    tokens_in = rolled.reshape(-1, channels)
    packed = rounded(jnp.dot(tokens_in, qkv_weight, preferred_element_type=jnp.float32))
    packed_view = packed.reshape(plans, height // WIN, WIN, breadth // WIN, WIN, 3, head_count, head_depth)
    queries = packed_view[:, :, :, :, :, 0]
    key_vecs = packed_view[:, :, :, :, :, 1]
    values = packed_view[:, :, :, :, :, 2]
    window_grid = (plans, height // WIN, breadth // WIN, head_count, WIN, WIN, WIN, WIN)
    scores = product('pawbxhe,pavbyhe->pabhwxvy', queries, key_vecs)
    scores = scores.reshape(window_grid[:4] + (WIN * WIN, WIN * WIN)) * head_depth ** (-0.5) + position_bias
    softmax_out = jax.nn.softmax(scores, axis=-1)
    weights = rounded(softmax_out).reshape(window_grid)
    mixed_out = rounded(product('pabhwxvy,pavbyhe->pawbxhe', weights, values)).reshape(-1, channels)
    projected = rounded(jnp.dot(mixed_out, proj_weight, preferred_element_type=jnp.float32))
    return (projected.reshape(plans, height, breadth, channels), (tokens_in, queries, key_vecs, values, softmax_out, weights, mixed_out))

def attend_back(upstream, saved, proj_weight):
    tokens_in, queries, key_vecs, values, softmax_out, weights, mixed_out = saved
    channels = mixed_out.shape[1]
    head_depth = queries.shape[-1]
    grad_flat = upstream.reshape(-1, channels)
    grad_proj = product('tc,td->cd', mixed_out, grad_flat)
    grad_mixed = rounded(product('td,cd->tc', grad_flat, proj_weight)).reshape(queries.shape)
    grad_weights = rounded(product('pawbxhe,pavbyhe->pabhwxvy', grad_mixed, values)).astype(jnp.float32)
    grad_weights = grad_weights.reshape(softmax_out.shape)
    grad_scores = softmax_out * (grad_weights - lax.optimization_barrier(jnp.sum(softmax_out * grad_weights, axis=-1, keepdims=True)))
    grad_scores = rounded(grad_scores * head_depth ** (-0.5)).reshape(weights.shape)
    grad_queries = product('pabhwxvy,pavbyhe->pawbxhe', grad_scores, key_vecs)
    grad_keys = product('pabhwxvy,pawbxhe->pavbyhe', grad_scores, queries)
    grad_values = product('pabhwxvy,pawbxhe->pavbyhe', weights, grad_mixed)
    grad_packed = rounded(jnp.stack([grad_queries, grad_keys, grad_values], axis=5)).reshape(-1, 3 * channels)
    grad_qkv = product('tc,td->cd', tokens_in, grad_packed)
    return (grad_qkv, grad_proj, grad_packed)

def reference(latents, actions, action_table, offsets, fine_gain, fine_qkv, fine_bias, fine_proj, merge_gain, merge_weight, coarse_gain, coarse_qkv, coarse_bias, coarse_proj, head_weight, cotangent):
    one_hot = (actions[:, :, None] == jnp.arange(ACT_VOCAB, dtype=jnp.int32)[None, None, :]).astype(jnp.float32)
    counts = lax.optimization_barrier(jnp.sum(one_hot, axis=1)) / ACTS
    condition = jnp.dot(counts, action_table.astype(jnp.float32), precision=lax.Precision.HIGHEST)
    fine_shift = offsets[0]
    coarse_shift = offsets[1]

    def one_plan(plan_items):
        latent, cond_row, cotangent_row = plan_items
        fine_residual = latent[None].astype(jnp.float32) + cond_row
        fine_normed = rounded(normalize(fine_residual, fine_gain)[0])
        fine_rolled = roll_ahead(fine_normed, fine_shift)
        fine_attn, fine_saved = attend(fine_rolled, fine_qkv, fine_bias, fine_proj)
        fine_next = rounded(fine_residual + roll_behind(fine_attn, fine_shift).astype(jnp.float32))
        merged = pair_up(fine_next)
        merge_full, merge_unit, merge_inverse = normalize(merged.astype(jnp.float32), merge_gain)
        merge_flat = rounded(merge_full).reshape(-1, merged.shape[-1])
        coarse_shape = merged.shape[:3] + (merge_weight.shape[1],)
        coarse_residual = rounded(jnp.dot(merge_flat, merge_weight, preferred_element_type=jnp.float32)).reshape(coarse_shape)
        coarse_float = coarse_residual.astype(jnp.float32)
        coarse_full, coarse_unit, coarse_inverse = normalize(coarse_float, coarse_gain)
        coarse_rolled = roll_ahead(rounded(coarse_full), coarse_shift)
        coarse_attn, coarse_saved = attend(coarse_rolled, coarse_qkv, coarse_bias, coarse_proj)
        coarse_next = rounded(coarse_float + roll_behind(coarse_attn, coarse_shift).astype(jnp.float32))
        coarse_flat = coarse_next.reshape(-1, coarse_shape[3])
        head_out = rounded(jnp.dot(coarse_flat, head_weight, preferred_element_type=jnp.float32))
        prediction = pull_apart(head_out.reshape(merged.shape))
        grad_out = pair_up(cotangent_row[None]).reshape(-1, merged.shape[-1])
        grad_head = product('tc,td->cd', coarse_flat, grad_out)
        grad_next = rounded(product('td,cd->tc', grad_out, head_weight)).reshape(coarse_shape)
        coarse_grad = roll_ahead(grad_next, coarse_shift)
        grad_coarseqkv, grad_coarseproj, coarse_packed = attend_back(coarse_grad, coarse_saved, coarse_proj)
        grad_rolled = rounded(product('td,cd->tc', coarse_packed, coarse_qkv)).reshape(coarse_rolled.shape)
        grad_normed = roll_behind(grad_rolled, coarse_shift)
        grad_residual = rounded(grad_next.astype(jnp.float32) + normalize_back(grad_normed.astype(jnp.float32), coarse_unit, coarse_inverse, coarse_gain)).reshape(-1, coarse_shape[3])
        grad_merge = product('tc,td->cd', merge_flat, grad_residual)
        merge_grad = rounded(product('td,cd->tc', grad_residual, merge_weight)).reshape(merged.shape)
        merged_grad = rounded(normalize_back(merge_grad.astype(jnp.float32), merge_unit, merge_inverse, merge_gain))
        fine_grad = roll_ahead(pull_apart(merged_grad), fine_shift)
        grad_fineqkv, grad_fineproj, fine_packed = attend_back(fine_grad, fine_saved, fine_proj)
        return (prediction[0], (grad_fineqkv, grad_fineproj, grad_merge, grad_coarseqkv, grad_coarseproj, grad_head))
    predictions, gradients = lax.map(one_plan, (latents, condition, cotangent))
    return (predictions, lax.optimization_barrier(jnp.sum(gradients[0], axis=0)), lax.optimization_barrier(jnp.sum(gradients[1], axis=0)), lax.optimization_barrier(jnp.sum(gradients[2], axis=0)), lax.optimization_barrier(jnp.sum(gradients[3], axis=0)), lax.optimization_barrier(jnp.sum(gradients[4], axis=0)), lax.optimization_barrier(jnp.sum(gradients[5], axis=0)))
```

```python
import jax
import jax.numpy as jnp
from jax import lax
from jax.experimental import pallas as pl
from jax.experimental.pallas import tpu as pltpu
from jax.sharding import PartitionSpec as P

MESH = pl.DeviceIdType.MESH
BF = jnp.bfloat16
F32 = jnp.float32
EPS = 1e-05
SCALE = 32 ** (-0.5)
FINE_GROUPS = ((0, 128, 4), (128, 64, 2))
COARSE_GROUPS = ((0, 128, 4), (128, 128, 4), (256, 128, 4))
UNITS = (224, 224, 160, 96)
USED = (216, 216, 144, 72)
ORDERS = (("x", "y", "z"), ("y", "z", "x"), ("z", "x", "y"), ("x", "y", "z"))


def mm(a, b):
    return lax.dot_general(a, b, (((1,), (0,)), ((), ())), preferred_element_type=F32)


def mm_nt(a, b):
    return lax.dot_general(a, b, (((1,), (1,)), ((), ())), preferred_element_type=F32)


def mm_tn(a, b):
    return lax.dot_general(a, b, (((0,), (0,)), ((), ())), preferred_element_type=F32)


def norm(x):
    centred = x - jnp.mean(x, axis=-1, keepdims=True)
    inverse = lax.rsqrt(jnp.mean(centred * centred, axis=-1, keepdims=True) + EPS)
    return centred * inverse, inverse


def norm_back(upstream, unit, inverse, gain):
    e = upstream * gain
    return inverse * (
        e - jnp.mean(e, axis=-1, keepdims=True) - unit * jnp.mean(e * unit, axis=-1, keepdims=True)
    )


def head_masks(width, heads, dtype):
    lane = lax.broadcasted_iota(jnp.int32, (1, width), 1) // 32
    return [jnp.where(lane == h, 1.0, 0.0).astype(dtype) for h in range(heads)]


def spread(x, masks):
    return jnp.concatenate([x * m for m in masks], axis=0)


def fold(x, masks):
    total = x[:64] * masks[0]
    for h in range(1, len(masks)):
        total = total + x[64 * h : 64 * h + 64] * masks[h]
    return total


def probabilities(q, k, bias, masks):
    s = mm_nt(k, spread(q, masks)) * SCALE + bias
    e = jnp.exp(s - jnp.max(s, axis=0, keepdims=True))
    return e / jnp.sum(e, axis=0, keepdims=True)


def select(rows_out, cols_in, picks):
    x = lax.broadcasted_iota(jnp.int32, (rows_out, cols_in), 0)
    u = lax.broadcasted_iota(jnp.int32, (rows_out, cols_in), 1)
    return jnp.where(picks(x) == u, 1.0, 0.0).astype(F32).astype(BF)


def folded_place(u):
    v = u & 15
    return (u - v) + (v & 1) * 8 + (v >> 1)


def true_place(p):
    v = p & 15
    return (p - v) + (v & 7) * 2 + (v >> 3)


def units(x):
    return x.reshape(x.shape[0] // 16, 16, 128)


class Net:
    def __init__(self, send, recv):
        self.r = lax.axis_index("rows")
        self.c = lax.axis_index("cols")
        r, c = self.r, self.c
        self.core = lax.rem(r, 2)
        xlo = lax.rem(r // 2, 2)
        self.y = r // 4
        self.z = c // 2
        xhi = lax.rem(c, 2)
        self.x = xhi * 2 + xlo
        self.low = lax.rem(r, 4)
        self.xhi = xhi
        self.send, self.recv = send, recv
        self.count = 0
        self.copies = []

    def near(self, dr, dc):
        return (lax.rem(self.r + dr + 16, 16), lax.rem(self.c + dc + 8, 8))

    def place(self, axis):
        return {"x": self.x, "y": self.y, "z": self.z}[axis]

    def peer(self, axis, index):
        if axis == "y":
            return (index * 4 + self.low, self.c)
        if axis == "z":
            return (self.r, index * 2 + self.xhi)
        return (self.y * 4 + lax.rem(index, 2) * 2 + self.core, self.z * 2 + index // 2)

    def sibling(self):
        return (self.r + 1 - 2 * self.core, self.c)

    def start(self, source, target, device):
        n = self.count
        self.count += 1
        copy = pltpu.make_async_remote_copy(
            src_ref=source,
            dst_ref=target,
            send_sem=self.send.at[n],
            recv_sem=self.recv.at[n],
            device_id=device,
            device_id_type=MESH,
        )
        copy.start()
        self.copies.append(copy)
        return copy

    def barrier(self):
        sem = pltpu.get_barrier_semaphore()
        others = [self.near(a, b) for a in (-1, 0, 1) for b in (-1, 0, 1) if (a, b) != (0, 0)]
        others.append(self.sibling())
        for axis in "xyz":
            others += [self.peer(axis, lax.rem(self.place(axis) + k, 4)) for k in (1, 2, 3)]
        for device in others:
            pl.semaphore_signal(sem, inc=1, device_id=device, device_id_type=MESH)
        pl.semaphore_wait(sem, len(others))


class Reduce:
    def __init__(self, net, order, terms, got_core, got_a, sum_a, got_b, sum_b, got_c, result):
        self.net, self.order = net, order
        self.terms, self.got_core, self.got_a, self.sum_a = terms, got_core, got_a, sum_a
        self.got_b, self.sum_b, self.got_c, self.result = got_b, sum_b, got_c, result
        self.n = terms.shape[0]
        self.stage = 0
        self.flight = []

    def step(self):
        getattr(self, "step%d" % self.stage)()
        self.stage += 1

    def finish(self):
        while self.stage < 8:
            self.step()

    def arrive(self):
        for copy in self.flight:
            copy.wait_recv()

    def step0(self):
        net, half = self.net, self.n // 2
        self.flight = [
            net.start(self.terms.at[pl.ds((1 - net.core) * half, half)], self.got_core, net.sibling())
        ]

    def step1(self):
        net, half, part = self.net, self.n // 2, self.n // 8
        self.arrive()
        own = self.terms[pl.ds(net.core * half, half)].astype(F32)
        self.sum_a[...] = (own + self.got_core[...].astype(F32)).astype(BF)
        me = net.place(self.order[0])
        self.flight = []
        for k in (1, 2, 3):
            to = lax.rem(me + k, 4)
            self.flight.append(
                net.start(
                    self.sum_a.at[pl.ds(to * part, part)],
                    self.got_a.at[k - 1],
                    net.peer(self.order[0], to),
                )
            )

    def step2(self):
        net, part, piece = self.net, self.n // 8, self.n // 32
        self.arrive()
        total = self.sum_a[pl.ds(net.place(self.order[0]) * part, part)].astype(F32)
        for k in range(3):
            total = total + self.got_a[k].astype(F32)
        self.sum_b[...] = total.astype(BF)
        me = net.place(self.order[1])
        self.flight = []
        for k in (1, 2, 3):
            to = lax.rem(me + k, 4)
            self.flight.append(
                net.start(
                    self.sum_b.at[pl.ds(to * piece, piece)],
                    self.got_b.at[k - 1],
                    net.peer(self.order[1], to),
                )
            )

    def step3(self):
        net, piece = self.net, self.n // 32
        self.arrive()
        total = self.sum_b[pl.ds(net.place(self.order[1]) * piece, piece)].astype(F32)
        for k in range(3):
            total = total + self.got_b[k].astype(F32)
        me = net.place(self.order[2])
        self.got_c[pl.ds(me, 1)] = total.astype(BF)[None]
        self.flight = []
        for k in (1, 2, 3):
            to = lax.rem(me + k, 4)
            self.flight.append(
                net.start(self.got_c.at[me], self.got_c.at[me], net.peer(self.order[2], to))
            )

    def slot(self, depth):
        net, n = self.net, self.n
        at = net.core * (n // 2)
        if depth > 0:
            at = at + net.place(self.order[0]) * (n // 8)
        if depth > 1:
            at = at + net.place(self.order[1]) * (n // 32)
        return self.result.at[pl.ds(at, n // (2, 8, 32)[depth])]

    def step4(self):
        net = self.net
        self.arrive()
        total = self.got_c[0].astype(F32)
        for k in (1, 2, 3):
            total = total + self.got_c[k].astype(F32)
        mine = self.slot(2)
        mine[...] = total.astype(BF)
        me = net.place(self.order[1])
        self.flight = [
            net.start(mine, mine, net.peer(self.order[1], lax.rem(me + k, 4))) for k in (1, 2, 3)
        ]

    def step5(self):
        net = self.net
        self.arrive()
        mine = self.slot(1)
        me = net.place(self.order[0])
        self.flight = [
            net.start(mine, mine, net.peer(self.order[0], lax.rem(me + k, 4))) for k in (1, 2, 3)
        ]

    def step6(self):
        net = self.net
        self.arrive()
        mine = self.slot(0)
        self.flight = [net.start(mine, mine, net.sibling())]

    def step7(self):
        self.arrive()


def to_map(x, rows, cols):
    wide = cols // 8
    out = []
    for i in range(rows):
        base = (i // 8) * wide
        out.append(
            jnp.concatenate(
                [x[(base + w) * 64 + (i % 8) * 8 :][:8] for w in range(wide)], axis=0
            )
        )
    return out


def to_windows(rows_list, cols):
    wide = cols // 8
    pieces = []
    for wr in range(len(rows_list) // 8):
        for w in range(wide):
            for i in range(8):
                pieces.append(rows_list[wr * 8 + i][8 * w : 8 * w + 8])
    return jnp.concatenate(pieces, axis=0)


def paired(rows_list):
    out = []
    for di in (0, 1):
        for dj in (0, 1):
            out.append(
                jnp.concatenate(
                    [
                        rows_list[2 * i + di][16 * w + 8 * dj :][:8]
                        for w in (0, 1)
                        for i in range(8)
                    ],
                    axis=0,
                )
            )
    return out


def unpaired(parts):
    rows_list = []
    for row in range(16):
        i, di = row // 2, row % 2
        rows_list.append(
            jnp.concatenate(
                [
                    parts[2 * di + dj][64 * w + 8 * i :][:8]
                    for w in (0, 1)
                    for dj in (0, 1)
                ],
                axis=0,
            )
        )
    return rows_list


def body(
    offsets, actions, table, fgain, fqkv, fbias, fproj, mgain, mweight, cgain, cqkv, cbias, cproj,
    hweight, lat_hbm, cot_hbm,
    pred, res0, res1, res2, res3,
    lat, cot, fine_ahead, head_back, grad_back,
    fprobs, cprobs,
    *rest,
):
    works = [rest[7 * g : 7 * g + 7] for g in range(4)]
    send, recv, local = rest[28:]
    results = (res0, res1, res2, res3)
    net = Net(send, recv)
    bundles = []
    for g in range(4):
        terms, got_core, got_a, sum_a, got_b, sum_b, got_c = works[g]
        bundles.append(
            Reduce(
                net, ORDERS[g], terms, got_core, got_a, sum_a, got_b, sum_b, got_c, results[g]
            )
        )

    a0, a1 = offsets[0, 0], offsets[0, 1]
    b0, b1 = 2 * offsets[1, 0], 2 * offsets[1, 1]
    d0, d1 = lax.rem(b0 - a0 + 8, 8), lax.rem(b1 - a1 + 8, 8)
    s0, s1 = b0 - d0, b1 - d1

    own_lat = pltpu.make_async_copy(
        lat_hbm.at[0], lat.at[pl.ds(8, 16), pl.ds(16, 32)], local.at[0]
    )
    own_cot = pltpu.make_async_copy(
        cot_hbm.at[0], cot.at[pl.ds(0, 16), pl.ds(0, 32)], local.at[1]
    )
    own_lat.start()
    own_cot.start()
    net.barrier()

    row_cut = {-1: (0, 16, 24), 0: (0, 16, 8), 1: (8, 8, 0)}
    col_cut = {-1: (0, 16, 48), 0: (0, 32, 16), 1: (16, 16, 0)}
    lat_halo = []
    for dr, dc in ((-1, 0), (1, 0), (0, -1), (0, 1), (-1, -1), (-1, 1), (1, -1), (1, 1)):
        fr, nr, tr = row_cut[dr]
        fc, nc, tc = col_cut[dc]
        lat_halo.append(
            net.start(
                lat_hbm.at[0, pl.ds(fr, nr), pl.ds(fc, nc)],
                lat.at[pl.ds(tr, nr), pl.ds(tc, nc)],
                net.near(dr, dc),
            )
        )
    cot_halo = [
        net.start(cot_hbm.at[0], cot.at[pl.ds(16, 16), pl.ds(0, 32)], net.near(-1, 0)),
        net.start(
            cot_hbm.at[0, :, pl.ds(0, 16)], cot.at[pl.ds(0, 16), pl.ds(32, 16)], net.near(0, -1)
        ),
        net.start(
            cot_hbm.at[0, :, pl.ds(0, 16)], cot.at[pl.ds(16, 16), pl.ds(32, 16)], net.near(-1, -1)
        ),
    ]

    code = lax.broadcasted_iota(jnp.int32, (8, 256), 1)
    counts = jnp.zeros((8, 256), F32)
    for j in range(16):
        counts = counts + jnp.where(code == actions[0, j], 1.0, 0.0)
    condition = mm(counts.astype(BF), table[...])[:1] * (1.0 / 16.0)
    f_masks16 = [head_masks(w, h, BF) for _, w, h in FINE_GROUPS]
    f_masks32 = [head_masks(w, h, F32) for _, w, h in FINE_GROUPS]
    c_masks16 = [head_masks(w, h, BF) for _, w, h in COARSE_GROUPS]
    c_masks32 = [head_masks(w, h, F32) for _, w, h in COARSE_GROUPS]
    fb = fbias[...].reshape(384, 64).T
    cb = cbias[...].reshape(768, 64).T
    fw = [fqkv[:, 192 * i : 192 * i + 192] for i in range(3)]
    cw = [cqkv[:, 384 * i : 384 * i + 384] for i in range(3)]
    f_gain = fgain[...].reshape(1, 192)
    m_gain = mgain[...].reshape(1, 768)
    c_gain = cgain[...].reshape(1, 384)

    own_lat.wait()
    for copy in lat_halo:
        copy.wait_recv()
    pick = select(32, 64, lambda x: x + (s1 + 16))
    block = lat[pl.ds(8 + s0, 16)]
    residual = to_windows([mm(pick, block[i]) for i in range(16)], 32) + condition
    n1 = (norm(residual)[0] * f_gain).astype(BF)
    fq, fk, fv = (mm(n1, w).astype(BF) for w in fw)
    mixed = []
    for w in range(8):
        tokens = slice(64 * w, 64 * w + 64)
        line = []
        for g, (at, wide, heads) in enumerate(FINE_GROUPS):
            lanes = slice(at, at + wide)
            p = probabilities(
                fq[tokens, lanes], fk[tokens, lanes], fb[:, 64 * (at // 32) :][:, : 64 * heads],
                f_masks16[g],
            )
            fprobs[w, :, pl.ds(64 * (at // 32), 64 * heads)] = p
            line.append(fold(mm_tn(p.astype(BF), fv[tokens, lanes]), f_masks32[g]))
        mixed.append(jnp.concatenate(line, axis=1))
    f_mixed = jnp.concatenate(mixed, axis=0).astype(BF)
    attn = mm(f_mixed, fproj[...]).astype(BF)
    f_next = residual + attn.astype(F32)
    for i, row in enumerate(to_map(f_next, 16, 32)):
        fine_ahead[i, pl.ds(0, 32)] = row.astype(BF)
    ahead = [
        net.start(
            fine_ahead.at[pl.ds(0, 8), pl.ds(0, 32)], fine_ahead.at[pl.ds(16, 8), pl.ds(0, 32)],
            net.near(-1, 0),
        ),
        net.start(
            fine_ahead.at[pl.ds(0, 16), pl.ds(0, 16)], fine_ahead.at[pl.ds(0, 16), pl.ds(32, 16)],
            net.near(0, -1),
        ),
        net.start(
            fine_ahead.at[pl.ds(0, 8), pl.ds(0, 16)], fine_ahead.at[pl.ds(16, 8), pl.ds(32, 16)],
            net.near(-1, -1),
        ),
    ]

    own_cot.wait()
    for copy in cot_halo:
        copy.wait_recv()
    pick = select(32, 48, lambda x: true_place(x) + b1)
    block = cot[pl.ds(b0, 16)]
    grad_out = jnp.concatenate(paired([mm(pick, block[i]) for i in range(16)]), axis=1).astype(BF)
    grad_next = mm_nt(grad_out, hweight[...]).astype(BF)
    c_mixed_grad = mm_nt(grad_next, cproj[...]).astype(BF)

    for copy in ahead:
        copy.wait_recv()
    pick = select(32, 48, lambda x: true_place(x) + d1)
    block = fine_ahead[pl.ds(d0, 16)]
    merged = jnp.concatenate(paired([mm(pick, block[i]) for i in range(16)]), axis=1)
    m_unit, m_inverse = norm(merged)
    n2 = (m_unit * m_gain).astype(BF)
    c_residual = mm(n2, mweight[...]).astype(BF).astype(F32)
    c_unit, c_inverse = norm(c_residual)
    n3 = (c_unit * c_gain).astype(BF)
    cq, ck, cv = (mm(n3, w).astype(BF) for w in cw)
    mixed = []
    for w in range(2):
        tokens = slice(64 * w, 64 * w + 64)
        line = []
        for g, (at, wide, heads) in enumerate(COARSE_GROUPS):
            lanes = slice(at, at + wide)
            p = probabilities(
                cq[tokens, lanes], ck[tokens, lanes], cb[:, 64 * (at // 32) :][:, : 64 * heads],
                c_masks16[g],
            )
            cprobs[w, :, pl.ds(64 * (at // 32), 64 * heads)] = p
            line.append(fold(mm_tn(p.astype(BF), cv[tokens, lanes]), c_masks32[g]))
        mixed.append(jnp.concatenate(line, axis=1))
    c_mixed = jnp.concatenate(mixed, axis=0).astype(BF)
    c_attn = mm(c_mixed, cproj[...]).astype(BF)
    c_next = (c_residual + c_attn.astype(F32)).astype(BF)

    g_head = mm_tn(c_next, grad_out)
    for j in range(6):
        works[0][0][pl.ds(24 * j, 24)] = units(g_head[:, 128 * j : 128 * j + 128].astype(BF))
    g_cproj = mm_tn(c_mixed, grad_next)
    for j in range(3):
        works[0][0][pl.ds(144 + 24 * j, 24)] = units(
            g_cproj[:, 128 * j : 128 * j + 128].astype(BF)
        )
    works[0][0][pl.ds(216, 8)] = jnp.zeros((8, 16, 128), BF)
    bundles[0].step()

    head_out = mm(c_next, hweight[...])
    for i, row in enumerate(unpaired([head_out[:, 192 * t : 192 * t + 192] for t in range(4)])):
        head_back[16 + i, pl.ds(16, 32)] = row.astype(BF)
    back = [
        net.start(
            head_back.at[pl.ds(16, 16), pl.ds(16, 32)], head_back.at[pl.ds(0, 16), pl.ds(16, 32)],
            net.near(1, 0),
        ),
        net.start(
            head_back.at[pl.ds(16, 16), pl.ds(32, 16)], head_back.at[pl.ds(16, 16), pl.ds(0, 16)],
            net.near(0, 1),
        ),
        net.start(
            head_back.at[pl.ds(16, 16), pl.ds(32, 16)], head_back.at[pl.ds(0, 16), pl.ds(0, 16)],
            net.near(1, 1),
        ),
    ]

    def attention_back(probs, w, q, k, v, mixed_grad, groups, masks16, masks32):
        tokens = slice(64 * w, 64 * w + 64)
        dq, dk, dv = [], [], []
        for g, (at, wide, heads) in enumerate(groups):
            lanes = slice(at, at + wide)
            p = probs[w, :, pl.ds(64 * (at // 32), 64 * heads)]
            many_grad = spread(mixed_grad[tokens, lanes], masks16[g])
            wg = mm_nt(v[tokens, lanes], many_grad).astype(BF).astype(F32)
            sg = (p * (wg - jnp.sum(p * wg, axis=0, keepdims=True)) * SCALE).astype(BF)
            dq.append(fold(mm_tn(sg, k[tokens, lanes]), masks32[g]))
            dk.append(mm(sg, spread(q[tokens, lanes], masks16[g])))
            dv.append(mm(p.astype(BF), many_grad))
        return [jnp.concatenate(t, axis=1) for t in (dq, dk, dv)]

    pieces = [
        attention_back(cprobs, w, cq, ck, cv, c_mixed_grad, COARSE_GROUPS, c_masks16, c_masks32)
        for w in range(2)
    ]
    c_packed = [
        jnp.concatenate([piece[i] for piece in pieces], axis=0).astype(BF) for i in range(3)
    ]
    rolled = mm_nt(c_packed[0], cw[0]) + mm_nt(c_packed[1], cw[1]) + mm_nt(c_packed[2], cw[2])
    bundles[0].step()
    grad_residual = (
        grad_next.astype(F32)
        + norm_back(rolled.astype(BF).astype(F32), c_unit, c_inverse, c_gain)
    ).astype(BF)
    norm_grad = mm_nt(grad_residual, mweight[...]).astype(BF).astype(F32)
    merged_grad = norm_back(norm_grad, m_unit, m_inverse, m_gain)
    for i, row in enumerate(unpaired([merged_grad[:, 192 * t : 192 * t + 192] for t in range(4)])):
        grad_back[8 + i, pl.ds(16, 32)] = row.astype(BF)
    grads = [
        net.start(
            grad_back.at[pl.ds(16, 8), pl.ds(16, 32)], grad_back.at[pl.ds(0, 8), pl.ds(16, 32)],
            net.near(1, 0),
        ),
        net.start(
            grad_back.at[pl.ds(8, 16), pl.ds(32, 16)], grad_back.at[pl.ds(8, 16), pl.ds(0, 16)],
            net.near(0, 1),
        ),
        net.start(
            grad_back.at[pl.ds(16, 8), pl.ds(32, 16)], grad_back.at[pl.ds(0, 8), pl.ds(0, 16)],
            net.near(1, 1),
        ),
    ]
    for t in range(3):
        g_part = mm_tn(n3, c_packed[t])
        for j in range(3):
            works[1][0][pl.ds(72 * t + 24 * j, 24)] = units(
                g_part[:, 128 * j : 128 * j + 128].astype(BF)
            )
    works[1][0][pl.ds(216, 8)] = jnp.zeros((8, 16, 128), BF)
    bundles[1].step()
    g_merge = mm_tn(n2, grad_residual)
    for j in range(3):
        works[2][0][pl.ds(48 * j, 48)] = units(g_merge[:, 128 * j : 128 * j + 128].astype(BF))
    works[2][0][pl.ds(144, 16)] = jnp.zeros((16, 16, 128), BF)
    bundles[2].step()
    bundles[0].step()
    bundles[1].step()

    for copy in grads:
        copy.wait_recv()
    pick = select(32, 48, lambda x: x)
    x = lax.broadcasted_iota(jnp.int32, (32, 48), 0)
    u = lax.broadcasted_iota(jnp.int32, (32, 48), 1)
    pick = jnp.where(folded_place(x + (16 - d1)) == u, 1.0, 0.0).astype(BF)
    block = grad_back[pl.ds(8 - d0, 16)]
    f_grad = to_windows([mm(pick, block[i]) for i in range(16)], 32).astype(BF)
    f_mixed_grad = mm_nt(f_grad, fproj[...]).astype(BF)
    g_fproj = mm_tn(f_mixed, f_grad)
    bundles[2].step()
    pieces = []
    for w in range(8):
        pieces.append(
            attention_back(fprobs, w, fq, fk, fv, f_mixed_grad, FINE_GROUPS, f_masks16, f_masks32)
        )
    g_parts = [
        mm_tn(n1, jnp.concatenate([piece[i] for piece in pieces], axis=0).astype(BF))
        for i in range(3)
    ]
    g_parts.append(g_fproj)
    for t in range(4):
        works[3][0][pl.ds(12 * t, 12)] = units(g_parts[t][:, :128].astype(BF))
    for t in (0, 2):
        tails = jnp.concatenate([g_parts[t][:, 128:], g_parts[t + 1][:, 128:]], axis=1)
        works[3][0][pl.ds(48 + 6 * t, 12)] = units(tails.astype(BF))
    works[3][0][pl.ds(72, 24)] = jnp.zeros((24, 16, 128), BF)
    bundles[3].step()

    for copy in back:
        copy.wait_recv()
    pick = jnp.where(folded_place(x + (16 - b1)) == u, 1.0, 0.0).astype(BF)
    block = head_back[pl.ds(16 - b0, 16)]
    for i in range(16):
        pred[i] = mm(pick, block[i]).astype(BF)

    while any(bundle.stage < 8 for bundle in bundles):
        for bundle in bundles:
            if bundle.stage < 8:
                bundle.step()
    for copy in net.copies:
        copy.wait_send()


N_COPIES = 8 + 3 + 3 + 3 + 3 + 4 * 17


def unpack(r0, r1, r2, r3, pred_in, pred, fq, fp, me, cq, cp, he):
    pred[0] = pred_in[...]

    def take(ref, at, count):
        return ref[pl.ds(at, count)].reshape(count * 16, 128).astype(F32)

    for j in range(6):
        he[:, pl.ds(128 * j, 128)] = take(r0, 24 * j, 24)
    for j in range(3):
        cp[:, pl.ds(128 * j, 128)] = take(r0, 144 + 24 * j, 24)
        me[:, pl.ds(128 * j, 128)] = take(r2, 48 * j, 48)
    for j in range(9):
        cq[:, pl.ds(128 * j, 128)] = take(r1, 24 * j, 24)
    parts = [take(r3, 12 * t, 12) for t in range(4)]
    tails = [take(r3, 48 + 12 * t, 12) for t in range(2)]
    fq[...] = jnp.concatenate(
        [parts[0], tails[0][:, :64], parts[1], tails[0][:, 64:], parts[2], tails[1][:, :64]], axis=1
    )
    fp[...] = jnp.concatenate([parts[3], tails[1][:, 64:]], axis=1)


def on_device(
    latents, actions, action_table, offsets, fine_gain, fine_qkv, fine_bias, fine_proj, merge_gain,
    merge_weight, coarse_gain, coarse_qkv, coarse_bias, coarse_proj, head_weight, cotangent,
):
    smem = pl.BlockSpec(memory_space=pltpu.SMEM)
    vmem = pl.BlockSpec(memory_space=pltpu.VMEM)
    anywhere = pl.BlockSpec(memory_space=pl.ANY)
    scratch = [
        pltpu.VMEM((40, 64, 192), BF),
        pltpu.VMEM((32, 48, 192), BF),
        pltpu.VMEM((24, 48, 192), BF),
        pltpu.VMEM((32, 48, 192), BF),
        pltpu.VMEM((24, 48, 192), BF),
        pltpu.VMEM((8, 64, 384), F32),
        pltpu.VMEM((2, 64, 768), F32),
    ]
    for n in UNITS:
        for shape in ((n,), (n // 2,), (3, n // 8), (n // 2,), (3, n // 32), (n // 8,), (4, n // 32)):
            scratch.append(pltpu.VMEM(shape + (16, 128), BF))
    scratch += [
        pltpu.SemaphoreType.DMA((N_COPIES,)),
        pltpu.SemaphoreType.DMA((N_COPIES,)),
        pltpu.SemaphoreType.DMA((2,)),
    ]
    pred, *results = pl.pallas_call(
        body,
        out_shape=[jax.ShapeDtypeStruct((16, 32, 192), BF)]
        + [jax.ShapeDtypeStruct((n, 16, 128), BF) for n in UNITS],
        in_specs=[smem, smem] + [vmem] * 12 + [anywhere] * 2,
        out_specs=[vmem] * 5,
        scratch_shapes=scratch,
        compiler_params=pltpu.CompilerParams(
            collective_id=0, has_side_effects=True, vmem_limit_bytes=48 * 1024 * 1024
        ),
        name="block_pair",
    )(
        offsets, actions, action_table, fine_gain, fine_qkv, fine_bias, fine_proj, merge_gain,
        merge_weight, coarse_gain, coarse_qkv, coarse_bias, coarse_proj, head_weight, latents,
        cotangent,
    )
    shapes = ((192, 576), (192, 192), (768, 384), (384, 1152), (384, 384), (384, 768))
    return tuple(
        pl.pallas_call(
            unpack,
            out_shape=[jax.ShapeDtypeStruct((1, 16, 32, 192), BF)]
            + [jax.ShapeDtypeStruct(s, F32) for s in shapes],
            in_specs=[vmem] * 5,
            out_specs=[vmem] * 7,
            compiler_params=pltpu.CompilerParams(vmem_limit_bytes=48 * 1024 * 1024),
            name="unpack",
        )(*results, pred)
    )


def solution(mesh):
    split = P(None, "rows", "cols", None)
    return jax.shard_map(
        on_device,
        mesh=mesh,
        in_specs=(split,) + (P(),) * 14 + (split,),
        out_specs=(split,) + (P(),) * 6,
        check_vma=False,
    )
```

```python
import jax
import jax.numpy as jnp
from jax import lax
from jax.experimental import pallas as pl
from jax.experimental.pallas import tpu as pltpu
from jax.sharding import PartitionSpec as P

MESH = pl.DeviceIdType.MESH
BF = jnp.bfloat16
F32 = jnp.float32
EPS = 1e-05
SCALE = 32 ** (-0.5)
FINE_GROUPS = ((0, 128, 4), (128, 64, 2))
COARSE_GROUPS = ((0, 128, 4), (128, 128, 4), (256, 128, 4))
N_BUNDLES, N_UNITS = 9, 72
ORDERS = (("y", "z", "x"), ("z", "x", "y"), ("x", "y", "z"))


def mm(a, b):
    return lax.dot_general(a, b, (((1,), (0,)), ((), ())), preferred_element_type=F32)


def mm_nt(a, b):
    return lax.dot_general(a, b, (((1,), (1,)), ((), ())), preferred_element_type=F32)


def mm_tn(a, b):
    return lax.dot_general(a, b, (((0,), (0,)), ((), ())), preferred_element_type=F32)


def norm(x):
    centred = x - jnp.mean(x, axis=-1, keepdims=True)
    inverse = lax.rsqrt(jnp.mean(centred * centred, axis=-1, keepdims=True) + EPS)
    return centred * inverse, inverse


def norm_back(upstream, unit, inverse, gain):
    e = upstream * gain
    return inverse * (
        e - jnp.mean(e, axis=-1, keepdims=True) - unit * jnp.mean(e * unit, axis=-1, keepdims=True)
    )


def head_masks(width, heads, dtype):
    lane = lax.broadcasted_iota(jnp.int32, (1, width), 1) // 32
    return [jnp.where(lane == h, 1.0, 0.0).astype(dtype) for h in range(heads)]


def spread(x, masks):
    return jnp.concatenate([x * m for m in masks], axis=0)


def fold(x, masks):
    total = x[:64] * masks[0]
    for h in range(1, len(masks)):
        total = total + x[64 * h : 64 * h + 64] * masks[h]
    return total


def probabilities(q, k, bias, masks):
    s = mm_nt(k, spread(q, masks)) * SCALE + bias
    e = jnp.exp(s - jnp.max(s, axis=0, keepdims=True))
    return e / jnp.sum(e, axis=0, keepdims=True)


def folded_place(u):
    v = u & 15
    return (u - v) + (v & 1) * 8 + (v >> 1)


def true_place(p):
    v = p & 15
    return (p - v) + (v & 7) * 2 + (v >> 3)


def units(x):
    return x.reshape(x.shape[0] // 16, 16, 128)


class Net:
    def __init__(self, send, recv):
        self.r = lax.axis_index("rows")
        self.c = lax.axis_index("cols")
        r, c = self.r, self.c
        self.core = lax.rem(r, 2)
        xlo = lax.rem(r // 2, 2)
        self.y = r // 4
        self.z = c // 2
        xhi = lax.rem(c, 2)
        self.x = xhi * 2 + xlo
        self.low = lax.rem(r, 4)
        self.xhi = xhi
        self.send, self.recv = send, recv
        self.count = 0
        self.copies = []

    def near(self, dr, dc):
        return (lax.rem(self.r + dr + 16, 16), lax.rem(self.c + dc + 8, 8))

    def place(self, axis):
        return {"x": self.x, "y": self.y, "z": self.z}[axis]

    def peer(self, axis, index):
        if axis == "y":
            return (index * 4 + self.low, self.c)
        if axis == "z":
            return (self.r, index * 2 + self.xhi)
        return (self.y * 4 + lax.rem(index, 2) * 2 + self.core, self.z * 2 + index // 2)

    def sibling(self):
        return (self.r + 1 - 2 * self.core, self.c)

    def start(self, source, target, device):
        n = self.count
        self.count += 1
        copy = pltpu.make_async_remote_copy(
            src_ref=source,
            dst_ref=target,
            send_sem=self.send.at[n],
            recv_sem=self.recv.at[n],
            device_id=device,
            device_id_type=MESH,
        )
        copy.start()
        self.copies.append(copy)
        return copy

    def greet(self):
        sem = pltpu.get_barrier_semaphore()
        others = [self.near(a, b) for a in (-1, 0, 1) for b in (-1, 0, 1) if (a, b) != (0, 0)]
        others.append(self.sibling())
        for axis in "xyz":
            others += [self.peer(axis, lax.rem(self.place(axis) + k, 4)) for k in (1, 2, 3)]
        for device in others:
            pl.semaphore_signal(sem, inc=1, device_id=device, device_id_type=MESH)
        self.greeted = len(others)

    def gather(self):
        pl.semaphore_wait(pltpu.get_barrier_semaphore(), self.greeted)


class Reduce:
    def __init__(self, net, order, terms, got_core, got_a, sum_a, got_b, got_c, result):
        self.net, self.order = net, order
        self.terms, self.got_core, self.got_a, self.sum_a = terms, got_core, got_a, sum_a
        self.got_b, self.got_c, self.result = got_b, got_c, result
        self.half, self.part = terms.shape[0] // 2, terms.shape[0] // 8
        self.stage = 0
        self.flight = []

    def step(self):
        getattr(self, "step%d" % self.stage)()
        self.stage += 1

    def arrive(self):
        for copy in self.flight:
            copy.wait_recv()

    def to_peers(self, axis, source, target):
        net = self.net
        me = net.place(axis)
        self.flight = []
        for k in (1, 2, 3):
            to = lax.rem(me + k, 4)
            self.flight.append(net.start(source(to), target(k), net.peer(axis, to)))

    def spread_out(self, total, got, axis):
        me = self.net.place(axis)
        got[pl.ds(me, 1)] = total.astype(BF)[None]
        self.to_peers(axis, lambda to: got.at[me], lambda k: got.at[me])

    def summed(self, got):
        total = got[0].astype(F32)
        for k in (1, 2, 3):
            total = total + got[k].astype(F32)
        return total

    def step0(self):
        net, half = self.net, self.half
        self.flight = [
            net.start(self.terms.at[pl.ds((1 - net.core) * half, half)], self.got_core, net.sibling())
        ]

    def step1(self):
        net, half, part = self.net, self.half, self.part
        self.arrive()
        own = self.terms[pl.ds(net.core * half, half)].astype(F32)
        self.sum_a[...] = (own + self.got_core[...].astype(F32)).astype(BF)
        self.to_peers(
            self.order[0],
            lambda to: self.sum_a.at[pl.ds(to * part, part)],
            lambda k: self.got_a.at[k - 1],
        )

    def step2(self):
        self.arrive()
        me = self.net.place(self.order[0])
        total = self.sum_a[pl.ds(me * self.part, self.part)].astype(F32)
        for k in range(3):
            total = total + self.got_a[k].astype(F32)
        self.spread_out(total, self.got_b, self.order[1])

    def step3(self):
        self.arrive()
        self.spread_out(self.summed(self.got_b), self.got_c, self.order[2])

    def step4(self):
        self.arrive()
        at = self.net.core * self.half + self.net.place(self.order[0]) * self.part
        mine = self.result.at[pl.ds(at, self.part)]
        mine[...] = self.summed(self.got_c).astype(BF)
        self.to_peers(self.order[0], lambda to: mine, lambda k: mine)

    def step5(self):
        self.arrive()
        mine = self.result.at[pl.ds(self.net.core * self.half, self.half)]
        self.flight = [self.net.start(mine, mine, self.net.sibling())]

    def step6(self):
        self.arrive()


def to_map(x, rows, cols):
    wide = cols // 8
    out = []
    for i in range(rows):
        base = (i // 8) * wide
        out.append(
            jnp.concatenate(
                [x[(base + w) * 64 + (i % 8) * 8 :][:8] for w in range(wide)], axis=0
            )
        )
    return out


def to_windows(rows_list, cols):
    wide = cols // 8
    pieces = []
    for wr in range(len(rows_list) // 8):
        for w in range(wide):
            for i in range(8):
                pieces.append(rows_list[wr * 8 + i][8 * w : 8 * w + 8])
    return jnp.concatenate(pieces, axis=0)


def paired(rows_list):
    out = []
    for di in (0, 1):
        for dj in (0, 1):
            out.append(
                jnp.concatenate(
                    [
                        rows_list[2 * i + di][16 * w + 8 * dj :][:8]
                        for w in (0, 1)
                        for i in range(8)
                    ],
                    axis=0,
                )
            )
    return out


def unpaired(parts):
    rows_list = []
    for row in range(16):
        i, di = row // 2, row % 2
        rows_list.append(
            jnp.concatenate(
                [
                    parts[2 * di + dj][64 * w + 8 * i :][:8]
                    for w in (0, 1)
                    for dj in (0, 1)
                ],
                axis=0,
            )
        )
    return rows_list


def packed(x):
    return x.reshape(128, x.shape[-1]).astype(BF).reshape(8, 16, x.shape[-1])


def one_hot(rows_out, cols_in, place):
    x = lax.broadcasted_iota(jnp.int32, (rows_out, cols_in), 0)
    u = lax.broadcasted_iota(jnp.int32, (rows_out, cols_in), 1)
    return jnp.where(place(x) == u, 1.0, 0.0).astype(BF)


def body(*refs):
    (
        offsets, actions, table, fgain, fqkv, fbias, fproj, mgain, mweight, cgain, cqkv, cbias,
        cproj, hweight,
    ) = refs[26:40]
    lat_hbm, cot_hbm = refs[14:16]
    pred_out, *result_outs = refs[16:26]
    (
        lat, lat_left, lat_right, lat_packs, cot, cot_main, cot_next, cot_prev, cot_pack, ahead,
        ahead_side, ahead_pack, head, head_prev, head_next, head_pack, head_rows, back, back_side,
        back_pack, fprobs, cprobs,
    ) = refs[40:62]
    rest = refs[62:]
    works = [rest[6 * g : 6 * g + 6] for g in range(N_BUNDLES)]
    pred, *results = rest[54:64]
    send, recv, local = rest[64:]
    loads = [
        pltpu.make_async_copy(refs[i], refs[26 + i], local.at[2 + i]) for i in range(14)
    ]
    net = Net(send, recv)
    net.greet()
    bundles = [
        Reduce(net, ORDERS[g % 3], *works[g], results[g]) for g in range(N_BUNDLES)
    ]

    def advance(*numbers):
        for g in numbers:
            bundles[g].step()
            if bundles[g].stage == 7:
                copy = pltpu.make_async_copy(results[g], result_outs[g], local.at[17 + g])
                copy.start()
                stores.append(copy)

    stores = []
    own_lat = pltpu.make_async_copy(lat_hbm.at[0], lat.at[pl.ds(8, 16)], local.at[0])
    own_cot = pltpu.make_async_copy(cot_hbm.at[0], cot.at[pl.ds(8, 16)], local.at[1])
    for copy in [own_lat] + loads[:6] + loads[6:] + [own_cot]:
        copy.start()

    own_lat.wait()
    low = lat[pl.ds(8, 16), pl.ds(0, 16)].astype(F32)
    high = lat[pl.ds(8, 16), pl.ds(16, 16)].astype(F32)
    lat_packs[0] = packed(low[:, :8])
    lat_packs[1] = packed(high[:, 8:])
    net.gather()
    lat_halo = []
    for side, (pack, dc) in enumerate(((0, -1), (1, 1))):
        target = lat_right if dc < 0 else lat_left
        for dr, fr, nr, tr in ((0, 0, 8, 4), (-1, 0, 4, 12), (1, 4, 4, 0)):
            lat_halo.append(
                net.start(
                    lat_packs.at[pack, pl.ds(fr, nr)], target.at[pl.ds(tr, nr)], net.near(dr, dc)
                )
            )
    for dr, fr, tr in ((-1, 0, 24), (1, 8, 0)):
        lat_halo.append(
            net.start(lat_hbm.at[0, pl.ds(fr, 8)], lat.at[pl.ds(tr, 8)], net.near(dr, 0))
        )

    for copy in loads:
        copy.wait()
    a0, a1 = offsets[0, 0], offsets[0, 1]
    b0, b1 = 2 * offsets[1, 0], 2 * offsets[1, 1]
    d0, d1 = lax.rem(b0 - a0 + 8, 8), lax.rem(b1 - a1 + 8, 8)
    s0, s1 = lax.rem(b0 - d0 + 8, 16) - 8, lax.rem(b1 - d1 + 8, 16) - 8
    t0, t1 = s0 + d0, s1 + d1
    code = lax.broadcasted_iota(jnp.int32, (8, 256), 1)
    counts = jnp.zeros((8, 256), F32)
    for j in range(16):
        counts = counts + jnp.where(code == actions[0, j], 1.0, 0.0)
    condition = mm_nt(counts.astype(BF), table[...])[:1] * (1.0 / 16.0)
    f_masks16 = [head_masks(w, h, BF) for _, w, h in FINE_GROUPS]
    f_masks32 = [head_masks(w, h, F32) for _, w, h in FINE_GROUPS]
    c_masks16 = [head_masks(w, h, BF) for _, w, h in COARSE_GROUPS]
    c_masks32 = [head_masks(w, h, F32) for _, w, h in COARSE_GROUPS]
    fb = fbias[...].reshape(384, 64).T
    cb = cbias[...].reshape(768, 64).T
    fw = [fqkv[:, 192 * i : 192 * i + 192] for i in range(3)]
    cw = [cqkv[:, 384 * i : 384 * i + 384] for i in range(3)]
    f_gain = fgain[...].reshape(1, 192)
    m_gain = mgain[...].reshape(1, 768)
    c_gain = cgain[...].reshape(1, 384)

    def two_picks(rows_out, cols_in, parity, place):
        return [
            one_hot(rows_out, cols_in, lambda x, p=p: place(x, p))
            for p in (parity * 8, 8 - parity * 8)
        ]

    for copy in lat_halo:
        copy.wait_recv()
    cot_rows = [
        net.start(cot_hbm.at[0], cot.at[pl.ds(24, 16)], net.near(-1, 0)),
        net.start(cot_hbm.at[0, pl.ds(8, 8)], cot.at[pl.ds(0, 8)], net.near(1, 0)),
    ]

    def lat_place(x, p):
        u = x + (s1 + 8)
        return jnp.where(u < 8, 32 + p + u, jnp.where(u < 40, u - 8, 48 + p + u - 40))

    pick = two_picks(32, 64, (8 + s0) & 1, lat_place)
    block = lat[pl.ds(8 + s0, 16)]
    rows_list = []
    for i in range(16):
        pair = (8 + s0 + i) >> 1
        source = jnp.concatenate([block[i], lat_left[pair], lat_right[pair]], axis=0)
        rows_list.append(mm(pick[i % 2], source))
    residual = to_windows(rows_list, 32) + condition
    n1 = (norm(residual)[0] * f_gain).astype(BF)
    fq, fk, fv = (mm(n1, w).astype(BF) for w in fw)
    mixed = []
    for w in range(8):
        tokens = slice(64 * w, 64 * w + 64)
        line = []
        for g, (at, wide, heads) in enumerate(FINE_GROUPS):
            lanes = slice(at, at + wide)
            p = probabilities(
                fq[tokens, lanes], fk[tokens, lanes], fb[:, 64 * (at // 32) :][:, : 64 * heads],
                f_masks16[g],
            )
            fprobs[w, :, pl.ds(64 * (at // 32), 64 * heads)] = p
            line.append(fold(mm_tn(p.astype(BF), fv[tokens, lanes]), f_masks32[g]))
        mixed.append(jnp.concatenate(line, axis=1))
    f_mixed = jnp.concatenate(mixed, axis=0).astype(BF)
    attn = mm(f_mixed, fproj[...]).astype(BF)
    f_next = residual + attn.astype(F32)
    for i, row in enumerate(to_map(f_next, 16, 32)):
        ahead[i] = row.astype(BF)
    for wr in range(2):
        ahead_pack[pl.ds(4 * wr, 4)] = (
            f_next[256 * wr : 256 * wr + 64].astype(BF).reshape(4, 16, 192)
        )
    ahead_halo = [
        net.start(ahead_pack, ahead_side.at[pl.ds(0, 8)], net.near(0, -1)),
        net.start(
            ahead_pack.at[pl.ds(0, 4)], ahead_side.at[pl.ds(8, 4)], net.near(-1, -1)
        ),
        net.start(ahead.at[pl.ds(0, 8)], ahead.at[pl.ds(16, 8)], net.near(-1, 0)),
    ]

    own_cot.wait()
    for copy in cot_rows:
        copy.wait_recv()
    block = cot[pl.ds(8 + t0, 16)]
    cot_main[...] = block
    cot_pack[...] = packed(block[:, 16:].astype(F32)[:, 8:])
    cot_halo = [
        net.start(cot_main.at[:, pl.ds(0, 16)], cot_next, net.near(0, -1)),
        net.start(cot_pack, cot_prev, net.near(0, 1)),
    ]

    def ahead_place(x, p):
        u = true_place(x) + d1
        return jnp.where(u < 32, u, u + p)

    pick = two_picks(32, 48, d0 & 1, ahead_place)
    for copy in ahead_halo:
        copy.wait_recv()
    block = ahead[pl.ds(d0, 16)]
    rows_list = []
    for i in range(16):
        source = jnp.concatenate([block[i], ahead_side[(d0 + i) >> 1]], axis=0)
        rows_list.append(mm(pick[i % 2], source))
    merged = jnp.concatenate(paired(rows_list), axis=1)
    m_unit, m_inverse = norm(merged)
    n2 = (m_unit * m_gain).astype(BF)
    c_residual = mm(n2, mweight[...]).astype(BF).astype(F32)
    c_unit, c_inverse = norm(c_residual)
    n3 = (c_unit * c_gain).astype(BF)
    cq, ck, cv = (mm(n3, w).astype(BF) for w in cw)
    mixed = []
    for w in range(2):
        tokens = slice(64 * w, 64 * w + 64)
        line = []
        for g, (at, wide, heads) in enumerate(COARSE_GROUPS):
            lanes = slice(at, at + wide)
            p = probabilities(
                cq[tokens, lanes], ck[tokens, lanes], cb[:, 64 * (at // 32) :][:, : 64 * heads],
                c_masks16[g],
            )
            cprobs[w, :, pl.ds(64 * (at // 32), 64 * heads)] = p
            line.append(fold(mm_tn(p.astype(BF), cv[tokens, lanes]), c_masks32[g]))
        mixed.append(jnp.concatenate(line, axis=1))
    c_mixed = jnp.concatenate(mixed, axis=0).astype(BF)
    c_attn = mm(c_mixed, cproj[...]).astype(BF)
    c_next = (c_residual + c_attn.astype(F32)).astype(BF)
    head_out = mm(c_next, hweight[...])
    for i, row in enumerate(unpaired([head_out[:, 192 * t : 192 * t + 192] for t in range(4)])):
        head[i] = row.astype(BF)

    for copy in cot_halo:
        copy.wait_recv()

    def cot_place(x, p):
        u = true_place(x) + (t1 + 8)
        return jnp.where(u < 8, 48 + p + u, u - 8)

    pick = two_picks(32, 64, 0, cot_place)
    rows_list = []
    for i in range(16):
        source = jnp.concatenate([cot_main[i], cot_next[i], cot_prev[i // 2]], axis=0)
        rows_list.append(mm(pick[i % 2], source))
    grad_out = jnp.concatenate(paired(rows_list), axis=1).astype(BF)
    grad_next = mm_nt(grad_out, hweight[...]).astype(BF)
    c_mixed_grad = mm_nt(grad_next, cproj[...]).astype(BF)

    g_head = mm_tn(c_next, grad_out)
    for j in range(6):
        works[j // 3][0][pl.ds(24 * (j % 3), 24)] = units(
            g_head[:, 128 * j : 128 * j + 128].astype(BF)
        )
    g_cproj = mm_tn(c_mixed, grad_next)
    for j in range(3):
        works[2][0][pl.ds(24 * j, 24)] = units(g_cproj[:, 128 * j : 128 * j + 128].astype(BF))
    advance(0, 1, 2)

    def attention_back(probs, w, q, k, v, mixed_grad, groups, masks16, masks32):
        tokens = slice(64 * w, 64 * w + 64)
        dq, dk, dv = [], [], []
        for g, (at, wide, heads) in enumerate(groups):
            lanes = slice(at, at + wide)
            p = probs[w, :, pl.ds(64 * (at // 32), 64 * heads)]
            many_grad = spread(mixed_grad[tokens, lanes], masks16[g])
            wg = mm_nt(v[tokens, lanes], many_grad).astype(BF).astype(F32)
            sg = (p * (wg - jnp.sum(p * wg, axis=0, keepdims=True)) * SCALE).astype(BF)
            dq.append(fold(mm_tn(sg, k[tokens, lanes]), masks32[g]))
            dk.append(mm(sg, spread(q[tokens, lanes], masks16[g])))
            dv.append(mm(p.astype(BF), many_grad))
        return [jnp.concatenate(t, axis=1) for t in (dq, dk, dv)]

    pieces = [
        attention_back(cprobs, w, cq, ck, cv, c_mixed_grad, COARSE_GROUPS, c_masks16, c_masks32)
        for w in range(2)
    ]
    c_packed = [
        jnp.concatenate([piece[i] for piece in pieces], axis=0).astype(BF) for i in range(3)
    ]
    rolled = mm_nt(c_packed[0], cw[0]) + mm_nt(c_packed[1], cw[1]) + mm_nt(c_packed[2], cw[2])
    grad_residual = (
        grad_next.astype(F32)
        + norm_back(rolled.astype(BF).astype(F32), c_unit, c_inverse, c_gain)
    ).astype(BF)
    norm_grad = mm_nt(grad_residual, mweight[...]).astype(BF).astype(F32)
    merged_grad = norm_back(norm_grad, m_unit, m_inverse, m_gain)
    rows_list = [
        row.astype(BF)
        for row in unpaired([merged_grad[:, 192 * t : 192 * t + 192] for t in range(4)])
    ]
    last = one_hot(16, 64, lambda x: (x >> 3) * 32 + folded_place(24 + (x & 7)))
    for i in range(8):
        both = jnp.concatenate(rows_list[2 * i : 2 * i + 2], axis=0)
        back[8 + 2 * i], back[9 + 2 * i] = rows_list[2 * i], rows_list[2 * i + 1]
        back_pack[i] = mm(last, both).astype(BF)
    back_halo = [
        net.start(back_pack, back_side.at[pl.ds(4, 8)], net.near(0, 1)),
        net.start(back_pack.at[pl.ds(4, 4)], back_side.at[pl.ds(0, 4)], net.near(1, 1)),
        net.start(back.at[pl.ds(16, 8)], back.at[pl.ds(0, 8)], net.near(1, 0)),
    ]
    advance(0, 1, 2)
    for t in range(3):
        g_part = mm_tn(n3, c_packed[t])
        for j in range(3):
            works[3 + t][0][pl.ds(24 * j, 24)] = units(
                g_part[:, 128 * j : 128 * j + 128].astype(BF)
            )
    advance(3, 4, 5)
    g_merge = mm_tn(n2, grad_residual)
    for t in range(2):
        for j in range(3):
            works[6 + t][0][pl.ds(24 * j, 24)] = units(
                g_merge[384 * t : 384 * t + 384, 128 * j : 128 * j + 128].astype(BF)
            )
    advance(6, 7)
    advance(3, 4, 5)
    first = one_hot(16, 64, lambda x: (x >> 3) * 32 + folded_place(x & 7))
    for i in range(8):
        both = jnp.concatenate([head[2 * i], head[2 * i + 1]], axis=0)
        head_pack[i] = mm(first, both).astype(BF)

    def back_place(x, p):
        u = x + (8 - d1)
        return jnp.where(u < 8, 32 + p + u, folded_place(u - 8))

    pick = two_picks(32, 48, d0 & 1, back_place)
    for copy in back_halo:
        copy.wait_recv()
    advance(6, 7)
    head_halo = [
        net.start(head.at[:, pl.ds(16, 16)], head_prev, net.near(0, 1)),
        net.start(head_pack, head_next, net.near(0, -1)),
    ]

    def turn_rows():
        for copy in head_halo:
            copy.wait_recv()
        pick = two_picks(32, 64, 0, head_place)
        for i in range(16):
            source = jnp.concatenate([head[i], head_prev[i], head_next[i // 2]], axis=0)
            head_rows[16 + i] = mm(pick[i % 2], source).astype(BF)
        return [
            net.start(head_rows.at[pl.ds(16, 16)], head_rows.at[pl.ds(0, 16)], net.near(1, 0)),
            net.start(head_rows.at[pl.ds(16, 8)], head_rows.at[pl.ds(32, 8)], net.near(-1, 0)),
        ]

    def head_place(x, p):
        u = x + (16 - t1)
        return jnp.where(
            u < 16, 32 + folded_place(u), jnp.where(u < 48, folded_place(u - 16), u + p)
        )

    block = back[pl.ds(8 - d0, 16)]
    rows_list = []
    for i in range(16):
        source = jnp.concatenate([block[i], back_side[(8 - d0 + i) >> 1]], axis=0)
        rows_list.append(mm(pick[i % 2], source))
    f_grad = to_windows(rows_list, 32).astype(BF)
    f_mixed_grad = mm_nt(f_grad, fproj[...]).astype(BF)
    g_fproj = mm_tn(f_mixed, f_grad)
    pieces = []
    for w in range(8):
        pieces.append(
            attention_back(fprobs, w, fq, fk, fv, f_mixed_grad, FINE_GROUPS, f_masks16, f_masks32)
        )
        if w == 1:
            advance(0, 1, 2)
        if w == 3:
            advance(3, 4, 5, 6, 7)
            rows_halo = turn_rows()
        if w == 5:
            advance(0, 1, 2)
    g_parts = [
        mm_tn(n1, jnp.concatenate([piece[i] for piece in pieces], axis=0).astype(BF))
        for i in range(3)
    ]
    g_parts.append(g_fproj)
    for t in range(4):
        works[8][0][pl.ds(12 * t, 12)] = units(g_parts[t][:, :128].astype(BF))
    for t in (0, 2):
        tails = jnp.concatenate([g_parts[t][:, 128:], g_parts[t + 1][:, 128:]], axis=1)
        works[8][0][pl.ds(48 + 6 * t, 12)] = units(tails.astype(BF))
    advance(8)
    advance(3, 4, 5, 6, 7)
    advance(8)
    advance(0, 1, 2)
    advance(8)
    advance(3, 4, 5, 6, 7)
    advance(0, 1, 2)
    advance(8)
    for copy in rows_halo:
        copy.wait_recv()
    pred[...] = head_rows[pl.ds(16 - t0, 16)]
    stores.append(pltpu.make_async_copy(pred, pred_out, local.at[16]))
    stores[-1].start()
    advance(3, 4, 5, 6, 7)
    advance(8)
    advance(0, 1, 2)
    advance(8)
    advance(3, 4, 5, 6, 7)
    advance(8)
    for copy in stores:
        copy.wait()
    for copy in net.copies:
        copy.wait_send()


N_COPIES = 8 + 4 + 3 + 3 + 4 + 14 * N_BUNDLES


def unpack(*refs):
    pred_in, *heres = refs[:10]
    pred_out, *outs = refs[10:17]
    packs, wides, held, sems = refs[17:26], refs[26:32], refs[32], refs[33]
    fq, fp, me, cq, cp, he = wides
    pass_in = pltpu.make_async_copy(pred_in, held, sems.at[15])
    pass_on = pltpu.make_async_copy(held, pred_out.at[0], sems.at[16])
    loads = [pltpu.make_async_copy(heres[g], packs[g], sems.at[g]) for g in range(9)]
    stores = [pltpu.make_async_copy(wides[i], outs[i], sems.at[9 + i]) for i in range(6)]
    for copy in loads + [pass_in]:
        copy.start()

    def take(g, at, count):
        return packs[g][pl.ds(at, count)].reshape(count * 16, 128).astype(F32)

    for t in range(3):
        loads[3 + t].wait()
        for j in range(3):
            cq[:, pl.ds(384 * t + 128 * j, 128)] = take(3 + t, 24 * j, 24)
    stores[3].start()
    for t in range(2):
        loads[t].wait()
        for j in range(3):
            he[:, pl.ds(384 * t + 128 * j, 128)] = take(t, 24 * j, 24)
    stores[5].start()
    for t in range(2):
        loads[6 + t].wait()
        for j in range(3):
            me[pl.ds(384 * t, 384), pl.ds(128 * j, 128)] = take(6 + t, 24 * j, 24)
    stores[2].start()
    loads[2].wait()
    for j in range(3):
        cp[:, pl.ds(128 * j, 128)] = take(2, 24 * j, 24)
    stores[4].start()
    pass_in.wait()
    pass_on.start()
    loads[8].wait()
    parts = [take(8, 12 * t, 12) for t in range(4)]
    tails = [take(8, 48 + 12 * t, 12) for t in range(2)]
    fq[...] = jnp.concatenate(
        [parts[0], tails[0][:, :64], parts[1], tails[0][:, 64:], parts[2], tails[1][:, :64]], axis=1
    )
    fp[...] = jnp.concatenate([parts[3], tails[1][:, 64:]], axis=1)
    stores[0].start()
    stores[1].start()
    for copy in stores + [pass_on]:
        copy.wait()


def on_device(
    latents, actions, action_table, offsets, fine_gain, fine_qkv, fine_bias, fine_proj, merge_gain,
    merge_weight, coarse_gain, coarse_qkv, coarse_bias, coarse_proj, head_weight, cotangent,
):
    hbm = pl.BlockSpec(memory_space=pltpu.HBM)
    held = (
        offsets, actions, action_table.T, fine_gain, fine_qkv, fine_bias, fine_proj, merge_gain,
        merge_weight, coarse_gain, coarse_qkv, coarse_bias, coarse_proj, head_weight,
    )
    scratch = [pltpu.SMEM(x.shape, x.dtype) for x in held[:2]]
    scratch += [pltpu.VMEM(x.shape, x.dtype) for x in held[2:]]
    scratch += [
        pltpu.VMEM(shape + (192,), BF)
        for shape in (
            (32, 32), (16, 16), (16, 16), (2, 8, 16), (40, 32), (16, 32), (16, 16), (8, 16),
            (8, 16), (24, 32), (12, 16), (8, 16), (16, 32), (16, 16), (8, 16), (8, 16), (40, 32),
            (24, 32), (12, 16), (8, 16),
        )
    ]
    scratch += [
        pltpu.VMEM((8, 64, 384), F32),
        pltpu.VMEM((2, 64, 768), F32),
    ]
    for _ in range(N_BUNDLES):
        for shape in ((72,), (36,), (3, 9), (36,), (4, 9), (4, 9)):
            scratch.append(pltpu.VMEM(shape + (16, 128), BF))
    scratch.append(pltpu.VMEM((16, 32, 192), BF))
    scratch += [pltpu.VMEM((N_UNITS, 16, 128), BF)] * N_BUNDLES
    scratch += [
        pltpu.SemaphoreType.DMA((N_COPIES,)),
        pltpu.SemaphoreType.DMA((N_COPIES,)),
        pltpu.SemaphoreType.DMA((26,)),
    ]
    pred, *results = pl.pallas_call(
        body,
        out_shape=[jax.ShapeDtypeStruct((16, 32, 192), BF)]
        + [jax.ShapeDtypeStruct((N_UNITS, 16, 128), BF)] * N_BUNDLES,
        in_specs=[hbm] * 16,
        out_specs=[hbm] * 10,
        scratch_shapes=scratch,
        compiler_params=pltpu.CompilerParams(
            collective_id=0, has_side_effects=True, vmem_limit_bytes=60 * 1024 * 1024
        ),
        name="block_pair",
    )(*held, latents, cotangent)
    shapes = ((192, 576), (192, 192), (768, 384), (384, 1152), (384, 384), (384, 768))
    return tuple(
        pl.pallas_call(
            unpack,
            out_shape=[jax.ShapeDtypeStruct((1, 16, 32, 192), BF)]
            + [jax.ShapeDtypeStruct(s, F32) for s in shapes],
            in_specs=[hbm] * 10,
            out_specs=[hbm] * 7,
            scratch_shapes=[pltpu.VMEM((N_UNITS, 16, 128), BF)] * N_BUNDLES
            + [pltpu.VMEM(s, F32) for s in shapes]
            + [pltpu.VMEM((16, 32, 192), BF), pltpu.SemaphoreType.DMA((17,))],
            compiler_params=pltpu.CompilerParams(vmem_limit_bytes=60 * 1024 * 1024),
            name="unpack",
        )(pred, *results)
    )


def solution(mesh):
    split = P(None, "rows", "cols", None)
    return jax.shard_map(
        on_device,
        mesh=mesh,
        in_specs=(split,) + (P(),) * 14 + (split,),
        out_specs=(split,) + (P(),) * 6,
        check_vma=False,
    )
```

```python
import jax
import jax.numpy as jnp
from jax import lax
from jax.experimental import pallas as pl
from jax.experimental.pallas import tpu as pltpu
from jax.sharding import PartitionSpec as P

MESH = pl.DeviceIdType.MESH
BF = jnp.bfloat16
F32 = jnp.float32
EPS = 1e-05
SCALE = 32 ** (-0.5)
FINE_GROUPS = ((0, 128, 4), (128, 64, 2))
COARSE_GROUPS = ((0, 128, 4), (128, 128, 4), (256, 128, 4))
UNITS = (72,) * 8 + (24,) * 3
N_BUNDLES = len(UNITS)
ORDERS = (("y", "z", "x"), ("z", "x", "y"), ("x", "y", "z"))


def mm(a, b):
    return lax.dot_general(a, b, (((1,), (0,)), ((), ())), preferred_element_type=F32)


def mm_nt(a, b):
    return lax.dot_general(a, b, (((1,), (1,)), ((), ())), preferred_element_type=F32)


def mm_tn(a, b):
    return lax.dot_general(a, b, (((0,), (0,)), ((), ())), preferred_element_type=F32)


def norm(x):
    centred = x - jnp.mean(x, axis=-1, keepdims=True)
    inverse = lax.rsqrt(jnp.mean(centred * centred, axis=-1, keepdims=True) + EPS)
    return centred * inverse, inverse


def norm_back(upstream, unit, inverse, gain):
    e = upstream * gain
    return inverse * (
        e - jnp.mean(e, axis=-1, keepdims=True) - unit * jnp.mean(e * unit, axis=-1, keepdims=True)
    )


def head_masks(width, heads, dtype):
    lane = lax.broadcasted_iota(jnp.int32, (1, width), 1) // 32
    return [jnp.where(lane == h, 1.0, 0.0).astype(dtype) for h in range(heads)]


def spread(x, masks):
    return jnp.concatenate([x * m for m in masks], axis=0)


def fold(x, masks):
    total = x[:64] * masks[0]
    for h in range(1, len(masks)):
        total = total + x[64 * h : 64 * h + 64] * masks[h]
    return total


def parts_of(groups, x, w):
    return [x[64 * w : 64 * w + 64, at : at + wide] for at, wide, _ in groups]


def lanes_of(groups, x):
    return [x[:, 2 * at : 2 * at + 64 * heads] for at, _, heads in groups]


def attention(count, groups, q, k, v, bias, masks16, masks32):
    scores = []
    for w in range(count):
        line = [
            mm_nt(kg, spread(qg, m))
            for qg, kg, m in zip(parts_of(groups, q, w), parts_of(groups, k, w), masks16)
        ]
        scores.append(jnp.concatenate(line, axis=1))
    s = jnp.stack(scores) * SCALE + bias[None]
    e = jnp.exp(s - jnp.max(s, axis=1, keepdims=True))
    probs = e * (1.0 / jnp.sum(e, axis=1, keepdims=True))
    weights = probs.astype(BF)
    mixed = []
    for w in range(count):
        line = [
            fold(mm_tn(pg, vg), m)
            for pg, vg, m in zip(lanes_of(groups, weights[w]), parts_of(groups, v, w), masks32)
        ]
        mixed.append(jnp.concatenate(line, axis=1))
    return probs, jnp.concatenate(mixed, axis=0).astype(BF)


def attention_back(count, groups, q, k, v, probs, mixed_grad, masks16, masks32, between):
    grads = []
    many = []
    for w in range(count):
        many.append(
            [spread(mg, m) for mg, m in zip(parts_of(groups, mixed_grad, w), masks16)]
        )
        line = [mm_nt(vg, mg) for vg, mg in zip(parts_of(groups, v, w), many[w])]
        grads.append(jnp.concatenate(line, axis=1))
    wg = jnp.stack(grads).astype(BF).astype(F32)
    sg = (probs * (wg - jnp.sum(probs * wg, axis=1, keepdims=True)) * SCALE).astype(BF)
    weights = probs.astype(BF)
    out = [[], [], []]
    for w in range(count):
        between(w)
        scored, weighed = lanes_of(groups, sg[w]), lanes_of(groups, weights[w])
        qs, ks = parts_of(groups, q, w), parts_of(groups, k, w)
        dq = [fold(mm_tn(x, kg), m) for x, kg, m in zip(scored, ks, masks32)]
        dk = [mm(x, spread(qg, m)) for x, qg, m in zip(scored, qs, masks16)]
        dv = [mm(x, mg) for x, mg in zip(weighed, many[w])]
        for have, line in zip(out, (dq, dk, dv)):
            have.append(jnp.concatenate(line, axis=1))
    return [jnp.concatenate(x, axis=0).astype(BF) for x in out]


def folded_place(u):
    v = u & 15
    return (u - v) + (v & 1) * 8 + (v >> 1)


def true_place(p):
    v = p & 15
    return (p - v) + (v & 7) * 2 + (v >> 3)


def units(x):
    return x.reshape(x.shape[0] // 16, 16, 128)


class Net:
    def __init__(self, send, recv):
        self.r = lax.axis_index("rows")
        self.c = lax.axis_index("cols")
        r, c = self.r, self.c
        self.core = lax.rem(r, 2)
        xlo = lax.rem(r // 2, 2)
        self.y = r // 4
        self.z = c // 2
        xhi = lax.rem(c, 2)
        self.x = xhi * 2 + xlo
        self.low = lax.rem(r, 4)
        self.xhi = xhi
        self.send, self.recv = send, recv
        self.count = 0
        self.copies = []

    def near(self, dr, dc):
        return (lax.rem(self.r + dr + 16, 16), lax.rem(self.c + dc + 8, 8))

    def place(self, axis):
        return {"x": self.x, "y": self.y, "z": self.z}[axis]

    def peer(self, axis, index, core=None):
        core = self.core if core is None else core
        low = self.low - self.core + core
        if axis == "y":
            return (index * 4 + low, self.c)
        if axis == "z":
            return (self.y * 4 + low, index * 2 + self.xhi)
        return (self.y * 4 + lax.rem(index, 2) * 2 + core, self.z * 2 + index // 2)

    def sibling(self):
        return (self.r + 1 - 2 * self.core, self.c)

    def start(self, source, target, device):
        n = self.count
        self.count += 1
        copy = pltpu.make_async_remote_copy(
            src_ref=source,
            dst_ref=target,
            send_sem=self.send.at[n],
            recv_sem=self.recv.at[n],
            device_id=device,
            device_id_type=MESH,
        )
        copy.start()
        self.copies.append(copy)
        return copy

    def greet(self):
        sem = pltpu.get_barrier_semaphore()
        others = [self.near(a, b) for a in (-1, 0, 1) for b in (-1, 0, 1) if (a, b) != (0, 0)]
        others.append(self.sibling())
        for axis in "xyz":
            others += [self.peer(axis, lax.rem(self.place(axis) + k, 4)) for k in (1, 2, 3)]
            others += [
                self.peer(axis, lax.rem(self.place(axis) + k, 4), 1 - self.core)
                for k in (1, 2, 3)
            ]
        for device in others:
            pl.semaphore_signal(sem, inc=1, device_id=device, device_id_type=MESH)
        self.greeted = len(others)

    def gather(self):
        pl.semaphore_wait(pltpu.get_barrier_semaphore(), self.greeted)


class Reduce:
    def __init__(self, net, order, terms, got_core, got_a, sum_a, got_b, got_c, result):
        self.net, self.order = net, order
        self.terms, self.got_core, self.got_a, self.sum_a = terms, got_core, got_a, sum_a
        self.got_b, self.got_c, self.result = got_b, got_c, result
        self.half, self.part = terms.shape[0] // 2, terms.shape[0] // 8
        self.stage = 0
        self.flight = []

    def step(self):
        getattr(self, "step%d" % self.stage)()
        self.stage += 1

    def arrive(self):
        for copy in self.flight:
            copy.wait_recv()

    def to_peers(self, axis, source, target):
        net = self.net
        me = net.place(axis)
        self.flight = []
        for k in (1, 2, 3):
            to = lax.rem(me + k, 4)
            self.flight.append(net.start(source(to), target(k), net.peer(axis, to)))

    def spread_out(self, total, got, axis):
        me = self.net.place(axis)
        got[pl.ds(me, 1)] = total.astype(BF)[None]
        self.to_peers(axis, lambda to: got.at[me], lambda k: got.at[me])

    def summed(self, got):
        total = got[0].astype(F32)
        for k in (1, 2, 3):
            total = total + got[k].astype(F32)
        return total

    def step0(self):
        net, half = self.net, self.half
        self.flight = [
            net.start(self.terms.at[pl.ds((1 - net.core) * half, half)], self.got_core, net.sibling())
        ]

    def step1(self):
        net, half, part = self.net, self.half, self.part
        self.arrive()
        own = self.terms[pl.ds(net.core * half, half)].astype(F32)
        self.sum_a[...] = (own + self.got_core[...].astype(F32)).astype(BF)
        self.to_peers(
            self.order[0],
            lambda to: self.sum_a.at[pl.ds(to * part, part)],
            lambda k: self.got_a.at[k - 1],
        )

    def step2(self):
        self.arrive()
        me = self.net.place(self.order[0])
        total = self.sum_a[pl.ds(me * self.part, self.part)].astype(F32)
        for k in range(3):
            total = total + self.got_a[k].astype(F32)
        self.spread_out(total, self.got_b, self.order[1])

    def step3(self):
        self.arrive()
        self.spread_out(self.summed(self.got_b), self.got_c, self.order[2])

    def step4(self):
        self.arrive()
        at = self.net.core * self.half + self.net.place(self.order[0]) * self.part
        mine = self.result.at[pl.ds(at, self.part)]
        mine[...] = self.summed(self.got_c).astype(BF)
        self.to_peers(self.order[0], lambda to: mine, lambda k: mine)

    def step5(self):
        self.arrive()
        mine = self.result.at[pl.ds(self.net.core * self.half, self.half)]
        self.flight = [self.net.start(mine, mine, self.net.sibling())]

    def step6(self):
        self.arrive()


class Direct(Reduce):
    def __init__(self, net, order, terms, got_a, got_b, got_c, result):
        super().__init__(net, order, terms, None, got_a, None, got_b, got_c, result)
        self.at = (net.core * 4 + net.place(order[0])) * self.part

    def to_eight(self, source, target):
        net = self.net
        me = net.place(self.order[0])
        self.flight = []
        for k in range(1, 8):
            to, core = lax.rem(me + k, 4), lax.rem(net.core + k // 4, 2)
            self.flight.append(
                net.start(
                    source((core * 4 + to) * self.part),
                    target(k - 1),
                    net.peer(self.order[0], to, core),
                )
            )

    def step0(self):
        self.to_eight(lambda at: self.terms.at[pl.ds(at, self.part)], lambda k: self.got_a.at[k])

    def step1(self):
        self.arrive()
        total = self.terms[pl.ds(self.at, self.part)].astype(F32)
        for k in range(7):
            total = total + self.got_a[k].astype(F32)
        self.spread_out(total, self.got_b, self.order[1])

    def step2(self):
        self.step3()

    def step3(self):
        if self.stage == 2:
            Reduce.step3(self)
        else:
            self.arrive()
            mine = self.result.at[pl.ds(self.at, self.part)]
            mine[...] = self.summed(self.got_c).astype(BF)
            self.to_eight(lambda at: mine, lambda k: mine)

    def step4(self):
        self.arrive()
        self.stage = 6


def to_map(x, rows, cols):
    wide = cols // 8
    out = []
    for i in range(rows):
        base = (i // 8) * wide
        out.append(
            jnp.concatenate(
                [x[(base + w) * 64 + (i % 8) * 8 :][:8] for w in range(wide)], axis=0
            )
        )
    return out


def to_windows(rows_list, cols):
    wide = cols // 8
    pieces = []
    for wr in range(len(rows_list) // 8):
        for w in range(wide):
            for i in range(8):
                pieces.append(rows_list[wr * 8 + i][8 * w : 8 * w + 8])
    return jnp.concatenate(pieces, axis=0)


def paired(rows_list):
    out = []
    for di in (0, 1):
        for dj in (0, 1):
            out.append(
                jnp.concatenate(
                    [
                        rows_list[2 * i + di][16 * w + 8 * dj :][:8]
                        for w in (0, 1)
                        for i in range(8)
                    ],
                    axis=0,
                )
            )
    return out


def unpaired(parts):
    rows_list = []
    for row in range(16):
        i, di = row // 2, row % 2
        rows_list.append(
            jnp.concatenate(
                [
                    parts[2 * di + dj][64 * w + 8 * i :][:8]
                    for w in (0, 1)
                    for dj in (0, 1)
                ],
                axis=0,
            )
        )
    return rows_list


def packed(x):
    return x.reshape(128, x.shape[-1]).astype(BF).reshape(8, 16, x.shape[-1])


def pack_rows(x):
    tails = jnp.concatenate([x[:, :16, 128:], x[:, 16:, 128:]], axis=2)
    return jnp.concatenate([x[:, :, :128], tails], axis=1)


def open_rows(x):
    tails = jnp.concatenate([x[:, 32:, :64], x[:, 32:, 64:]], axis=1)
    return jnp.concatenate([x[:, :32], tails], axis=2)


def pack_tiles(x):
    m = x.shape[0] // 2
    x = x.reshape(m, 2, 16, 192)
    tails = jnp.concatenate([x[:, 0, :, 128:], x[:, 1, :, 128:]], axis=2)
    return jnp.stack([x[:, 0, :, :128], x[:, 1, :, :128], tails], axis=1).reshape(3 * m, 16, 128)


def open_tiles(x):
    m = x.shape[0] // 3
    x = x.reshape(m, 3, 16, 128)
    first = jnp.concatenate([x[:, 0], x[:, 2, :, :64]], axis=2)
    second = jnp.concatenate([x[:, 1], x[:, 2, :, 64:]], axis=2)
    return jnp.stack([first, second], axis=1).reshape(2 * m, 16, 192)


def one_hot(rows_out, cols_in, place):
    x = lax.broadcasted_iota(jnp.int32, (rows_out, cols_in), 0)
    u = lax.broadcasted_iota(jnp.int32, (rows_out, cols_in), 1)
    return jnp.where(place(x) == u, 1.0, 0.0).astype(BF)


def body(*refs):
    (
        offsets, actions, table, fgain, fqkv, fbias, fproj, mgain, mweight, cgain, cqkv, cbias,
        cproj, hweight,
    ) = refs[28:42]
    lat_hbm, cot_hbm = refs[14:16]
    pred_out, *result_outs = refs[16:28]
    (
        lat, lat_left, lat_right, cot, ahead, ahead_side, head, head_rows, back, back_side,
        lat_rows_out, lat_rows_in, lat_out, lat_left_in, lat_right_in, cot_rows_out, cot_rows_in,
        cot_next_out, cot_next_in, cot_prev_out, cot_prev_in, ahead_rows_out, ahead_rows_in,
        ahead_out, ahead_in, back_rows_out, back_rows_in, back_out, back_in, head_prev_out,
        head_prev_in, head_next_out, head_next_in, head_rows_out, head_rows_in, fprobs, cprobs,
    ) = refs[42:79]
    rest = refs[79:]
    works = [rest[6 * g : 6 * g + 6] for g in range(8)]
    works += [rest[48 + 4 * g : 52 + 4 * g] for g in range(3)]
    pred, *results = rest[60:72]
    send, recv, local = rest[72:]
    loads = [
        pltpu.make_async_copy(refs[i], refs[28 + i], local.at[2 + i]) for i in range(14)
    ]
    net = Net(send, recv)
    net.greet()
    bundles = [
        (Reduce if g < 8 else Direct)(net, ORDERS[g % 3], *works[g], results[g])
        for g in range(N_BUNDLES)
    ]

    def advance(*numbers):
        for g in numbers:
            bundles[g].step()
            if bundles[g].stage == 7:
                copy = pltpu.make_async_copy(results[g], result_outs[g], local.at[17 + g])
                copy.start()
                stores.append(copy)

    stores = []
    own_lat = pltpu.make_async_copy(lat_hbm.at[0], lat.at[pl.ds(8, 16)], local.at[0])
    own_cot = pltpu.make_async_copy(cot_hbm.at[0], cot.at[pl.ds(8, 16)], local.at[1])
    for copy in [own_lat] + loads[:6] + loads[6:] + [own_cot]:
        copy.start()

    own_lat.wait()
    low = lat[pl.ds(8, 16), pl.ds(0, 16)].astype(F32)
    high = lat[pl.ds(8, 16), pl.ds(16, 16)].astype(F32)
    lat_out[0] = pack_tiles(packed(low[:, :8]))
    lat_out[1] = pack_tiles(packed(high[:, 8:]))
    lat_rows_out[0] = pack_rows(lat[pl.ds(8, 8)])
    lat_rows_out[1] = pack_rows(lat[pl.ds(16, 8)])
    net.gather()
    lat_halo = []
    for side, dc, target in ((0, -1, lat_right_in), (1, 1, lat_left_in)):
        for dr, fr, nr, tr in ((0, 0, 12, 6), (-1, 0, 6, 18), (1, 6, 6, 0)):
            lat_halo.append(
                net.start(
                    lat_out.at[side, pl.ds(fr, nr)], target.at[pl.ds(tr, nr)], net.near(dr, dc)
                )
            )
    lat_halo.append(net.start(lat_rows_out.at[0], lat_rows_in.at[1], net.near(-1, 0)))
    lat_halo.append(net.start(lat_rows_out.at[1], lat_rows_in.at[0], net.near(1, 0)))

    for copy in loads:
        copy.wait()
    a0, a1 = offsets[0, 0], offsets[0, 1]
    b0, b1 = 2 * offsets[1, 0], 2 * offsets[1, 1]
    d0, d1 = lax.rem(b0 - a0 + 8, 8), lax.rem(b1 - a1 + 8, 8)
    s0, s1 = lax.rem(b0 - d0 + 8, 16) - 8, lax.rem(b1 - d1 + 8, 16) - 8
    t0, t1 = s0 + d0, s1 + d1
    code = lax.broadcasted_iota(jnp.int32, (8, 256), 1)
    counts = jnp.zeros((8, 256), F32)
    for j in range(16):
        counts = counts + jnp.where(code == actions[0, j], 1.0, 0.0)
    condition = mm_nt(counts.astype(BF), table[...])[:1] * (1.0 / 16.0)
    f_masks16 = [head_masks(w, h, BF) for _, w, h in FINE_GROUPS]
    f_masks32 = [head_masks(w, h, F32) for _, w, h in FINE_GROUPS]
    c_masks16 = [head_masks(w, h, BF) for _, w, h in COARSE_GROUPS]
    c_masks32 = [head_masks(w, h, F32) for _, w, h in COARSE_GROUPS]
    fb = fbias[...].reshape(384, 64).T
    cb = cbias[...].reshape(768, 64).T
    fw = [fqkv[:, 192 * i : 192 * i + 192] for i in range(3)]
    cw = [cqkv[:, 384 * i : 384 * i + 384] for i in range(3)]
    fproj_t, cproj_t, hweight_t = fproj[...].T, cproj[...].T, hweight[...].T
    cw_t, mweight_t = [w.T for w in cw], mweight[...].T
    f_gain = fgain[...].reshape(1, 192)
    m_gain = mgain[...].reshape(1, 768)
    c_gain = cgain[...].reshape(1, 384)

    def two_picks(rows_out, cols_in, parity, place):
        return [
            one_hot(rows_out, cols_in, lambda x, p=p: place(x, p))
            for p in (parity * 8, 8 - parity * 8)
        ]

    own_cot.wait()
    cot_rows_out[...] = pack_rows(cot[pl.ds(8, 16)])

    for copy in lat_halo:
        copy.wait_recv()
    cot_rows = [
        net.start(cot_rows_out, cot_rows_in.at[pl.ds(8, 16)], net.near(-1, 0)),
        net.start(cot_rows_out.at[pl.ds(8, 8)], cot_rows_in.at[pl.ds(0, 8)], net.near(1, 0)),
    ]
    lat_left[...] = open_tiles(lat_left_in[...])
    lat_right[...] = open_tiles(lat_right_in[...])
    lat[pl.ds(0, 8)] = open_rows(lat_rows_in[0])
    lat[pl.ds(24, 8)] = open_rows(lat_rows_in[1])

    def lat_place(x, p):
        u = x + (s1 + 8)
        return jnp.where(u < 8, 32 + p + u, jnp.where(u < 40, u - 8, 48 + p + u - 40))

    pick = two_picks(32, 64, (8 + s0) & 1, lat_place)
    block = lat[pl.ds(8 + s0, 16)]
    rows_list = []
    for i in range(16):
        pair = (8 + s0 + i) >> 1
        source = jnp.concatenate([block[i], lat_left[pair], lat_right[pair]], axis=0)
        rows_list.append(mm(pick[i % 2], source))
    residual = to_windows(rows_list, 32) + condition
    n1 = (norm(residual)[0] * f_gain).astype(BF)
    fq, fk, fv = (mm(n1, w).astype(BF) for w in fw)
    f_probs, f_mixed = attention(8, FINE_GROUPS, fq, fk, fv, fb, f_masks16, f_masks32)
    fprobs[...] = f_probs
    attn = mm(f_mixed, fproj[...]).astype(BF)
    f_next = residual + attn.astype(F32)
    for i, row in enumerate(to_map(f_next, 16, 32)):
        ahead[i] = row.astype(BF)
    edges = [f_next[256 * wr : 256 * wr + 64].astype(BF) for wr in range(2)]
    ahead_out[...] = pack_tiles(jnp.concatenate(edges, axis=0).reshape(8, 16, 192))
    ahead_rows_out[...] = pack_rows(ahead[pl.ds(0, 8)])
    ahead_halo = [
        net.start(ahead_out, ahead_in.at[pl.ds(0, 12)], net.near(0, -1)),
        net.start(ahead_out.at[pl.ds(0, 6)], ahead_in.at[pl.ds(12, 6)], net.near(-1, -1)),
        net.start(ahead_rows_out, ahead_rows_in, net.near(-1, 0)),
    ]

    for copy in cot_rows:
        copy.wait_recv()
    cot[pl.ds(0, 8)] = open_rows(cot_rows_in[pl.ds(0, 8)])
    cot[pl.ds(24, 16)] = open_rows(cot_rows_in[pl.ds(8, 16)])
    cot_main = cot[pl.ds(8 + t0, 16)]
    cot_next_out[...] = pack_tiles(cot_main[:, :16])
    cot_prev_out[...] = pack_tiles(packed(cot_main[:, 16:].astype(F32)[:, 8:]))
    cot_halo = [
        net.start(cot_next_out, cot_next_in, net.near(0, -1)),
        net.start(cot_prev_out, cot_prev_in, net.near(0, 1)),
    ]

    def ahead_place(x, p):
        u = true_place(x) + d1
        return jnp.where(u < 32, u, u + p)

    pick = two_picks(32, 48, d0 & 1, ahead_place)
    for copy in ahead_halo:
        copy.wait_recv()
    ahead_side[...] = open_tiles(ahead_in[...])
    ahead[pl.ds(16, 8)] = open_rows(ahead_rows_in[...])
    block = ahead[pl.ds(d0, 16)]
    rows_list = []
    for i in range(16):
        source = jnp.concatenate([block[i], ahead_side[(d0 + i) >> 1]], axis=0)
        rows_list.append(mm(pick[i % 2], source))
    merged = jnp.concatenate(paired(rows_list), axis=1)
    m_unit, m_inverse = norm(merged)
    n2 = (m_unit * m_gain).astype(BF)
    c_residual = mm(n2, mweight[...]).astype(BF).astype(F32)
    c_unit, c_inverse = norm(c_residual)
    n3 = (c_unit * c_gain).astype(BF)
    cq, ck, cv = (mm(n3, w).astype(BF) for w in cw)
    c_probs, c_mixed = attention(2, COARSE_GROUPS, cq, ck, cv, cb, c_masks16, c_masks32)
    cprobs[...] = c_probs
    c_attn = mm(c_mixed, cproj[...]).astype(BF)
    c_next = (c_residual + c_attn.astype(F32)).astype(BF)

    for copy in cot_halo:
        copy.wait_recv()

    def cot_place(x, p):
        u = true_place(x) + (t1 + 8)
        return jnp.where(u < 8, 48 + p + u, u - 8)

    pick = two_picks(32, 64, 0, cot_place)
    cot_next, cot_prev = open_tiles(cot_next_in[...]), open_tiles(cot_prev_in[...])
    rows_list = []
    for i in range(16):
        source = jnp.concatenate([cot_main[i], cot_next[i], cot_prev[i // 2]], axis=0)
        rows_list.append(mm(pick[i % 2], source))
    grad_out = jnp.concatenate(paired(rows_list), axis=1).astype(BF)
    grad_next = mm(grad_out, hweight_t).astype(BF)
    c_mixed_grad = mm(grad_next, cproj_t).astype(BF)

    g_head = mm_tn(c_next, grad_out)
    for j in range(6):
        works[j // 3][0][pl.ds(24 * (j % 3), 24)] = units(
            g_head[:, 128 * j : 128 * j + 128].astype(BF)
        )
    g_cproj = mm_tn(c_mixed, grad_next)
    for j in range(3):
        works[2][0][pl.ds(24 * j, 24)] = units(g_cproj[:, 128 * j : 128 * j + 128].astype(BF))
    advance(0, 1, 2)

    c_packed = attention_back(
        2, COARSE_GROUPS, cq, ck, cv, cprobs[...], c_mixed_grad, c_masks16, c_masks32,
        lambda w: None,
    )
    rolled = mm(c_packed[0], cw_t[0]) + mm(c_packed[1], cw_t[1]) + mm(c_packed[2], cw_t[2])
    grad_residual = (
        grad_next.astype(F32)
        + norm_back(rolled.astype(BF).astype(F32), c_unit, c_inverse, c_gain)
    ).astype(BF)
    norm_grad = mm(grad_residual, mweight_t).astype(BF).astype(F32)
    merged_grad = norm_back(norm_grad, m_unit, m_inverse, m_gain)
    rows_list = [
        row.astype(BF)
        for row in unpaired([merged_grad[:, 192 * t : 192 * t + 192] for t in range(4)])
    ]
    last = one_hot(16, 64, lambda x: (x >> 3) * 32 + folded_place(24 + (x & 7)))
    edges = []
    for i in range(8):
        both = jnp.concatenate(rows_list[2 * i : 2 * i + 2], axis=0)
        back[8 + 2 * i], back[9 + 2 * i] = rows_list[2 * i], rows_list[2 * i + 1]
        edges.append(mm(last, both).astype(BF))
    back_out[...] = pack_tiles(jnp.stack(edges))
    back_rows_out[...] = pack_rows(jnp.stack(rows_list[8:]))
    back_halo = [
        net.start(back_out, back_in.at[pl.ds(6, 12)], net.near(0, 1)),
        net.start(back_out.at[pl.ds(6, 6)], back_in.at[pl.ds(0, 6)], net.near(1, 1)),
        net.start(back_rows_out, back_rows_in, net.near(1, 0)),
    ]
    advance(0, 1, 2)
    for t in range(3):
        g_part = mm_tn(n3, c_packed[t])
        for j in range(3):
            works[3 + t][0][pl.ds(24 * j, 24)] = units(
                g_part[:, 128 * j : 128 * j + 128].astype(BF)
            )
    advance(3, 4, 5)
    g_merge = mm_tn(n2, grad_residual)
    for t in range(2):
        for j in range(3):
            works[6 + t][0][pl.ds(24 * j, 24)] = units(
                g_merge[384 * t : 384 * t + 384, 128 * j : 128 * j + 128].astype(BF)
            )
    advance(6, 7)
    advance(3, 4, 5)
    head_out = mm(c_next, hweight[...])
    for i, row in enumerate(unpaired([head_out[:, 192 * t : 192 * t + 192] for t in range(4)])):
        head[i] = row.astype(BF)
    first = one_hot(16, 64, lambda x: (x >> 3) * 32 + folded_place(x & 7))
    edges = []
    for i in range(8):
        both = jnp.concatenate([head[2 * i], head[2 * i + 1]], axis=0)
        edges.append(mm(first, both).astype(BF))
    head_next_out[...] = pack_tiles(jnp.stack(edges))
    head_prev_out[...] = pack_tiles(head[:, pl.ds(16, 16)])

    def back_place(x, p):
        u = x + (8 - d1)
        return jnp.where(u < 8, 32 + p + u, folded_place(u - 8))

    pick = two_picks(32, 48, d0 & 1, back_place)
    for copy in back_halo:
        copy.wait_recv()
    advance(6, 7)
    head_halo = [
        net.start(head_prev_out, head_prev_in, net.near(0, 1)),
        net.start(head_next_out, head_next_in, net.near(0, -1)),
    ]

    def turn_rows():
        for copy in head_halo:
            copy.wait_recv()
        pick = two_picks(32, 64, 0, head_place)
        head_prev, head_next = open_tiles(head_prev_in[...]), open_tiles(head_next_in[...])
        for i in range(16):
            source = jnp.concatenate([head[i], head_prev[i], head_next[i // 2]], axis=0)
            head_rows[16 + i] = mm(pick[i % 2], source).astype(BF)
        head_rows_out[...] = pack_rows(head_rows[pl.ds(16, 16)])
        return [
            net.start(head_rows_out, head_rows_in.at[pl.ds(0, 16)], net.near(1, 0)),
            net.start(head_rows_out.at[pl.ds(0, 8)], head_rows_in.at[pl.ds(16, 8)], net.near(-1, 0)),
        ]

    def head_place(x, p):
        u = x + (16 - t1)
        return jnp.where(
            u < 16, 32 + folded_place(u), jnp.where(u < 48, folded_place(u - 16), u + p)
        )

    back_side[...] = open_tiles(back_in[...])
    back[pl.ds(0, 8)] = open_rows(back_rows_in[...])
    block = back[pl.ds(8 - d0, 16)]
    rows_list = []
    for i in range(16):
        source = jnp.concatenate([block[i], back_side[(8 - d0 + i) >> 1]], axis=0)
        rows_list.append(mm(pick[i % 2], source))
    f_grad = to_windows(rows_list, 32).astype(BF)
    f_mixed_grad = mm(f_grad, fproj_t).astype(BF)
    g_fproj = mm_tn(f_mixed, f_grad)

    def between(w):
        if w == 0:
            advance(0, 1, 2)
        if w == 3:
            advance(3, 4, 5, 6, 7)
        if w == 6:
            advance(0, 1, 2)

    f_packed = attention_back(
        8, FINE_GROUPS, fq, fk, fv, fprobs[...], f_mixed_grad, f_masks16, f_masks32, between
    )
    g_parts = [mm_tn(n1, x) for x in f_packed]
    g_parts.append(g_fproj)
    for t in range(4):
        works[8 + t // 2][0][pl.ds(12 * (t % 2), 12)] = units(g_parts[t][:, :128].astype(BF))
    for t in (0, 2):
        tails = jnp.concatenate([g_parts[t][:, 128:], g_parts[t + 1][:, 128:]], axis=1)
        works[10][0][pl.ds(6 * t, 12)] = units(tails.astype(BF))
    advance(8, 9, 10)
    advance(3, 4, 5, 6, 7)
    advance(8, 9, 10)
    advance(0, 1, 2)
    advance(3, 4, 5, 6, 7)
    advance(8, 9, 10)
    rows_halo = turn_rows()
    advance(0, 1, 2)
    advance(8, 9, 10)
    advance(3, 4, 5, 6, 7)
    advance(0, 1, 2)
    for copy in rows_halo:
        copy.wait_recv()
    head_rows[pl.ds(0, 16)] = open_rows(head_rows_in[pl.ds(0, 16)])
    head_rows[pl.ds(32, 8)] = open_rows(head_rows_in[pl.ds(16, 8)])
    pred[...] = head_rows[pl.ds(16 - t0, 16)]
    stores.append(pltpu.make_async_copy(pred, pred_out, local.at[16]))
    stores[-1].start()
    advance(3, 4, 5, 6, 7)
    advance(8, 9, 10)
    for copy in stores:
        copy.wait()
    for copy in net.copies:
        copy.wait_send()


N_COPIES = 8 + 4 + 3 + 3 + 4 + 14 * 8 + 20 * 3


def unpack(*refs):
    pred_in, *heres = refs[:12]
    pred_out, *outs = refs[12:19]
    packs, wides, held, sems = refs[19:30], refs[30:36], refs[36], refs[37]
    fq, fp, me, cq, cp, he = wides
    pass_in = pltpu.make_async_copy(pred_in, held, sems.at[17])
    pass_on = pltpu.make_async_copy(held, pred_out.at[0], sems.at[18])
    loads = [pltpu.make_async_copy(heres[g], packs[g], sems.at[g]) for g in range(11)]
    stores = [pltpu.make_async_copy(wides[i], outs[i], sems.at[11 + i]) for i in range(6)]
    for copy in loads + [pass_in]:
        copy.start()

    def take(g, at, count):
        return packs[g][pl.ds(at, count)].reshape(count * 16, 128).astype(F32)

    for t in range(3):
        loads[3 + t].wait()
        for j in range(3):
            cq[:, pl.ds(384 * t + 128 * j, 128)] = take(3 + t, 24 * j, 24)
    stores[3].start()
    for t in range(2):
        loads[t].wait()
        for j in range(3):
            he[:, pl.ds(384 * t + 128 * j, 128)] = take(t, 24 * j, 24)
    stores[5].start()
    for t in range(2):
        loads[6 + t].wait()
        for j in range(3):
            me[pl.ds(384 * t, 384), pl.ds(128 * j, 128)] = take(6 + t, 24 * j, 24)
    stores[2].start()
    loads[2].wait()
    for j in range(3):
        cp[:, pl.ds(128 * j, 128)] = take(2, 24 * j, 24)
    stores[4].start()
    pass_in.wait()
    pass_on.start()
    for g in (8, 9, 10):
        loads[g].wait()
    parts = [take(8 + t // 2, 12 * (t % 2), 12) for t in range(4)]
    tails = [take(10, 12 * t, 12) for t in range(2)]
    fq[...] = jnp.concatenate(
        [parts[0], tails[0][:, :64], parts[1], tails[0][:, 64:], parts[2], tails[1][:, :64]], axis=1
    )
    fp[...] = jnp.concatenate([parts[3], tails[1][:, 64:]], axis=1)
    stores[0].start()
    stores[1].start()
    for copy in stores + [pass_on]:
        copy.wait()


def on_device(
    latents, actions, action_table, offsets, fine_gain, fine_qkv, fine_bias, fine_proj, merge_gain,
    merge_weight, coarse_gain, coarse_qkv, coarse_bias, coarse_proj, head_weight, cotangent,
):
    hbm = pl.BlockSpec(memory_space=pltpu.HBM)
    held = (
        offsets, actions, action_table.T, fine_gain, fine_qkv, fine_bias, fine_proj, merge_gain,
        merge_weight, coarse_gain, coarse_qkv, coarse_bias, coarse_proj, head_weight,
    )
    scratch = [pltpu.SMEM(x.shape, x.dtype) for x in held[:2]]
    scratch += [pltpu.VMEM(x.shape, x.dtype) for x in held[2:]]
    scratch += [
        pltpu.VMEM(shape + (192,), BF)
        for shape in (
            (32, 32), (16, 16), (16, 16), (40, 32), (24, 32), (12, 16), (16, 32), (40, 32), (24, 32),
            (12, 16),
        )
    ]
    scratch += [
        pltpu.VMEM(shape + (128,), BF)
        for shape in (
            (2, 8, 48), (2, 8, 48), (2, 12, 16), (24, 16), (24, 16), (16, 48), (24, 48), (24, 16),
            (24, 16), (12, 16), (12, 16), (8, 48), (8, 48), (12, 16), (18, 16), (8, 48), (8, 48),
            (12, 16), (18, 16), (24, 16), (24, 16), (12, 16), (12, 16), (16, 48), (24, 48),
        )
    ]
    scratch += [
        pltpu.VMEM((8, 64, 384), F32),
        pltpu.VMEM((2, 64, 768), F32),
    ]
    wide = ((72,), (36,), (3, 9), (36,), (4, 9), (4, 9))
    narrow = ((24,), (7, 3), (4, 3), (4, 3))
    for shape in wide * 8 + narrow * 3:
        scratch.append(pltpu.VMEM(shape + (16, 128), BF))
    scratch.append(pltpu.VMEM((16, 32, 192), BF))
    scratch += [pltpu.VMEM((n, 16, 128), BF) for n in UNITS]
    scratch += [
        pltpu.SemaphoreType.DMA((N_COPIES,)),
        pltpu.SemaphoreType.DMA((N_COPIES,)),
        pltpu.SemaphoreType.DMA((28,)),
    ]
    pred, *results = pl.pallas_call(
        body,
        out_shape=[jax.ShapeDtypeStruct((16, 32, 192), BF)]
        + [jax.ShapeDtypeStruct((n, 16, 128), BF) for n in UNITS],
        in_specs=[hbm] * 16,
        out_specs=[hbm] * 12,
        scratch_shapes=scratch,
        compiler_params=pltpu.CompilerParams(
            collective_id=0, has_side_effects=True, vmem_limit_bytes=60 * 1024 * 1024
        ),
        name="block_pair",
    )(*held, latents, cotangent)
    shapes = ((192, 576), (192, 192), (768, 384), (384, 1152), (384, 384), (384, 768))
    return tuple(
        pl.pallas_call(
            unpack,
            out_shape=[jax.ShapeDtypeStruct((1, 16, 32, 192), BF)]
            + [jax.ShapeDtypeStruct(s, F32) for s in shapes],
            in_specs=[hbm] * 12,
            out_specs=[hbm] * 7,
            scratch_shapes=[pltpu.VMEM((n, 16, 128), BF) for n in UNITS]
            + [pltpu.VMEM(s, F32) for s in shapes]
            + [pltpu.VMEM((16, 32, 192), BF), pltpu.SemaphoreType.DMA((19,))],
            compiler_params=pltpu.CompilerParams(vmem_limit_bytes=60 * 1024 * 1024),
            name="unpack",
        )(pred, *results)
    )


def solution(mesh):
    split = P(None, "rows", "cols", None)
    return jax.shard_map(
        on_device,
        mesh=mesh,
        in_specs=(split,) + (P(),) * 14 + (split,),
        out_specs=(split,) + (P(),) * 6,
        check_vma=False,
    )
```

```python
import jax
import jax.numpy as jnp
from jax import lax
from jax.experimental import pallas as pl
from jax.experimental.pallas import tpu as pltpu
from jax.sharding import PartitionSpec as P

MESH = pl.DeviceIdType.MESH
BF = jnp.bfloat16
F32 = jnp.float32
EPS = 1e-05
SCALE = 32 ** (-0.5)
FINE_GROUPS = ((0, 128, 4), (128, 64, 2))
COARSE_GROUPS = ((0, 128, 4), (128, 128, 4), (256, 128, 4))
UNITS = (72,) * 8 + (24,) * 3
N_BUNDLES = len(UNITS)
ORDERS = (("y", "z", "x"), ("z", "x", "y"), ("x", "y", "z"))


def mm(a, b):
    return lax.dot_general(a, b, (((1,), (0,)), ((), ())), preferred_element_type=F32)


def mm_nt(a, b):
    return lax.dot_general(a, b, (((1,), (1,)), ((), ())), preferred_element_type=F32)


def mm_tn(a, b):
    return lax.dot_general(a, b, (((0,), (0,)), ((), ())), preferred_element_type=F32)


def norm(x):
    centred = x - jnp.mean(x, axis=-1, keepdims=True)
    inverse = lax.rsqrt(jnp.mean(centred * centred, axis=-1, keepdims=True) + EPS)
    return centred * inverse, inverse


def norm_back(upstream, unit, inverse, gain):
    e = upstream * gain
    return inverse * (
        e - jnp.mean(e, axis=-1, keepdims=True) - unit * jnp.mean(e * unit, axis=-1, keepdims=True)
    )


def head_masks(width, heads, dtype):
    lane = lax.broadcasted_iota(jnp.int32, (1, width), 1) // 32
    return [jnp.where(lane == h, 1.0, 0.0).astype(dtype) for h in range(heads)]


def spread(x, masks):
    return jnp.concatenate([x * m for m in masks], axis=0)


def fold(x, masks):
    total = x[:64] * masks[0]
    for h in range(1, len(masks)):
        total = total + x[64 * h : 64 * h + 64] * masks[h]
    return total


def parts_of(groups, x, w):
    return [x[64 * w : 64 * w + 64, at : at + wide] for at, wide, _ in groups]


def lanes_of(groups, x):
    return [x[:, 2 * at : 2 * at + 64 * heads] for at, _, heads in groups]


def attention(count, groups, q, k, v, bias, masks16, masks32):
    scores = []
    for w in range(count):
        line = [
            mm_nt(kg, spread(qg, m))
            for qg, kg, m in zip(parts_of(groups, q, w), parts_of(groups, k, w), masks16)
        ]
        scores.append(jnp.concatenate(line, axis=1))
    s = jnp.stack(scores) * SCALE + bias[None]
    e = jnp.exp(s - jnp.max(s, axis=1, keepdims=True))
    probs = e * (1.0 / jnp.sum(e, axis=1, keepdims=True))
    weights = probs.astype(BF)
    mixed = []
    for w in range(count):
        line = [
            fold(mm_tn(pg, vg), m)
            for pg, vg, m in zip(lanes_of(groups, weights[w]), parts_of(groups, v, w), masks32)
        ]
        mixed.append(jnp.concatenate(line, axis=1))
    return probs, jnp.concatenate(mixed, axis=0).astype(BF)


def attention_back(count, groups, q, k, v, probs, mixed_grad, masks16, masks32, between):
    grads = []
    many = []
    for w in range(count):
        many.append(
            [spread(mg, m) for mg, m in zip(parts_of(groups, mixed_grad, w), masks16)]
        )
        line = [mm_nt(vg, mg) for vg, mg in zip(parts_of(groups, v, w), many[w])]
        grads.append(jnp.concatenate(line, axis=1))
    wg = jnp.stack(grads).astype(BF).astype(F32)
    sg = (probs * (wg - jnp.sum(probs * wg, axis=1, keepdims=True)) * SCALE).astype(BF)
    weights = probs.astype(BF)
    out = [[], [], []]
    for w in range(count):
        between(w)
        scored, weighed = lanes_of(groups, sg[w]), lanes_of(groups, weights[w])
        qs, ks = parts_of(groups, q, w), parts_of(groups, k, w)
        dq = [fold(mm_tn(x, kg), m) for x, kg, m in zip(scored, ks, masks32)]
        dk = [mm(x, spread(qg, m)) for x, qg, m in zip(scored, qs, masks16)]
        dv = [mm(x, mg) for x, mg in zip(weighed, many[w])]
        for have, line in zip(out, (dq, dk, dv)):
            have.append(jnp.concatenate(line, axis=1))
    return [jnp.concatenate(x, axis=0).astype(BF) for x in out]


def folded_place(u):
    v = u & 15
    return (u - v) + (v & 1) * 8 + (v >> 1)


def true_place(p):
    v = p & 15
    return (p - v) + (v & 7) * 2 + (v >> 3)


def units(x):
    return x.reshape(x.shape[0] // 16, 16, 128)


class Net:
    def __init__(self, send, recv):
        self.r = lax.axis_index("rows")
        self.c = lax.axis_index("cols")
        r, c = self.r, self.c
        self.core = lax.rem(r, 2)
        xlo = lax.rem(r // 2, 2)
        self.y = r // 4
        self.z = c // 2
        xhi = lax.rem(c, 2)
        self.x = xhi * 2 + xlo
        self.low = lax.rem(r, 4)
        self.xhi = xhi
        self.send, self.recv = send, recv
        self.count = 0
        self.copies = []

    def near(self, dr, dc):
        return (lax.rem(self.r + dr + 16, 16), lax.rem(self.c + dc + 8, 8))

    def place(self, axis):
        return {"x": self.x, "y": self.y, "z": self.z}[axis]

    def peer(self, axis, index, core=None):
        core = self.core if core is None else core
        low = self.low - self.core + core
        if axis == "y":
            return (index * 4 + low, self.c)
        if axis == "z":
            return (self.y * 4 + low, index * 2 + self.xhi)
        return (self.y * 4 + lax.rem(index, 2) * 2 + core, self.z * 2 + index // 2)

    def sibling(self):
        return (self.r + 1 - 2 * self.core, self.c)

    def start(self, source, target, device):
        n = self.count
        self.count += 1
        copy = pltpu.make_async_remote_copy(
            src_ref=source,
            dst_ref=target,
            send_sem=self.send.at[n],
            recv_sem=self.recv.at[n],
            device_id=device,
            device_id_type=MESH,
        )
        copy.start()
        self.copies.append(copy)
        return copy

    def greet(self):
        sem = pltpu.get_barrier_semaphore()
        others = [self.near(a, b) for a in (-1, 0, 1) for b in (-1, 0, 1) if (a, b) != (0, 0)]
        others.append(self.sibling())
        for axis in "xyz":
            others += [self.peer(axis, lax.rem(self.place(axis) + k, 4)) for k in (1, 2, 3)]
            others += [
                self.peer(axis, lax.rem(self.place(axis) + k, 4), 1 - self.core)
                for k in (1, 2, 3)
            ]
        for device in others:
            pl.semaphore_signal(sem, inc=1, device_id=device, device_id_type=MESH)
        self.greeted = len(others)

    def gather(self):
        pl.semaphore_wait(pltpu.get_barrier_semaphore(), self.greeted)


class Reduce:
    def __init__(self, net, order, terms, got_core, got_a, sum_a, got_b, got_c, result):
        self.net, self.order = net, order
        self.terms, self.got_core, self.got_a, self.sum_a = terms, got_core, got_a, sum_a
        self.got_b, self.got_c, self.result = got_b, got_c, result
        self.half, self.part = terms.shape[0] // 2, terms.shape[0] // 8
        self.stage = 0
        self.flight = []

    def step(self):
        getattr(self, "step%d" % self.stage)()
        self.stage += 1

    def arrive(self):
        for copy in self.flight:
            copy.wait_recv()

    def to_peers(self, axis, source, target):
        net = self.net
        me = net.place(axis)
        self.flight = []
        for k in (1, 2, 3):
            to = lax.rem(me + k, 4)
            self.flight.append(net.start(source(to), target(k), net.peer(axis, to)))

    def spread_out(self, total, got, axis):
        me = self.net.place(axis)
        got[pl.ds(me, 1)] = total.astype(BF)[None]
        self.to_peers(axis, lambda to: got.at[me], lambda k: got.at[me])

    def summed(self, got):
        total = got[0].astype(F32)
        for k in (1, 2, 3):
            total = total + got[k].astype(F32)
        return total

    def step0(self):
        net, half = self.net, self.half
        self.flight = [
            net.start(self.terms.at[pl.ds((1 - net.core) * half, half)], self.got_core, net.sibling())
        ]

    def step1(self):
        net, half, part = self.net, self.half, self.part
        self.arrive()
        own = self.terms[pl.ds(net.core * half, half)].astype(F32)
        self.sum_a[...] = (own + self.got_core[...].astype(F32)).astype(BF)
        self.to_peers(
            self.order[0],
            lambda to: self.sum_a.at[pl.ds(to * part, part)],
            lambda k: self.got_a.at[k - 1],
        )

    def step2(self):
        self.arrive()
        me = self.net.place(self.order[0])
        total = self.sum_a[pl.ds(me * self.part, self.part)].astype(F32)
        for k in range(3):
            total = total + self.got_a[k].astype(F32)
        self.spread_out(total, self.got_b, self.order[1])

    def step3(self):
        self.arrive()
        self.spread_out(self.summed(self.got_b), self.got_c, self.order[2])

    def step4(self):
        self.arrive()
        at = self.net.core * self.half + self.net.place(self.order[0]) * self.part
        mine = self.result.at[pl.ds(at, self.part)]
        mine[...] = self.summed(self.got_c).astype(BF)
        self.to_peers(self.order[0], lambda to: mine, lambda k: mine)

    def step5(self):
        self.arrive()
        mine = self.result.at[pl.ds(self.net.core * self.half, self.half)]
        self.flight = [self.net.start(mine, mine, self.net.sibling())]

    def step6(self):
        self.arrive()


class Direct(Reduce):
    def __init__(self, net, order, terms, got_a, got_b, got_c, result):
        super().__init__(net, order, terms, None, got_a, None, got_b, got_c, result)
        self.at = (net.core * 4 + net.place(order[0])) * self.part

    def to_eight(self, source, target):
        net = self.net
        me = net.place(self.order[0])
        self.flight = []
        for k in range(1, 8):
            to, core = lax.rem(me + k, 4), lax.rem(net.core + k // 4, 2)
            self.flight.append(
                net.start(
                    source((core * 4 + to) * self.part),
                    target(k - 1),
                    net.peer(self.order[0], to, core),
                )
            )

    def step0(self):
        self.to_eight(lambda at: self.terms.at[pl.ds(at, self.part)], lambda k: self.got_a.at[k])

    def step1(self):
        self.arrive()
        total = self.terms[pl.ds(self.at, self.part)].astype(F32)
        for k in range(7):
            total = total + self.got_a[k].astype(F32)
        self.spread_out(total, self.got_b, self.order[1])

    def step2(self):
        self.step3()

    def step3(self):
        if self.stage == 2:
            Reduce.step3(self)
        else:
            self.arrive()
            mine = self.result.at[pl.ds(self.at, self.part)]
            mine[...] = self.summed(self.got_c).astype(BF)
            self.to_eight(lambda at: mine, lambda k: mine)

    def step4(self):
        self.arrive()
        self.stage = 6


def to_map(x, rows, cols):
    wide = cols // 8
    out = []
    for i in range(rows):
        base = (i // 8) * wide
        out.append(
            jnp.concatenate(
                [x[(base + w) * 64 + (i % 8) * 8 :][:8] for w in range(wide)], axis=0
            )
        )
    return out


def to_windows(rows_list, cols):
    wide = cols // 8
    pieces = []
    for wr in range(len(rows_list) // 8):
        for w in range(wide):
            for i in range(8):
                pieces.append(rows_list[wr * 8 + i][8 * w : 8 * w + 8])
    return jnp.concatenate(pieces, axis=0)


def paired(rows_list):
    out = []
    for di in (0, 1):
        for dj in (0, 1):
            out.append(
                jnp.concatenate(
                    [
                        rows_list[2 * i + di][16 * w + 8 * dj :][:8]
                        for w in (0, 1)
                        for i in range(8)
                    ],
                    axis=0,
                )
            )
    return out


def unpaired(parts):
    rows_list = []
    for row in range(16):
        i, di = row // 2, row % 2
        rows_list.append(
            jnp.concatenate(
                [
                    parts[2 * di + dj][64 * w + 8 * i :][:8]
                    for w in (0, 1)
                    for dj in (0, 1)
                ],
                axis=0,
            )
        )
    return rows_list


def packed(x):
    return x.reshape(128, x.shape[-1]).astype(BF).reshape(8, 16, x.shape[-1])


def pack_rows(x):
    tails = jnp.concatenate([x[:, :16, 128:], x[:, 16:, 128:]], axis=2)
    return jnp.concatenate([x[:, :, :128], tails], axis=1)


def open_rows(x):
    tails = jnp.concatenate([x[:, 32:, :64], x[:, 32:, 64:]], axis=1)
    return jnp.concatenate([x[:, :32], tails], axis=2)


def pack_tiles(x):
    m = x.shape[0] // 2
    x = x.reshape(m, 2, 16, 192)
    tails = jnp.concatenate([x[:, 0, :, 128:], x[:, 1, :, 128:]], axis=2)
    return jnp.stack([x[:, 0, :, :128], x[:, 1, :, :128], tails], axis=1).reshape(3 * m, 16, 128)


def open_tiles(x):
    m = x.shape[0] // 3
    x = x.reshape(m, 3, 16, 128)
    first = jnp.concatenate([x[:, 0], x[:, 2, :, :64]], axis=2)
    second = jnp.concatenate([x[:, 1], x[:, 2, :, 64:]], axis=2)
    return jnp.stack([first, second], axis=1).reshape(2 * m, 16, 192)


def one_hot(rows_out, cols_in, place):
    x = lax.broadcasted_iota(jnp.int32, (rows_out, cols_in), 0)
    u = lax.broadcasted_iota(jnp.int32, (rows_out, cols_in), 1)
    return jnp.where(place(x) == u, 1.0, 0.0).astype(BF)


def body(*refs):
    (
        offsets, actions, table, fgain, fqkv, fbias, fproj, mgain, mweight, cgain, cqkv, cbias,
        cproj, hweight,
    ) = refs[28:42]
    lat_hbm, cot_hbm = refs[14:16]
    pred_out, *result_outs = refs[16:28]
    (
        lat, lat_left, lat_right, cot, ahead, ahead_side, head, head_rows, back, back_side,
        lat_rows_out, lat_rows_in, lat_out, lat_left_in, lat_right_in, cot_rows_out, cot_rows_in,
        cot_next_out, cot_next_in, cot_prev_out, cot_prev_in, ahead_rows_out, ahead_rows_in,
        ahead_out, ahead_in, back_rows_out, back_rows_in, back_out, back_in, head_prev_out,
        head_prev_in, head_next_out, head_next_in, head_rows_out, head_rows_in, fprobs, cprobs,
    ) = refs[42:79]
    rest = refs[79:]
    works = [rest[6 * g : 6 * g + 6] for g in range(8)]
    works += [rest[48 + 4 * g : 52 + 4 * g] for g in range(3)]
    pred, *results = rest[60:72]
    send, recv, local = rest[72:]
    loads = [
        pltpu.make_async_copy(refs[i], refs[28 + i], local.at[2 + i]) for i in range(14)
    ]
    net = Net(send, recv)
    net.greet()
    bundles = [
        (Reduce if g < 8 else Direct)(net, ORDERS[g % 3], *works[g], results[g])
        for g in range(N_BUNDLES)
    ]

    def advance(*numbers):
        for g in numbers:
            bundles[g].step()
            if bundles[g].stage == 7:
                copy = pltpu.make_async_copy(results[g], result_outs[g], local.at[17 + g])
                copy.start()
                stores.append(copy)

    stores = []
    own_lat = pltpu.make_async_copy(lat_hbm.at[0], lat.at[pl.ds(8, 16)], local.at[0])
    own_cot = pltpu.make_async_copy(cot_hbm.at[0], cot.at[pl.ds(8, 16)], local.at[1])
    for copy in [own_lat] + loads[:6] + loads[6:] + [own_cot]:
        copy.start()

    own_lat.wait()
    low = lat[pl.ds(8, 16), pl.ds(0, 16)].astype(F32)
    high = lat[pl.ds(8, 16), pl.ds(16, 16)].astype(F32)
    lat_out[0] = pack_tiles(packed(low[:, :8]))
    lat_out[1] = pack_tiles(packed(high[:, 8:]))
    lat_rows_out[0] = pack_rows(lat[pl.ds(8, 8)])
    lat_rows_out[1] = pack_rows(lat[pl.ds(16, 8)])
    net.gather()
    lat_halo = []
    for side, dc, target in ((0, -1, lat_right_in), (1, 1, lat_left_in)):
        for dr, fr, nr, tr in ((0, 0, 12, 6), (-1, 0, 6, 18), (1, 6, 6, 0)):
            lat_halo.append(
                net.start(
                    lat_out.at[side, pl.ds(fr, nr)], target.at[pl.ds(tr, nr)], net.near(dr, dc)
                )
            )
    lat_halo.append(net.start(lat_rows_out.at[0], lat_rows_in.at[1], net.near(-1, 0)))
    lat_halo.append(net.start(lat_rows_out.at[1], lat_rows_in.at[0], net.near(1, 0)))

    own_cot.wait()
    cot_rows_out[...] = pack_rows(cot[pl.ds(8, 16)])
    cot_rows = [
        net.start(cot_rows_out, cot_rows_in.at[pl.ds(8, 16)], net.near(-1, 0)),
        net.start(cot_rows_out.at[pl.ds(8, 8)], cot_rows_in.at[pl.ds(0, 8)], net.near(1, 0)),
    ]

    for copy in loads:
        copy.wait()
    a0, a1 = offsets[0, 0], offsets[0, 1]
    b0, b1 = 2 * offsets[1, 0], 2 * offsets[1, 1]
    d0, d1 = lax.rem(b0 - a0 + 8, 8), lax.rem(b1 - a1 + 8, 8)
    s0, s1 = lax.rem(b0 - d0 + 8, 16) - 8, lax.rem(b1 - d1 + 8, 16) - 8
    t0, t1 = s0 + d0, s1 + d1
    code = lax.broadcasted_iota(jnp.int32, (8, 256), 1)
    counts = jnp.zeros((8, 256), F32)
    for j in range(16):
        counts = counts + jnp.where(code == actions[0, j], 1.0, 0.0)
    condition = mm_nt(counts.astype(BF), table[...])[:1] * (1.0 / 16.0)
    f_masks16 = [head_masks(w, h, BF) for _, w, h in FINE_GROUPS]
    f_masks32 = [head_masks(w, h, F32) for _, w, h in FINE_GROUPS]
    c_masks16 = [head_masks(w, h, BF) for _, w, h in COARSE_GROUPS]
    c_masks32 = [head_masks(w, h, F32) for _, w, h in COARSE_GROUPS]
    fb = fbias[...].reshape(384, 64).T
    cb = cbias[...].reshape(768, 64).T
    fw = [fqkv[:, 192 * i : 192 * i + 192] for i in range(3)]
    cw = [cqkv[:, 384 * i : 384 * i + 384] for i in range(3)]
    fproj_t, cproj_t, hweight_t = fproj[...].T, cproj[...].T, hweight[...].T
    cw_t, mweight_t = [w.T for w in cw], mweight[...].T
    f_gain = fgain[...].reshape(1, 192)
    m_gain = mgain[...].reshape(1, 768)
    c_gain = cgain[...].reshape(1, 384)

    def two_picks(rows_out, cols_in, parity, place):
        return [
            one_hot(rows_out, cols_in, lambda x, p=p: place(x, p))
            for p in (parity * 8, 8 - parity * 8)
        ]

    for copy in lat_halo:
        copy.wait_recv()
    lat_left[...] = open_tiles(lat_left_in[...])
    lat_right[...] = open_tiles(lat_right_in[...])
    lat[pl.ds(0, 8)] = open_rows(lat_rows_in[0])
    lat[pl.ds(24, 8)] = open_rows(lat_rows_in[1])

    def lat_place(x, p):
        u = x + (s1 + 8)
        return jnp.where(u < 8, 32 + p + u, jnp.where(u < 40, u - 8, 48 + p + u - 40))

    pick = two_picks(32, 64, (8 + s0) & 1, lat_place)
    block = lat[pl.ds(8 + s0, 16)]
    rows_list = []
    for i in range(16):
        pair = (8 + s0 + i) >> 1
        source = jnp.concatenate([block[i], lat_left[pair], lat_right[pair]], axis=0)
        rows_list.append(mm(pick[i % 2], source))
    residual = to_windows(rows_list, 32) + condition
    n1 = (norm(residual)[0] * f_gain).astype(BF)
    fq, fk, fv = (mm(n1, w).astype(BF) for w in fw)
    f_probs, f_mixed = attention(8, FINE_GROUPS, fq, fk, fv, fb, f_masks16, f_masks32)
    fprobs[...] = f_probs
    attn = mm(f_mixed, fproj[...]).astype(BF)
    f_next = residual + attn.astype(F32)
    for i, row in enumerate(to_map(f_next, 16, 32)):
        ahead[i] = row.astype(BF)
    edges = [f_next[256 * wr : 256 * wr + 64].astype(BF) for wr in range(2)]
    ahead_out[...] = pack_tiles(jnp.concatenate(edges, axis=0).reshape(8, 16, 192))
    ahead_rows_out[...] = pack_rows(ahead[pl.ds(0, 8)])
    ahead_halo = [
        net.start(ahead_out, ahead_in.at[pl.ds(0, 12)], net.near(0, -1)),
        net.start(ahead_out.at[pl.ds(0, 6)], ahead_in.at[pl.ds(12, 6)], net.near(-1, -1)),
        net.start(ahead_rows_out, ahead_rows_in, net.near(-1, 0)),
    ]

    for copy in cot_rows:
        copy.wait_recv()
    cot[pl.ds(0, 8)] = open_rows(cot_rows_in[pl.ds(0, 8)])
    cot[pl.ds(24, 16)] = open_rows(cot_rows_in[pl.ds(8, 16)])
    cot_main = cot[pl.ds(8 + t0, 16)]
    cot_next_out[...] = pack_tiles(cot_main[:, :16])
    cot_prev_out[...] = pack_tiles(packed(cot_main[:, 16:].astype(F32)[:, 8:]))
    cot_halo = [
        net.start(cot_next_out, cot_next_in, net.near(0, -1)),
        net.start(cot_prev_out, cot_prev_in, net.near(0, 1)),
    ]

    def ahead_place(x, p):
        u = true_place(x) + d1
        return jnp.where(u < 32, u, u + p)

    pick = two_picks(32, 48, d0 & 1, ahead_place)
    for copy in ahead_halo:
        copy.wait_recv()
    ahead_side[...] = open_tiles(ahead_in[...])
    ahead[pl.ds(16, 8)] = open_rows(ahead_rows_in[...])
    block = ahead[pl.ds(d0, 16)]
    rows_list = []
    for i in range(16):
        source = jnp.concatenate([block[i], ahead_side[(d0 + i) >> 1]], axis=0)
        rows_list.append(mm(pick[i % 2], source))
    merged = jnp.concatenate(paired(rows_list), axis=1)
    m_unit, m_inverse = norm(merged)
    n2 = (m_unit * m_gain).astype(BF)
    c_residual = mm(n2, mweight[...]).astype(BF).astype(F32)
    c_unit, c_inverse = norm(c_residual)
    n3 = (c_unit * c_gain).astype(BF)
    cq, ck, cv = (mm(n3, w).astype(BF) for w in cw)
    c_probs, c_mixed = attention(2, COARSE_GROUPS, cq, ck, cv, cb, c_masks16, c_masks32)
    cprobs[...] = c_probs
    c_attn = mm(c_mixed, cproj[...]).astype(BF)
    c_next = (c_residual + c_attn.astype(F32)).astype(BF)

    head_out = mm(c_next, hweight[...])
    for i, row in enumerate(unpaired([head_out[:, 192 * t : 192 * t + 192] for t in range(4)])):
        head[i] = row.astype(BF)
    first = one_hot(16, 64, lambda x: (x >> 3) * 32 + folded_place(x & 7))
    edges = []
    for i in range(8):
        both = jnp.concatenate([head[2 * i], head[2 * i + 1]], axis=0)
        edges.append(mm(first, both).astype(BF))
    head_next_out[...] = pack_tiles(jnp.stack(edges))
    head_prev_out[...] = pack_tiles(head[:, pl.ds(16, 16)])
    head_halo = [
        net.start(head_prev_out, head_prev_in, net.near(0, 1)),
        net.start(head_next_out, head_next_in, net.near(0, -1)),
    ]

    for copy in cot_halo:
        copy.wait_recv()

    def cot_place(x, p):
        u = true_place(x) + (t1 + 8)
        return jnp.where(u < 8, 48 + p + u, u - 8)

    pick = two_picks(32, 64, 0, cot_place)
    cot_next, cot_prev = open_tiles(cot_next_in[...]), open_tiles(cot_prev_in[...])
    rows_list = []
    for i in range(16):
        source = jnp.concatenate([cot_main[i], cot_next[i], cot_prev[i // 2]], axis=0)
        rows_list.append(mm(pick[i % 2], source))
    grad_out = jnp.concatenate(paired(rows_list), axis=1).astype(BF)
    grad_next = mm(grad_out, hweight_t).astype(BF)
    c_mixed_grad = mm(grad_next, cproj_t).astype(BF)

    g_head = mm_tn(c_next, grad_out)
    for j in range(6):
        works[j // 3][0][pl.ds(24 * (j % 3), 24)] = units(
            g_head[:, 128 * j : 128 * j + 128].astype(BF)
        )
    g_cproj = mm_tn(c_mixed, grad_next)
    for j in range(3):
        works[2][0][pl.ds(24 * j, 24)] = units(g_cproj[:, 128 * j : 128 * j + 128].astype(BF))
    advance(0, 1, 2)

    c_packed = attention_back(
        2, COARSE_GROUPS, cq, ck, cv, cprobs[...], c_mixed_grad, c_masks16, c_masks32,
        lambda w: None,
    )
    rolled = mm(c_packed[0], cw_t[0]) + mm(c_packed[1], cw_t[1]) + mm(c_packed[2], cw_t[2])
    grad_residual = (
        grad_next.astype(F32)
        + norm_back(rolled.astype(BF).astype(F32), c_unit, c_inverse, c_gain)
    ).astype(BF)
    norm_grad = mm(grad_residual, mweight_t).astype(BF).astype(F32)
    merged_grad = norm_back(norm_grad, m_unit, m_inverse, m_gain)
    rows_list = [
        row.astype(BF)
        for row in unpaired([merged_grad[:, 192 * t : 192 * t + 192] for t in range(4)])
    ]
    last = one_hot(16, 64, lambda x: (x >> 3) * 32 + folded_place(24 + (x & 7)))
    edges = []
    for i in range(8):
        both = jnp.concatenate(rows_list[2 * i : 2 * i + 2], axis=0)
        back[8 + 2 * i], back[9 + 2 * i] = rows_list[2 * i], rows_list[2 * i + 1]
        edges.append(mm(last, both).astype(BF))
    back_out[...] = pack_tiles(jnp.stack(edges))
    back_rows_out[...] = pack_rows(jnp.stack(rows_list[8:]))
    back_halo = [
        net.start(back_out, back_in.at[pl.ds(6, 12)], net.near(0, 1)),
        net.start(back_out.at[pl.ds(6, 6)], back_in.at[pl.ds(0, 6)], net.near(1, 1)),
        net.start(back_rows_out, back_rows_in, net.near(1, 0)),
    ]
    advance(0, 1, 2)
    for t in range(3):
        g_part = mm_tn(n3, c_packed[t])
        for j in range(3):
            works[3 + t][0][pl.ds(24 * j, 24)] = units(
                g_part[:, 128 * j : 128 * j + 128].astype(BF)
            )
    advance(3, 4, 5)
    g_merge = mm_tn(n2, grad_residual)
    for t in range(2):
        for j in range(3):
            works[6 + t][0][pl.ds(24 * j, 24)] = units(
                g_merge[384 * t : 384 * t + 384, 128 * j : 128 * j + 128].astype(BF)
            )
    advance(6, 7)
    advance(3, 4, 5)
    def turn_rows():
        for copy in head_halo:
            copy.wait_recv()
        pick = two_picks(32, 64, 0, head_place)
        head_prev, head_next = open_tiles(head_prev_in[...]), open_tiles(head_next_in[...])
        for i in range(16):
            source = jnp.concatenate([head[i], head_prev[i], head_next[i // 2]], axis=0)
            head_rows[16 + i] = mm(pick[i % 2], source).astype(BF)
        head_rows_out[...] = pack_rows(head_rows[pl.ds(16, 16)])
        return [
            net.start(head_rows_out, head_rows_in.at[pl.ds(0, 16)], net.near(1, 0)),
            net.start(head_rows_out.at[pl.ds(0, 8)], head_rows_in.at[pl.ds(16, 8)], net.near(-1, 0)),
        ]

    def head_place(x, p):
        u = x + (16 - t1)
        return jnp.where(
            u < 16, 32 + folded_place(u), jnp.where(u < 48, folded_place(u - 16), u + p)
        )

    rows_halo = turn_rows()

    def back_place(x, p):
        u = x + (8 - d1)
        return jnp.where(u < 8, 32 + p + u, folded_place(u - 8))

    pick = two_picks(32, 48, d0 & 1, back_place)
    for copy in back_halo:
        copy.wait_recv()
    advance(6, 7)

    back_side[...] = open_tiles(back_in[...])
    back[pl.ds(0, 8)] = open_rows(back_rows_in[...])
    block = back[pl.ds(8 - d0, 16)]
    rows_list = []
    for i in range(16):
        source = jnp.concatenate([block[i], back_side[(8 - d0 + i) >> 1]], axis=0)
        rows_list.append(mm(pick[i % 2], source))
    f_grad = to_windows(rows_list, 32).astype(BF)
    f_mixed_grad = mm(f_grad, fproj_t).astype(BF)
    g_fproj = mm_tn(f_mixed, f_grad)

    def between(w):
        if w == 2:
            advance(0, 1, 2)
        if w == 7:
            advance(3, 4, 5, 6, 7)

    f_packed = attention_back(
        8, FINE_GROUPS, fq, fk, fv, fprobs[...], f_mixed_grad, f_masks16, f_masks32, between
    )
    g_parts = [mm_tn(n1, x) for x in f_packed]
    g_parts.append(g_fproj)
    for t in range(4):
        works[8 + t // 2][0][pl.ds(12 * (t % 2), 12)] = units(g_parts[t][:, :128].astype(BF))
    for t in (0, 2):
        tails = jnp.concatenate([g_parts[t][:, 128:], g_parts[t + 1][:, 128:]], axis=1)
        works[10][0][pl.ds(6 * t, 12)] = units(tails.astype(BF))
    advance(8, 9, 10)
    advance(3, 4, 5, 6, 7)
    advance(0, 1, 2)
    advance(8, 9, 10)
    advance(3, 4, 5, 6, 7)
    for copy in rows_halo:
        copy.wait_recv()
    head_rows[pl.ds(0, 16)] = open_rows(head_rows_in[pl.ds(0, 16)])
    head_rows[pl.ds(32, 8)] = open_rows(head_rows_in[pl.ds(16, 8)])
    pred[...] = head_rows[pl.ds(16 - t0, 16)]
    stores.append(pltpu.make_async_copy(pred, pred_out, local.at[16]))
    stores[-1].start()
    advance(8, 9, 10)
    advance(0, 1, 2)
    advance(3, 4, 5, 6, 7)
    advance(8, 9, 10)
    advance(0, 1, 2)
    advance(3, 4, 5, 6, 7)
    advance(8, 9, 10)
    advance(0, 1, 2)
    for copy in stores:
        copy.wait()
    for copy in net.copies:
        copy.wait_send()


N_COPIES = 8 + 4 + 3 + 3 + 4 + 14 * 8 + 20 * 3


def unpack(*refs):
    pred_in, *heres = refs[:12]
    pred_out, *outs = refs[12:19]
    packs, wides, held, sems = refs[19:30], refs[30:36], refs[36], refs[37]
    fq, fp, me, cq, cp, he = wides
    pass_in = pltpu.make_async_copy(pred_in, held, sems.at[17])
    pass_on = pltpu.make_async_copy(held, pred_out.at[0], sems.at[18])
    loads = [pltpu.make_async_copy(heres[g], packs[g], sems.at[g]) for g in range(11)]
    stores = [pltpu.make_async_copy(wides[i], outs[i], sems.at[11 + i]) for i in range(6)]
    for copy in loads + [pass_in]:
        copy.start()

    def take(g, at, count):
        return packs[g][pl.ds(at, count)].reshape(count * 16, 128).astype(F32)

    for t in range(2):
        loads[t].wait()
        for j in range(3):
            he[:, pl.ds(384 * t + 128 * j, 128)] = take(t, 24 * j, 24)
    stores[5].start()
    loads[2].wait()
    for j in range(3):
        cp[:, pl.ds(128 * j, 128)] = take(2, 24 * j, 24)
    stores[4].start()
    for t in range(3):
        loads[3 + t].wait()
        for j in range(3):
            cq[:, pl.ds(384 * t + 128 * j, 128)] = take(3 + t, 24 * j, 24)
    stores[3].start()
    for t in range(2):
        loads[6 + t].wait()
        for j in range(3):
            me[pl.ds(384 * t, 384), pl.ds(128 * j, 128)] = take(6 + t, 24 * j, 24)
    stores[2].start()
    pass_in.wait()
    pass_on.start()
    for g in (8, 9, 10):
        loads[g].wait()
    parts = [take(8 + t // 2, 12 * (t % 2), 12) for t in range(4)]
    tails = [take(10, 12 * t, 12) for t in range(2)]
    fq[...] = jnp.concatenate(
        [parts[0], tails[0][:, :64], parts[1], tails[0][:, 64:], parts[2], tails[1][:, :64]], axis=1
    )
    fp[...] = jnp.concatenate([parts[3], tails[1][:, 64:]], axis=1)
    stores[0].start()
    stores[1].start()
    for copy in stores + [pass_on]:
        copy.wait()


def on_device(
    latents, actions, action_table, offsets, fine_gain, fine_qkv, fine_bias, fine_proj, merge_gain,
    merge_weight, coarse_gain, coarse_qkv, coarse_bias, coarse_proj, head_weight, cotangent,
):
    hbm = pl.BlockSpec(memory_space=pltpu.HBM)
    held = (
        offsets, actions, action_table.T, fine_gain, fine_qkv, fine_bias, fine_proj, merge_gain,
        merge_weight, coarse_gain, coarse_qkv, coarse_bias, coarse_proj, head_weight,
    )
    scratch = [pltpu.SMEM(x.shape, x.dtype) for x in held[:2]]
    scratch += [pltpu.VMEM(x.shape, x.dtype) for x in held[2:]]
    scratch += [
        pltpu.VMEM(shape + (192,), BF)
        for shape in (
            (32, 32), (16, 16), (16, 16), (40, 32), (24, 32), (12, 16), (16, 32), (40, 32), (24, 32),
            (12, 16),
        )
    ]
    scratch += [
        pltpu.VMEM(shape + (128,), BF)
        for shape in (
            (2, 8, 48), (2, 8, 48), (2, 12, 16), (24, 16), (24, 16), (16, 48), (24, 48), (24, 16),
            (24, 16), (12, 16), (12, 16), (8, 48), (8, 48), (12, 16), (18, 16), (8, 48), (8, 48),
            (12, 16), (18, 16), (24, 16), (24, 16), (12, 16), (12, 16), (16, 48), (24, 48),
        )
    ]
    scratch += [
        pltpu.VMEM((8, 64, 384), F32),
        pltpu.VMEM((2, 64, 768), F32),
    ]
    wide = ((72,), (36,), (3, 9), (36,), (4, 9), (4, 9))
    narrow = ((24,), (7, 3), (4, 3), (4, 3))
    for shape in wide * 8 + narrow * 3:
        scratch.append(pltpu.VMEM(shape + (16, 128), BF))
    scratch.append(pltpu.VMEM((16, 32, 192), BF))
    scratch += [pltpu.VMEM((n, 16, 128), BF) for n in UNITS]
    scratch += [
        pltpu.SemaphoreType.DMA((N_COPIES,)),
        pltpu.SemaphoreType.DMA((N_COPIES,)),
        pltpu.SemaphoreType.DMA((28,)),
    ]
    pred, *results = pl.pallas_call(
        body,
        out_shape=[jax.ShapeDtypeStruct((16, 32, 192), BF)]
        + [jax.ShapeDtypeStruct((n, 16, 128), BF) for n in UNITS],
        in_specs=[hbm] * 16,
        out_specs=[hbm] * 12,
        scratch_shapes=scratch,
        compiler_params=pltpu.CompilerParams(
            collective_id=0, has_side_effects=True, vmem_limit_bytes=60 * 1024 * 1024
        ),
        name="block_pair",
    )(*held, latents, cotangent)
    shapes = ((192, 576), (192, 192), (768, 384), (384, 1152), (384, 384), (384, 768))
    return tuple(
        pl.pallas_call(
            unpack,
            out_shape=[jax.ShapeDtypeStruct((1, 16, 32, 192), BF)]
            + [jax.ShapeDtypeStruct(s, F32) for s in shapes],
            in_specs=[hbm] * 12,
            out_specs=[hbm] * 7,
            scratch_shapes=[pltpu.VMEM((n, 16, 128), BF) for n in UNITS]
            + [pltpu.VMEM(s, F32) for s in shapes]
            + [pltpu.VMEM((16, 32, 192), BF), pltpu.SemaphoreType.DMA((19,))],
            compiler_params=pltpu.CompilerParams(vmem_limit_bytes=60 * 1024 * 1024),
            name="unpack",
        )(pred, *results)
    )


def solution(mesh):
    split = P(None, "rows", "cols", None)
    return jax.shard_map(
        on_device,
        mesh=mesh,
        in_specs=(split,) + (P(),) * 14 + (split,),
        out_specs=(split,) + (P(),) * 6,
        check_vma=False,
    )
```

```python
import jax
import jax.numpy as jnp
from jax import lax
from jax.experimental import pallas as pl
from jax.experimental.pallas import tpu as pltpu
from jax.sharding import PartitionSpec as P

MESH = pl.DeviceIdType.MESH
BF = jnp.bfloat16
F32 = jnp.float32
EPS = 1e-05
SCALE = 32 ** (-0.5)
FINE_GROUPS = ((0, 128, 4), (128, 64, 2))
COARSE_GROUPS = ((0, 128, 4), (128, 128, 4), (256, 128, 4))
UNITS = (72,) * 8 + (24,) * 3
N_BUNDLES = len(UNITS)
ORDERS = (("y", "z", "x"), ("z", "x", "y"), ("x", "y", "z"))


def mm(a, b):
    return lax.dot_general(a, b, (((1,), (0,)), ((), ())), preferred_element_type=F32)


def mm_nt(a, b):
    return lax.dot_general(a, b, (((1,), (1,)), ((), ())), preferred_element_type=F32)


def mm_tn(a, b):
    return lax.dot_general(a, b, (((0,), (0,)), ((), ())), preferred_element_type=F32)


def norm(x):
    centred = x - jnp.mean(x, axis=-1, keepdims=True)
    inverse = lax.rsqrt(jnp.mean(centred * centred, axis=-1, keepdims=True) + EPS)
    return centred * inverse, inverse


def norm_back(upstream, unit, inverse, gain):
    e = upstream * gain
    return inverse * (
        e - jnp.mean(e, axis=-1, keepdims=True) - unit * jnp.mean(e * unit, axis=-1, keepdims=True)
    )


def head_masks(width, heads, dtype):
    lane = lax.broadcasted_iota(jnp.int32, (1, width), 1) // 32
    return [jnp.where(lane == h, 1.0, 0.0).astype(dtype) for h in range(heads)]


def spread(x, masks):
    return jnp.concatenate([x * m for m in masks], axis=0)


def fold(x, masks):
    total = x[:64] * masks[0]
    for h in range(1, len(masks)):
        total = total + x[64 * h : 64 * h + 64] * masks[h]
    return total


def parts_of(groups, x, w):
    return [x[64 * w : 64 * w + 64, at : at + wide] for at, wide, _ in groups]


def lanes_of(groups, x):
    return [x[:, 2 * at : 2 * at + 64 * heads] for at, _, heads in groups]


def attention(count, groups, q, k, v, bias, masks16, masks32):
    scores = []
    for w in range(count):
        line = [
            mm_nt(kg, spread(qg, m))
            for qg, kg, m in zip(parts_of(groups, q, w), parts_of(groups, k, w), masks16)
        ]
        scores.append(jnp.concatenate(line, axis=1))
    s = jnp.stack(scores) * SCALE + bias[None]
    e = jnp.exp(s - jnp.max(s, axis=1, keepdims=True))
    probs = e * (1.0 / jnp.sum(e, axis=1, keepdims=True))
    weights = probs.astype(BF)
    mixed = []
    for w in range(count):
        line = [
            fold(mm_tn(pg, vg), m)
            for pg, vg, m in zip(lanes_of(groups, weights[w]), parts_of(groups, v, w), masks32)
        ]
        mixed.append(jnp.concatenate(line, axis=1))
    return probs, jnp.concatenate(mixed, axis=0).astype(BF)


def attention_back(count, groups, q, k, v, probs, mixed_grad, masks16, masks32, between):
    grads = []
    many = []
    for w in range(count):
        many.append(
            [spread(mg, m) for mg, m in zip(parts_of(groups, mixed_grad, w), masks16)]
        )
        line = [mm_nt(vg, mg) for vg, mg in zip(parts_of(groups, v, w), many[w])]
        grads.append(jnp.concatenate(line, axis=1))
    wg = jnp.stack(grads).astype(BF).astype(F32)
    sg = (probs * (wg - jnp.sum(probs * wg, axis=1, keepdims=True)) * SCALE).astype(BF)
    weights = probs.astype(BF)
    out = [[], [], []]
    for w in range(count):
        between(w)
        scored, weighed = lanes_of(groups, sg[w]), lanes_of(groups, weights[w])
        qs, ks = parts_of(groups, q, w), parts_of(groups, k, w)
        dq = [fold(mm_tn(x, kg), m) for x, kg, m in zip(scored, ks, masks32)]
        dk = [mm(x, spread(qg, m)) for x, qg, m in zip(scored, qs, masks16)]
        dv = [mm(x, mg) for x, mg in zip(weighed, many[w])]
        for have, line in zip(out, (dq, dk, dv)):
            have.append(jnp.concatenate(line, axis=1))
    return [jnp.concatenate(x, axis=0).astype(BF) for x in out]


def folded_place(u):
    v = u & 15
    return (u - v) + (v & 1) * 8 + (v >> 1)


def true_place(p):
    v = p & 15
    return (p - v) + (v & 7) * 2 + (v >> 3)


def units(x):
    return x.reshape(x.shape[0] // 16, 16, 128)


class Net:
    def __init__(self, send, recv):
        self.r = lax.axis_index("rows")
        self.c = lax.axis_index("cols")
        r, c = self.r, self.c
        self.core = lax.rem(r, 2)
        xlo = lax.rem(r // 2, 2)
        self.y = r // 4
        self.z = c // 2
        xhi = lax.rem(c, 2)
        self.x = xhi * 2 + xlo
        self.low = lax.rem(r, 4)
        self.xhi = xhi
        self.send, self.recv = send, recv
        self.count = 0
        self.copies = []

    def near(self, dr, dc):
        return (lax.rem(self.r + dr + 16, 16), lax.rem(self.c + dc + 8, 8))

    def place(self, axis):
        return {"x": self.x, "y": self.y, "z": self.z}[axis]

    def peer(self, axis, index, core=None):
        core = self.core if core is None else core
        low = self.low - self.core + core
        if axis == "y":
            return (index * 4 + low, self.c)
        if axis == "z":
            return (self.y * 4 + low, index * 2 + self.xhi)
        return (self.y * 4 + lax.rem(index, 2) * 2 + core, self.z * 2 + index // 2)

    def sibling(self):
        return (self.r + 1 - 2 * self.core, self.c)

    def start(self, source, target, device):
        n = self.count
        self.count += 1
        copy = pltpu.make_async_remote_copy(
            src_ref=source,
            dst_ref=target,
            send_sem=self.send.at[n],
            recv_sem=self.recv.at[n],
            device_id=device,
            device_id_type=MESH,
        )
        copy.start()
        self.copies.append(copy)
        return copy

    def greet(self):
        sem = pltpu.get_barrier_semaphore()
        others = [self.near(a, b) for a in (-1, 0, 1) for b in (-1, 0, 1) if (a, b) != (0, 0)]
        others.append(self.sibling())
        for axis in "xyz":
            others += [self.peer(axis, lax.rem(self.place(axis) + k, 4)) for k in (1, 2, 3)]
            others += [
                self.peer(axis, lax.rem(self.place(axis) + k, 4), 1 - self.core)
                for k in (1, 2, 3)
            ]
        for device in others:
            pl.semaphore_signal(sem, inc=1, device_id=device, device_id_type=MESH)
        self.greeted = len(others)

    def gather(self):
        pl.semaphore_wait(pltpu.get_barrier_semaphore(), self.greeted)


class Reduce:
    def __init__(self, net, order, terms, got_core, got_a, sum_a, got_b, got_c, result):
        self.net, self.order = net, order
        self.terms, self.got_core, self.got_a, self.sum_a = terms, got_core, got_a, sum_a
        self.got_b, self.got_c, self.result = got_b, got_c, result
        self.half, self.part = terms.shape[0] // 2, terms.shape[0] // 8
        self.stage = 0
        self.flight = []

    def step(self):
        getattr(self, "step%d" % self.stage)()
        self.stage += 1

    def arrive(self):
        for copy in self.flight:
            copy.wait_recv()

    def to_peers(self, axis, source, target):
        net = self.net
        me = net.place(axis)
        self.flight = []
        for k in (1, 2, 3):
            to = lax.rem(me + k, 4)
            self.flight.append(net.start(source(to), target(k), net.peer(axis, to)))

    def spread_out(self, total, got, axis):
        me = self.net.place(axis)
        got[pl.ds(me, 1)] = total.astype(BF)[None]
        self.to_peers(axis, lambda to: got.at[me], lambda k: got.at[me])

    def summed(self, got):
        total = got[0].astype(F32)
        for k in (1, 2, 3):
            total = total + got[k].astype(F32)
        return total

    def step0(self):
        net, half = self.net, self.half
        self.flight = [
            net.start(self.terms.at[pl.ds((1 - net.core) * half, half)], self.got_core, net.sibling())
        ]

    def step1(self):
        net, half, part = self.net, self.half, self.part
        self.arrive()
        own = self.terms[pl.ds(net.core * half, half)].astype(F32)
        self.sum_a[...] = (own + self.got_core[...].astype(F32)).astype(BF)
        self.to_peers(
            self.order[0],
            lambda to: self.sum_a.at[pl.ds(to * part, part)],
            lambda k: self.got_a.at[k - 1],
        )

    def step2(self):
        self.arrive()
        me = self.net.place(self.order[0])
        total = self.sum_a[pl.ds(me * self.part, self.part)].astype(F32)
        for k in range(3):
            total = total + self.got_a[k].astype(F32)
        self.spread_out(total, self.got_b, self.order[1])

    def step3(self):
        self.arrive()
        self.spread_out(self.summed(self.got_b), self.got_c, self.order[2])

    def step4(self):
        self.arrive()
        at = self.net.core * self.half + self.net.place(self.order[0]) * self.part
        mine = self.result.at[pl.ds(at, self.part)]
        mine[...] = self.summed(self.got_c).astype(BF)
        self.to_peers(self.order[0], lambda to: mine, lambda k: mine)

    def step5(self):
        self.arrive()
        mine = self.result.at[pl.ds(self.net.core * self.half, self.half)]
        self.flight = [self.net.start(mine, mine, self.net.sibling())]

    def step6(self):
        self.arrive()


class Direct(Reduce):
    def __init__(self, net, order, terms, got_a, got_b, got_c, result):
        super().__init__(net, order, terms, None, got_a, None, got_b, got_c, result)
        self.at = (net.core * 4 + net.place(order[0])) * self.part

    def to_eight(self, source, target):
        net = self.net
        me = net.place(self.order[0])
        self.flight = []
        for k in range(1, 8):
            to, core = lax.rem(me + k, 4), lax.rem(net.core + k // 4, 2)
            self.flight.append(
                net.start(
                    source((core * 4 + to) * self.part),
                    target(k - 1),
                    net.peer(self.order[0], to, core),
                )
            )

    def step0(self):
        self.to_eight(lambda at: self.terms.at[pl.ds(at, self.part)], lambda k: self.got_a.at[k])

    def step1(self):
        self.arrive()
        total = self.terms[pl.ds(self.at, self.part)].astype(F32)
        for k in range(7):
            total = total + self.got_a[k].astype(F32)
        self.spread_out(total, self.got_b, self.order[1])

    def step2(self):
        self.step3()

    def step3(self):
        if self.stage == 2:
            Reduce.step3(self)
        else:
            self.arrive()
            mine = self.result.at[pl.ds(self.at, self.part)]
            mine[...] = self.summed(self.got_c).astype(BF)
            self.to_eight(lambda at: mine, lambda k: mine)

    def step4(self):
        self.arrive()
        self.stage = 6


def to_map(x, rows, cols):
    wide = cols // 8
    out = []
    for i in range(rows):
        base = (i // 8) * wide
        out.append(
            jnp.concatenate(
                [x[(base + w) * 64 + (i % 8) * 8 :][:8] for w in range(wide)], axis=0
            )
        )
    return out


def to_windows(rows_list, cols):
    wide = cols // 8
    pieces = []
    for wr in range(len(rows_list) // 8):
        for w in range(wide):
            for i in range(8):
                pieces.append(rows_list[wr * 8 + i][8 * w : 8 * w + 8])
    return jnp.concatenate(pieces, axis=0)


def paired(rows_list):
    out = []
    for di in (0, 1):
        for dj in (0, 1):
            out.append(
                jnp.concatenate(
                    [
                        rows_list[2 * i + di][16 * w + 8 * dj :][:8]
                        for w in (0, 1)
                        for i in range(8)
                    ],
                    axis=0,
                )
            )
    return out


def unpaired(parts):
    rows_list = []
    for row in range(16):
        i, di = row // 2, row % 2
        rows_list.append(
            jnp.concatenate(
                [
                    parts[2 * di + dj][64 * w + 8 * i :][:8]
                    for w in (0, 1)
                    for dj in (0, 1)
                ],
                axis=0,
            )
        )
    return rows_list


def packed(x):
    return x.reshape(128, x.shape[-1]).astype(BF).reshape(8, 16, x.shape[-1])


def pack_rows(x):
    tails = jnp.concatenate([x[:, :16, 128:], x[:, 16:, 128:]], axis=2)
    return jnp.concatenate([x[:, :, :128], tails], axis=1)


def open_rows(x):
    tails = jnp.concatenate([x[:, 32:, :64], x[:, 32:, 64:]], axis=1)
    return jnp.concatenate([x[:, :32], tails], axis=2)


def pack_tiles(x):
    m = x.shape[0] // 2
    x = x.reshape(m, 2, 16, 192)
    tails = jnp.concatenate([x[:, 0, :, 128:], x[:, 1, :, 128:]], axis=2)
    return jnp.stack([x[:, 0, :, :128], x[:, 1, :, :128], tails], axis=1).reshape(3 * m, 16, 128)


def open_tiles(x):
    m = x.shape[0] // 3
    x = x.reshape(m, 3, 16, 128)
    first = jnp.concatenate([x[:, 0], x[:, 2, :, :64]], axis=2)
    second = jnp.concatenate([x[:, 1], x[:, 2, :, 64:]], axis=2)
    return jnp.stack([first, second], axis=1).reshape(2 * m, 16, 192)


def one_hot(rows_out, cols_in, place):
    x = lax.broadcasted_iota(jnp.int32, (rows_out, cols_in), 0)
    u = lax.broadcasted_iota(jnp.int32, (rows_out, cols_in), 1)
    return jnp.where(place(x) == u, 1.0, 0.0).astype(BF)


def body(*refs):
    (
        offsets, actions, table, fgain, fqkv, fbias, fproj, mgain, mweight, cgain, cqkv, cbias,
        cproj, hweight,
    ) = refs[28:42]
    lat_hbm, cot_hbm = refs[14:16]
    pred_out, *result_outs = refs[16:28]
    (
        lat, lat_left, lat_right, cot, ahead, ahead_side, head, head_rows, back, back_side,
        lat_rows_out, lat_rows_in, lat_out, lat_left_in, lat_right_in, cot_rows_out, cot_rows_in,
        cot_next_out, cot_next_in, cot_prev_out, cot_prev_in, ahead_rows_out, ahead_rows_in,
        ahead_out, ahead_in, back_rows_out, back_rows_in, back_out, back_in, head_prev_out,
        head_prev_in, head_next_out, head_next_in, head_rows_out, head_rows_in, fprobs, cprobs,
    ) = refs[42:79]
    rest = refs[79:]
    works = [rest[6 * g : 6 * g + 6] for g in range(8)]
    works += [rest[48 + 4 * g : 52 + 4 * g] for g in range(3)]
    pred, *results = rest[60:72]
    send, recv, local = rest[72:]
    loads = [
        pltpu.make_async_copy(refs[i], refs[28 + i], local.at[2 + i]) for i in range(14)
    ]
    net = Net(send, recv)
    net.greet()
    bundles = [
        (Reduce if g < 8 else Direct)(net, ORDERS[g % 3], *works[g], results[g])
        for g in range(N_BUNDLES)
    ]

    def advance(*numbers):
        for g in numbers:
            bundles[g].step()
            if bundles[g].stage == 7:
                copy = pltpu.make_async_copy(results[g], result_outs[g], local.at[17 + g])
                copy.start()
                stores.append(copy)

    stores = []
    own_lat = pltpu.make_async_copy(lat_hbm.at[0], lat.at[pl.ds(8, 16)], local.at[0])
    own_cot = pltpu.make_async_copy(cot_hbm.at[0], cot.at[pl.ds(8, 16)], local.at[1])
    for copy in [own_lat] + loads[:6] + loads[6:] + [own_cot]:
        copy.start()

    own_lat.wait()
    low = lat[pl.ds(8, 16), pl.ds(0, 16)].astype(F32)
    high = lat[pl.ds(8, 16), pl.ds(16, 16)].astype(F32)
    lat_out[0] = pack_tiles(packed(low[:, :8]))
    lat_out[1] = pack_tiles(packed(high[:, 8:]))
    lat_rows_out[0] = pack_rows(lat[pl.ds(8, 8)])
    lat_rows_out[1] = pack_rows(lat[pl.ds(16, 8)])
    net.gather()
    lat_halo = []
    for side, dc, target in ((0, -1, lat_right_in), (1, 1, lat_left_in)):
        for dr, fr, nr, tr in ((0, 0, 12, 6), (-1, 0, 6, 18), (1, 6, 6, 0)):
            lat_halo.append(
                net.start(
                    lat_out.at[side, pl.ds(fr, nr)], target.at[pl.ds(tr, nr)], net.near(dr, dc)
                )
            )
    lat_halo.append(net.start(lat_rows_out.at[0], lat_rows_in.at[1], net.near(-1, 0)))
    lat_halo.append(net.start(lat_rows_out.at[1], lat_rows_in.at[0], net.near(1, 0)))

    own_cot.wait()
    cot_rows_out[...] = pack_rows(cot[pl.ds(8, 16)])
    cot_rows = [
        net.start(cot_rows_out, cot_rows_in.at[pl.ds(8, 16)], net.near(-1, 0)),
        net.start(cot_rows_out.at[pl.ds(8, 8)], cot_rows_in.at[pl.ds(0, 8)], net.near(1, 0)),
    ]

    for copy in loads:
        copy.wait()
    a0, a1 = offsets[0, 0], offsets[0, 1]
    b0, b1 = 2 * offsets[1, 0], 2 * offsets[1, 1]
    d0, d1 = lax.rem(b0 - a0 + 8, 8), lax.rem(b1 - a1 + 8, 8)
    s0, s1 = lax.rem(b0 - d0 + 8, 16) - 8, lax.rem(b1 - d1 + 8, 16) - 8
    t0, t1 = s0 + d0, s1 + d1
    code = lax.broadcasted_iota(jnp.int32, (8, 256), 1)
    counts = jnp.zeros((8, 256), F32)
    for j in range(16):
        counts = counts + jnp.where(code == actions[0, j], 1.0, 0.0)
    condition = mm_nt(counts.astype(BF), table[...])[:1] * (1.0 / 16.0)
    f_masks16 = [head_masks(w, h, BF) for _, w, h in FINE_GROUPS]
    f_masks32 = [head_masks(w, h, F32) for _, w, h in FINE_GROUPS]
    c_masks16 = [head_masks(w, h, BF) for _, w, h in COARSE_GROUPS]
    c_masks32 = [head_masks(w, h, F32) for _, w, h in COARSE_GROUPS]
    fb = fbias[...].reshape(384, 64).T
    cb = cbias[...].reshape(768, 64).T
    fw = [fqkv[:, 192 * i : 192 * i + 192] for i in range(3)]
    cw = [cqkv[:, 384 * i : 384 * i + 384] for i in range(3)]
    fproj_t, cproj_t, hweight_t = fproj[...].T, cproj[...].T, hweight[...].T
    cw_t, mweight_t = [w.T for w in cw], mweight[...].T
    f_gain = fgain[...].reshape(1, 192)
    m_gain = mgain[...].reshape(1, 768)
    c_gain = cgain[...].reshape(1, 384)

    def two_picks(rows_out, cols_in, parity, place):
        return [
            one_hot(rows_out, cols_in, lambda x, p=p: place(x, p))
            for p in (parity * 8, 8 - parity * 8)
        ]

    for copy in lat_halo:
        copy.wait_recv()
    lat_left[...] = open_tiles(lat_left_in[...])
    lat_right[...] = open_tiles(lat_right_in[...])
    lat[pl.ds(0, 8)] = open_rows(lat_rows_in[0])
    lat[pl.ds(24, 8)] = open_rows(lat_rows_in[1])

    def lat_place(x, p):
        u = x + (s1 + 8)
        return jnp.where(u < 8, 32 + p + u, jnp.where(u < 40, u - 8, 48 + p + u - 40))

    pick = two_picks(32, 64, (8 + s0) & 1, lat_place)
    block = lat[pl.ds(8 + s0, 16)]
    rows_list = []
    for i in range(16):
        pair = (8 + s0 + i) >> 1
        source = jnp.concatenate([block[i], lat_left[pair], lat_right[pair]], axis=0)
        rows_list.append(mm(pick[i % 2], source))
    residual = to_windows(rows_list, 32) + condition
    n1 = (norm(residual)[0] * f_gain).astype(BF)
    fq, fk, fv = (mm(n1, w).astype(BF) for w in fw)
    f_probs, f_mixed = attention(8, FINE_GROUPS, fq, fk, fv, fb, f_masks16, f_masks32)
    fprobs[...] = f_probs
    attn = mm(f_mixed, fproj[...]).astype(BF)
    f_next = residual + attn.astype(F32)
    for i, row in enumerate(to_map(f_next, 16, 32)):
        ahead[i] = row.astype(BF)
    edges = [f_next[256 * wr : 256 * wr + 64].astype(BF) for wr in range(2)]
    ahead_out[...] = pack_tiles(jnp.concatenate(edges, axis=0).reshape(8, 16, 192))
    ahead_rows_out[...] = pack_rows(ahead[pl.ds(0, 8)])
    ahead_halo = [
        net.start(ahead_out, ahead_in.at[pl.ds(0, 12)], net.near(0, -1)),
        net.start(ahead_out.at[pl.ds(0, 6)], ahead_in.at[pl.ds(12, 6)], net.near(-1, -1)),
        net.start(ahead_rows_out, ahead_rows_in, net.near(-1, 0)),
    ]

    for copy in cot_rows:
        copy.wait_recv()
    cot[pl.ds(0, 8)] = open_rows(cot_rows_in[pl.ds(0, 8)])
    cot[pl.ds(24, 16)] = open_rows(cot_rows_in[pl.ds(8, 16)])
    cot_main = cot[pl.ds(8 + t0, 16)]
    cot_next_out[...] = pack_tiles(cot_main[:, :16])
    cot_prev_out[...] = pack_tiles(packed(cot_main[:, 16:].astype(F32)[:, 8:]))
    cot_halo = [
        net.start(cot_next_out, cot_next_in, net.near(0, -1)),
        net.start(cot_prev_out, cot_prev_in, net.near(0, 1)),
    ]

    def ahead_place(x, p):
        u = true_place(x) + d1
        return jnp.where(u < 32, u, u + p)

    pick = two_picks(32, 48, d0 & 1, ahead_place)
    for copy in ahead_halo:
        copy.wait_recv()
    ahead_side[...] = open_tiles(ahead_in[...])
    ahead[pl.ds(16, 8)] = open_rows(ahead_rows_in[...])
    block = ahead[pl.ds(d0, 16)]
    rows_list = []
    for i in range(16):
        source = jnp.concatenate([block[i], ahead_side[(d0 + i) >> 1]], axis=0)
        rows_list.append(mm(pick[i % 2], source))
    merged = jnp.concatenate(paired(rows_list), axis=1)
    m_unit, m_inverse = norm(merged)
    n2 = (m_unit * m_gain).astype(BF)
    c_residual = mm(n2, mweight[...]).astype(BF).astype(F32)
    c_unit, c_inverse = norm(c_residual)
    n3 = (c_unit * c_gain).astype(BF)
    cq, ck, cv = (mm(n3, w).astype(BF) for w in cw)
    c_probs, c_mixed = attention(2, COARSE_GROUPS, cq, ck, cv, cb, c_masks16, c_masks32)
    cprobs[...] = c_probs
    c_attn = mm(c_mixed, cproj[...]).astype(BF)
    c_next = (c_residual + c_attn.astype(F32)).astype(BF)

    head_out = mm(c_next, hweight[...])
    for i, row in enumerate(unpaired([head_out[:, 192 * t : 192 * t + 192] for t in range(4)])):
        head[i] = row.astype(BF)
    first = one_hot(16, 64, lambda x: (x >> 3) * 32 + folded_place(x & 7))
    edges = []
    for i in range(8):
        both = jnp.concatenate([head[2 * i], head[2 * i + 1]], axis=0)
        edges.append(mm(first, both).astype(BF))
    head_next_out[...] = pack_tiles(jnp.stack(edges))
    head_prev_out[...] = pack_tiles(head[:, pl.ds(16, 16)])
    head_halo = [
        net.start(head_prev_out, head_prev_in, net.near(0, 1)),
        net.start(head_next_out, head_next_in, net.near(0, -1)),
    ]

    for copy in cot_halo:
        copy.wait_recv()

    def cot_place(x, p):
        u = true_place(x) + (t1 + 8)
        return jnp.where(u < 8, 48 + p + u, u - 8)

    pick = two_picks(32, 64, 0, cot_place)
    cot_next, cot_prev = open_tiles(cot_next_in[...]), open_tiles(cot_prev_in[...])
    rows_list = []
    for i in range(16):
        source = jnp.concatenate([cot_main[i], cot_next[i], cot_prev[i // 2]], axis=0)
        rows_list.append(mm(pick[i % 2], source))
    grad_out = jnp.concatenate(paired(rows_list), axis=1).astype(BF)
    grad_next = mm(grad_out, hweight_t).astype(BF)
    c_mixed_grad = mm(grad_next, cproj_t).astype(BF)

    g_head = mm_tn(c_next, grad_out)
    for j in range(6):
        works[j // 3][0][pl.ds(24 * (j % 3), 24)] = units(
            g_head[:, 128 * j : 128 * j + 128].astype(BF)
        )
    g_cproj = mm_tn(c_mixed, grad_next)
    for j in range(3):
        works[2][0][pl.ds(24 * j, 24)] = units(g_cproj[:, 128 * j : 128 * j + 128].astype(BF))
    advance(0, 1, 2)

    c_packed = attention_back(
        2, COARSE_GROUPS, cq, ck, cv, cprobs[...], c_mixed_grad, c_masks16, c_masks32,
        lambda w: None,
    )
    rolled = mm(c_packed[0], cw_t[0]) + mm(c_packed[1], cw_t[1]) + mm(c_packed[2], cw_t[2])
    grad_residual = (
        grad_next.astype(F32)
        + norm_back(rolled.astype(BF).astype(F32), c_unit, c_inverse, c_gain)
    ).astype(BF)
    norm_grad = mm(grad_residual, mweight_t).astype(BF).astype(F32)
    merged_grad = norm_back(norm_grad, m_unit, m_inverse, m_gain)
    rows_list = [
        row.astype(BF)
        for row in unpaired([merged_grad[:, 192 * t : 192 * t + 192] for t in range(4)])
    ]
    last = one_hot(16, 64, lambda x: (x >> 3) * 32 + folded_place(24 + (x & 7)))
    edges = []
    for i in range(8):
        both = jnp.concatenate(rows_list[2 * i : 2 * i + 2], axis=0)
        back[8 + 2 * i], back[9 + 2 * i] = rows_list[2 * i], rows_list[2 * i + 1]
        edges.append(mm(last, both).astype(BF))
    back_out[...] = pack_tiles(jnp.stack(edges))
    back_rows_out[...] = pack_rows(jnp.stack(rows_list[8:]))
    back_halo = [
        net.start(back_out, back_in.at[pl.ds(6, 12)], net.near(0, 1)),
        net.start(back_out.at[pl.ds(6, 6)], back_in.at[pl.ds(0, 6)], net.near(1, 1)),
        net.start(back_rows_out, back_rows_in, net.near(1, 0)),
    ]
    advance(0, 1, 2)
    for t in range(3):
        g_part = mm_tn(n3, c_packed[t])
        for j in range(3):
            works[3 + t][0][pl.ds(24 * j, 24)] = units(
                g_part[:, 128 * j : 128 * j + 128].astype(BF)
            )
    advance(3, 4, 5)
    g_merge = mm_tn(n2, grad_residual)
    for t in range(2):
        for j in range(3):
            works[6 + t][0][pl.ds(24 * j, 24)] = units(
                g_merge[384 * t : 384 * t + 384, 128 * j : 128 * j + 128].astype(BF)
            )
    advance(6, 7)
    advance(3, 4, 5)
    def turn_rows():
        for copy in head_halo:
            copy.wait_recv()
        pick = two_picks(32, 64, 0, head_place)
        head_prev, head_next = open_tiles(head_prev_in[...]), open_tiles(head_next_in[...])
        for i in range(16):
            source = jnp.concatenate([head[i], head_prev[i], head_next[i // 2]], axis=0)
            head_rows[16 + i] = mm(pick[i % 2], source).astype(BF)
        head_rows_out[...] = pack_rows(head_rows[pl.ds(16, 16)])
        return [
            net.start(head_rows_out, head_rows_in.at[pl.ds(0, 16)], net.near(1, 0)),
            net.start(head_rows_out.at[pl.ds(0, 8)], head_rows_in.at[pl.ds(16, 8)], net.near(-1, 0)),
        ]

    def head_place(x, p):
        u = x + (16 - t1)
        return jnp.where(
            u < 16, 32 + folded_place(u), jnp.where(u < 48, folded_place(u - 16), u + p)
        )

    advance(6, 7)
    rows_halo = turn_rows()

    def back_place(x, p):
        u = x + (8 - d1)
        return jnp.where(u < 8, 32 + p + u, folded_place(u - 8))

    pick = two_picks(32, 48, d0 & 1, back_place)
    for copy in back_halo:
        copy.wait_recv()

    back_side[...] = open_tiles(back_in[...])
    back[pl.ds(0, 8)] = open_rows(back_rows_in[...])
    block = back[pl.ds(8 - d0, 16)]
    rows_list = []
    for i in range(16):
        source = jnp.concatenate([block[i], back_side[(8 - d0 + i) >> 1]], axis=0)
        rows_list.append(mm(pick[i % 2], source))
    f_grad = to_windows(rows_list, 32).astype(BF)
    f_mixed_grad = mm(f_grad, fproj_t).astype(BF)
    g_fproj = mm_tn(f_mixed, f_grad)

    def between(w):
        if w == 2:
            advance(0, 1, 2)
        if w == 7:
            advance(3, 4, 5, 6, 7)

    f_packed = attention_back(
        8, FINE_GROUPS, fq, fk, fv, fprobs[...], f_mixed_grad, f_masks16, f_masks32, between
    )
    g_parts = [mm_tn(n1, x) for x in f_packed]
    g_parts.append(g_fproj)
    for t in range(4):
        works[8 + t // 2][0][pl.ds(12 * (t % 2), 12)] = units(g_parts[t][:, :128].astype(BF))
    for t in (0, 2):
        tails = jnp.concatenate([g_parts[t][:, 128:], g_parts[t + 1][:, 128:]], axis=1)
        works[10][0][pl.ds(6 * t, 12)] = units(tails.astype(BF))
    advance(8, 9, 10)
    advance(3, 4, 5, 6, 7)
    advance(0, 1, 2)
    advance(8, 9, 10)
    advance(3, 4, 5, 6, 7)
    for copy in rows_halo:
        copy.wait_recv()
    head_rows[pl.ds(0, 16)] = open_rows(head_rows_in[pl.ds(0, 16)])
    head_rows[pl.ds(32, 8)] = open_rows(head_rows_in[pl.ds(16, 8)])
    pred[...] = head_rows[pl.ds(16 - t0, 16)]
    stores.append(pltpu.make_async_copy(pred, pred_out, local.at[16]))
    stores[-1].start()
    advance(8, 9, 10)
    advance(0, 1, 2)
    advance(3, 4, 5, 6, 7)
    advance(8, 9, 10)
    advance(0, 1, 2)
    advance(3, 4, 5, 6, 7)
    advance(8, 9, 10)
    advance(0, 1, 2)
    for copy in stores:
        copy.wait()
    for copy in net.copies:
        copy.wait_send()


N_COPIES = 8 + 4 + 3 + 3 + 4 + 14 * 8 + 20 * 3


def unpack(*refs):
    pred_in, *heres = refs[:12]
    pred_out, *outs = refs[12:19]
    packs, wides, held, sems = refs[19:30], refs[30:36], refs[36], refs[37]
    fq, fp, me, cq, cp, he = wides
    pass_in = pltpu.make_async_copy(pred_in, held, sems.at[17])
    pass_on = pltpu.make_async_copy(held, pred_out.at[0], sems.at[18])
    loads = [pltpu.make_async_copy(heres[g], packs[g], sems.at[g]) for g in range(11)]
    stores = [pltpu.make_async_copy(wides[i], outs[i], sems.at[11 + i]) for i in range(6)]
    for copy in loads + [pass_in]:
        copy.start()

    def take(g, at, count):
        return packs[g][pl.ds(at, count)].reshape(count * 16, 128).astype(F32)

    for t in range(2):
        loads[t].wait()
        for j in range(3):
            he[:, pl.ds(384 * t + 128 * j, 128)] = take(t, 24 * j, 24)
    stores[5].start()
    loads[2].wait()
    for j in range(3):
        cp[:, pl.ds(128 * j, 128)] = take(2, 24 * j, 24)
    stores[4].start()
    for t in range(3):
        loads[3 + t].wait()
        for j in range(3):
            cq[:, pl.ds(384 * t + 128 * j, 128)] = take(3 + t, 24 * j, 24)
    stores[3].start()
    for t in range(2):
        loads[6 + t].wait()
        for j in range(3):
            me[pl.ds(384 * t, 384), pl.ds(128 * j, 128)] = take(6 + t, 24 * j, 24)
    stores[2].start()
    pass_in.wait()
    pass_on.start()
    for g in (8, 9, 10):
        loads[g].wait()
    parts = [take(8 + t // 2, 12 * (t % 2), 12) for t in range(4)]
    tails = [take(10, 12 * t, 12) for t in range(2)]
    fq[...] = jnp.concatenate(
        [parts[0], tails[0][:, :64], parts[1], tails[0][:, 64:], parts[2], tails[1][:, :64]], axis=1
    )
    fp[...] = jnp.concatenate([parts[3], tails[1][:, 64:]], axis=1)
    stores[0].start()
    stores[1].start()
    for copy in stores + [pass_on]:
        copy.wait()


def on_device(
    latents, actions, action_table, offsets, fine_gain, fine_qkv, fine_bias, fine_proj, merge_gain,
    merge_weight, coarse_gain, coarse_qkv, coarse_bias, coarse_proj, head_weight, cotangent,
):
    hbm = pl.BlockSpec(memory_space=pltpu.HBM)
    held = (
        offsets, actions, action_table.T, fine_gain, fine_qkv, fine_bias, fine_proj, merge_gain,
        merge_weight, coarse_gain, coarse_qkv, coarse_bias, coarse_proj, head_weight,
    )
    scratch = [pltpu.SMEM(x.shape, x.dtype) for x in held[:2]]
    scratch += [pltpu.VMEM(x.shape, x.dtype) for x in held[2:]]
    scratch += [
        pltpu.VMEM(shape + (192,), BF)
        for shape in (
            (32, 32), (16, 16), (16, 16), (40, 32), (24, 32), (12, 16), (16, 32), (40, 32), (24, 32),
            (12, 16),
        )
    ]
    scratch += [
        pltpu.VMEM(shape + (128,), BF)
        for shape in (
            (2, 8, 48), (2, 8, 48), (2, 12, 16), (24, 16), (24, 16), (16, 48), (24, 48), (24, 16),
            (24, 16), (12, 16), (12, 16), (8, 48), (8, 48), (12, 16), (18, 16), (8, 48), (8, 48),
            (12, 16), (18, 16), (24, 16), (24, 16), (12, 16), (12, 16), (16, 48), (24, 48),
        )
    ]
    scratch += [
        pltpu.VMEM((8, 64, 384), F32),
        pltpu.VMEM((2, 64, 768), F32),
    ]
    wide = ((72,), (36,), (3, 9), (36,), (4, 9), (4, 9))
    narrow = ((24,), (7, 3), (4, 3), (4, 3))
    for shape in wide * 8 + narrow * 3:
        scratch.append(pltpu.VMEM(shape + (16, 128), BF))
    scratch.append(pltpu.VMEM((16, 32, 192), BF))
    scratch += [pltpu.VMEM((n, 16, 128), BF) for n in UNITS]
    scratch += [
        pltpu.SemaphoreType.DMA((N_COPIES,)),
        pltpu.SemaphoreType.DMA((N_COPIES,)),
        pltpu.SemaphoreType.DMA((28,)),
    ]
    pred, *results = pl.pallas_call(
        body,
        out_shape=[jax.ShapeDtypeStruct((16, 32, 192), BF)]
        + [jax.ShapeDtypeStruct((n, 16, 128), BF) for n in UNITS],
        in_specs=[hbm] * 16,
        out_specs=[hbm] * 12,
        scratch_shapes=scratch,
        compiler_params=pltpu.CompilerParams(
            collective_id=0, has_side_effects=True, vmem_limit_bytes=60 * 1024 * 1024
        ),
        name="block_pair",
    )(*held, latents, cotangent)
    shapes = ((192, 576), (192, 192), (768, 384), (384, 1152), (384, 384), (384, 768))
    return tuple(
        pl.pallas_call(
            unpack,
            out_shape=[jax.ShapeDtypeStruct((1, 16, 32, 192), BF)]
            + [jax.ShapeDtypeStruct(s, F32) for s in shapes],
            in_specs=[hbm] * 12,
            out_specs=[hbm] * 7,
            scratch_shapes=[pltpu.VMEM((n, 16, 128), BF) for n in UNITS]
            + [pltpu.VMEM(s, F32) for s in shapes]
            + [pltpu.VMEM((16, 32, 192), BF), pltpu.SemaphoreType.DMA((19,))],
            compiler_params=pltpu.CompilerParams(vmem_limit_bytes=60 * 1024 * 1024),
            name="unpack",
        )(pred, *results)
    )


def solution(mesh):
    split = P(None, "rows", "cols", None)
    return jax.shard_map(
        on_device,
        mesh=mesh,
        in_specs=(split,) + (P(),) * 14 + (split,),
        out_specs=(split,) + (P(),) * 6,
        check_vma=False,
    )
```

```python
import jax
import jax.numpy as jnp
from jax import lax
from jax.experimental import pallas as pl
from jax.experimental.pallas import tpu as pltpu
from jax.sharding import PartitionSpec as P

MESH = pl.DeviceIdType.MESH
BF = jnp.bfloat16
F32 = jnp.float32
EPS = 1e-05
SCALE = 32 ** (-0.5)
FINE_GROUPS = ((0, 128, 4), (128, 64, 2))
COARSE_GROUPS = ((0, 128, 4), (128, 128, 4), (256, 128, 4))
UNITS = (72,) * 8 + (24,) * 3
N_BUNDLES = len(UNITS)
ORDERS = (("y", "z", "x"), ("z", "x", "y"), ("x", "y", "z"))


def mm(a, b):
    return lax.dot_general(a, b, (((1,), (0,)), ((), ())), preferred_element_type=F32)


def mm_nt(a, b):
    return lax.dot_general(a, b, (((1,), (1,)), ((), ())), preferred_element_type=F32)


def mm_tn(a, b):
    return lax.dot_general(a, b, (((0,), (0,)), ((), ())), preferred_element_type=F32)


def norm(x):
    centred = x - jnp.mean(x, axis=-1, keepdims=True)
    inverse = lax.rsqrt(jnp.mean(centred * centred, axis=-1, keepdims=True) + EPS)
    return centred * inverse, inverse


def norm_back(upstream, unit, inverse, gain):
    e = upstream * gain
    return inverse * (
        e - jnp.mean(e, axis=-1, keepdims=True) - unit * jnp.mean(e * unit, axis=-1, keepdims=True)
    )


def head_masks(width, heads, dtype):
    lane = lax.broadcasted_iota(jnp.int32, (1, width), 1) // 32
    return [jnp.where(lane == h, 1.0, 0.0).astype(dtype) for h in range(heads)]


def spread(x, masks):
    return jnp.concatenate([x * m for m in masks], axis=0)


def fold(x, masks):
    total = x[:64] * masks[0]
    for h in range(1, len(masks)):
        total = total + x[64 * h : 64 * h + 64] * masks[h]
    return total


def parts_of(groups, x, w):
    return [x[64 * w : 64 * w + 64, at : at + wide] for at, wide, _ in groups]


def lanes_of(groups, x):
    return [x[:, 2 * at : 2 * at + 64 * heads] for at, _, heads in groups]


def attention(count, groups, q, k, v, bias, masks16, masks32):
    scores = []
    for w in range(count):
        line = [
            mm_nt(kg, spread(qg, m))
            for qg, kg, m in zip(parts_of(groups, q, w), parts_of(groups, k, w), masks16)
        ]
        scores.append(jnp.concatenate(line, axis=1))
    s = jnp.stack(scores) * SCALE + bias[None]
    e = jnp.exp(s - jnp.max(s, axis=1, keepdims=True))
    probs = e * (1.0 / jnp.sum(e, axis=1, keepdims=True))
    weights = probs.astype(BF)
    mixed = []
    for w in range(count):
        line = [
            fold(mm_tn(pg, vg), m)
            for pg, vg, m in zip(lanes_of(groups, weights[w]), parts_of(groups, v, w), masks32)
        ]
        mixed.append(jnp.concatenate(line, axis=1))
    return probs, jnp.concatenate(mixed, axis=0).astype(BF)


def attention_back(count, groups, q, k, v, probs, mixed_grad, masks16, masks32, between):
    grads = []
    many = []
    for w in range(count):
        many.append(
            [spread(mg, m) for mg, m in zip(parts_of(groups, mixed_grad, w), masks16)]
        )
        line = [mm_nt(vg, mg) for vg, mg in zip(parts_of(groups, v, w), many[w])]
        grads.append(jnp.concatenate(line, axis=1))
    wg = jnp.stack(grads).astype(BF).astype(F32)
    sg = (probs * (wg - jnp.sum(probs * wg, axis=1, keepdims=True)) * SCALE).astype(BF)
    weights = probs.astype(BF)
    out = [[], [], []]
    for w in range(count):
        between(w)
        scored, weighed = lanes_of(groups, sg[w]), lanes_of(groups, weights[w])
        qs, ks = parts_of(groups, q, w), parts_of(groups, k, w)
        dq = [fold(mm_tn(x, kg), m) for x, kg, m in zip(scored, ks, masks32)]
        dk = [mm(x, spread(qg, m)) for x, qg, m in zip(scored, qs, masks16)]
        dv = [mm(x, mg) for x, mg in zip(weighed, many[w])]
        for have, line in zip(out, (dq, dk, dv)):
            have.append(jnp.concatenate(line, axis=1))
    return [jnp.concatenate(x, axis=0).astype(BF) for x in out]


def folded_place(u):
    v = u & 15
    return (u - v) + (v & 1) * 8 + (v >> 1)


def true_place(p):
    v = p & 15
    return (p - v) + (v & 7) * 2 + (v >> 3)


def units(x):
    return x.reshape(x.shape[0] // 16, 16, 128)


class Net:
    def __init__(self, send, recv):
        self.r = lax.axis_index("rows")
        self.c = lax.axis_index("cols")
        r, c = self.r, self.c
        self.core = lax.rem(r, 2)
        xlo = lax.rem(r // 2, 2)
        self.y = r // 4
        self.z = c // 2
        xhi = lax.rem(c, 2)
        self.x = xhi * 2 + xlo
        self.low = lax.rem(r, 4)
        self.xhi = xhi
        self.send, self.recv = send, recv
        self.count = 0
        self.copies = []

    def near(self, dr, dc):
        return (lax.rem(self.r + dr + 16, 16), lax.rem(self.c + dc + 8, 8))

    def place(self, axis):
        return {"x": self.x, "y": self.y, "z": self.z}[axis]

    def peer(self, axis, index, core=None):
        core = self.core if core is None else core
        low = self.low - self.core + core
        if axis == "y":
            return (index * 4 + low, self.c)
        if axis == "z":
            return (self.y * 4 + low, index * 2 + self.xhi)
        return (self.y * 4 + lax.rem(index, 2) * 2 + core, self.z * 2 + index // 2)

    def sibling(self):
        return (self.r + 1 - 2 * self.core, self.c)

    def start(self, source, target, device):
        n = self.count
        self.count += 1
        copy = pltpu.make_async_remote_copy(
            src_ref=source,
            dst_ref=target,
            send_sem=self.send.at[n],
            recv_sem=self.recv.at[n],
            device_id=device,
            device_id_type=MESH,
        )
        copy.start()
        self.copies.append(copy)
        return copy

    def greet(self):
        sem = pltpu.get_barrier_semaphore()
        others = [self.near(a, b) for a in (-1, 0, 1) for b in (-1, 0, 1) if (a, b) != (0, 0)]
        others.append(self.sibling())
        for axis in "xyz":
            others += [self.peer(axis, lax.rem(self.place(axis) + k, 4)) for k in (1, 2, 3)]
            others += [
                self.peer(axis, lax.rem(self.place(axis) + k, 4), 1 - self.core)
                for k in (1, 2, 3)
            ]
        for device in others:
            pl.semaphore_signal(sem, inc=1, device_id=device, device_id_type=MESH)
        self.greeted = len(others)

    def gather(self):
        pl.semaphore_wait(pltpu.get_barrier_semaphore(), self.greeted)


class Reduce:
    def __init__(self, net, order, terms, got_core, got_a, sum_a, got_b, got_c, result):
        self.net, self.order = net, order
        self.terms, self.got_core, self.got_a, self.sum_a = terms, got_core, got_a, sum_a
        self.got_b, self.got_c, self.result = got_b, got_c, result
        self.half, self.part = terms.shape[0] // 2, terms.shape[0] // 8
        self.stage = 0
        self.flight = []

    def step(self):
        getattr(self, "step%d" % self.stage)()
        self.stage += 1

    def arrive(self):
        for copy in self.flight:
            copy.wait_recv()

    def to_peers(self, axis, source, target):
        net = self.net
        me = net.place(axis)
        self.flight = []
        for k in (1, 2, 3):
            to = lax.rem(me + k, 4)
            self.flight.append(net.start(source(to), target(k), net.peer(axis, to)))

    def spread_out(self, total, got, axis):
        me = self.net.place(axis)
        got[pl.ds(me, 1)] = total.astype(BF)[None]
        self.to_peers(axis, lambda to: got.at[me], lambda k: got.at[me])

    def summed(self, got):
        total = got[0].astype(F32)
        for k in (1, 2, 3):
            total = total + got[k].astype(F32)
        return total

    def step0(self):
        net, half = self.net, self.half
        self.flight = [
            net.start(self.terms.at[pl.ds((1 - net.core) * half, half)], self.got_core, net.sibling())
        ]

    def step1(self):
        net, half, part = self.net, self.half, self.part
        self.arrive()
        own = self.terms[pl.ds(net.core * half, half)].astype(F32)
        self.sum_a[...] = (own + self.got_core[...].astype(F32)).astype(BF)
        self.to_peers(
            self.order[0],
            lambda to: self.sum_a.at[pl.ds(to * part, part)],
            lambda k: self.got_a.at[k - 1],
        )

    def step2(self):
        self.arrive()
        me = self.net.place(self.order[0])
        total = self.sum_a[pl.ds(me * self.part, self.part)].astype(F32)
        for k in range(3):
            total = total + self.got_a[k].astype(F32)
        self.spread_out(total, self.got_b, self.order[1])

    def step3(self):
        self.arrive()
        self.spread_out(self.summed(self.got_b), self.got_c, self.order[2])

    def step4(self):
        self.arrive()
        at = self.net.core * self.half + self.net.place(self.order[0]) * self.part
        mine = self.result.at[pl.ds(at, self.part)]
        mine[...] = self.summed(self.got_c).astype(BF)
        self.to_peers(self.order[0], lambda to: mine, lambda k: mine)

    def step5(self):
        self.arrive()
        mine = self.result.at[pl.ds(self.net.core * self.half, self.half)]
        self.flight = [self.net.start(mine, mine, self.net.sibling())]

    def step6(self):
        self.arrive()


class Direct(Reduce):
    def __init__(self, net, order, terms, got_a, got_b, got_c, result):
        super().__init__(net, order, terms, None, got_a, None, got_b, got_c, result)
        self.at = (net.core * 4 + net.place(order[0])) * self.part

    def to_eight(self, source, target):
        net = self.net
        me = net.place(self.order[0])
        self.flight = []
        for k in range(1, 8):
            to, core = lax.rem(me + k, 4), lax.rem(net.core + k // 4, 2)
            self.flight.append(
                net.start(
                    source((core * 4 + to) * self.part),
                    target(k - 1),
                    net.peer(self.order[0], to, core),
                )
            )

    def step0(self):
        self.to_eight(lambda at: self.terms.at[pl.ds(at, self.part)], lambda k: self.got_a.at[k])

    def step1(self):
        self.arrive()
        total = self.terms[pl.ds(self.at, self.part)].astype(F32)
        for k in range(7):
            total = total + self.got_a[k].astype(F32)
        self.spread_out(total, self.got_b, self.order[1])

    def step2(self):
        self.step3()

    def step3(self):
        if self.stage == 2:
            Reduce.step3(self)
        else:
            self.arrive()
            mine = self.result.at[pl.ds(self.at, self.part)]
            mine[...] = self.summed(self.got_c).astype(BF)
            self.to_eight(lambda at: mine, lambda k: mine)

    def step4(self):
        self.arrive()
        self.stage = 6


def to_map(x, rows, cols):
    wide = cols // 8
    out = []
    for i in range(rows):
        base = (i // 8) * wide
        out.append(
            jnp.concatenate(
                [x[(base + w) * 64 + (i % 8) * 8 :][:8] for w in range(wide)], axis=0
            )
        )
    return out


def to_windows(rows_list, cols):
    wide = cols // 8
    pieces = []
    for wr in range(len(rows_list) // 8):
        for w in range(wide):
            for i in range(8):
                pieces.append(rows_list[wr * 8 + i][8 * w : 8 * w + 8])
    return jnp.concatenate(pieces, axis=0)


def paired(rows_list):
    out = []
    for di in (0, 1):
        for dj in (0, 1):
            out.append(
                jnp.concatenate(
                    [
                        rows_list[2 * i + di][16 * w + 8 * dj :][:8]
                        for w in (0, 1)
                        for i in range(8)
                    ],
                    axis=0,
                )
            )
    return out


def unpaired(parts):
    rows_list = []
    for row in range(16):
        i, di = row // 2, row % 2
        rows_list.append(
            jnp.concatenate(
                [
                    parts[2 * di + dj][64 * w + 8 * i :][:8]
                    for w in (0, 1)
                    for dj in (0, 1)
                ],
                axis=0,
            )
        )
    return rows_list


def packed(x):
    return x.reshape(128, x.shape[-1]).astype(BF).reshape(8, 16, x.shape[-1])


def pack_rows(x):
    tails = jnp.concatenate([x[:, :16, 128:], x[:, 16:, 128:]], axis=2)
    return jnp.concatenate([x[:, :, :128], tails], axis=1)


def open_rows(x):
    tails = jnp.concatenate([x[:, 32:, :64], x[:, 32:, 64:]], axis=1)
    return jnp.concatenate([x[:, :32], tails], axis=2)


def pack_tiles(x):
    m = x.shape[0] // 2
    x = x.reshape(m, 2, 16, 192)
    tails = jnp.concatenate([x[:, 0, :, 128:], x[:, 1, :, 128:]], axis=2)
    return jnp.stack([x[:, 0, :, :128], x[:, 1, :, :128], tails], axis=1).reshape(3 * m, 16, 128)


def open_tiles(x):
    m = x.shape[0] // 3
    x = x.reshape(m, 3, 16, 128)
    first = jnp.concatenate([x[:, 0], x[:, 2, :, :64]], axis=2)
    second = jnp.concatenate([x[:, 1], x[:, 2, :, 64:]], axis=2)
    return jnp.stack([first, second], axis=1).reshape(2 * m, 16, 192)


def one_hot(rows_out, cols_in, place):
    x = lax.broadcasted_iota(jnp.int32, (rows_out, cols_in), 0)
    u = lax.broadcasted_iota(jnp.int32, (rows_out, cols_in), 1)
    return jnp.where(place(x) == u, 1.0, 0.0).astype(BF)


def body(*refs):
    (
        offsets, actions, table, fgain, fqkv, fbias, fproj, mgain, mweight, cgain, cqkv, cbias,
        cproj, hweight,
    ) = refs[28:42]
    lat_hbm, cot_hbm = refs[14:16]
    pred_out, *result_outs = refs[16:28]
    (
        lat, lat_left, lat_right, cot, ahead, ahead_side, head, head_rows, back, back_side,
        lat_rows_out, lat_rows_in, lat_out, lat_left_in, lat_right_in, cot_rows_out, cot_rows_in,
        cot_next_out, cot_next_in, cot_prev_out, cot_prev_in, ahead_rows_out, ahead_rows_in,
        ahead_out, ahead_in, back_rows_out, back_rows_in, back_out, back_in, head_prev_out,
        head_prev_in, head_next_out, head_next_in, head_rows_out, head_rows_in, fprobs, cprobs,
    ) = refs[42:79]
    rest = refs[79:]
    works = [rest[6 * g : 6 * g + 6] for g in range(8)]
    works += [rest[48 + 4 * g : 52 + 4 * g] for g in range(3)]
    pred, *results = rest[60:72]
    send, recv, local = rest[72:]
    loads = [
        pltpu.make_async_copy(refs[i], refs[28 + i], local.at[2 + i]) for i in range(14)
    ]
    net = Net(send, recv)
    net.greet()
    bundles = [
        (Reduce if g < 8 else Direct)(net, ORDERS[g % 3], *works[g], results[g])
        for g in range(N_BUNDLES)
    ]

    def store(g, start, count, sem):
        run = pl.ds(start, count)
        copy = pltpu.make_async_copy(
            results[g].at[run], result_outs[g].at[run], local.at[sem]
        )
        copy.start()
        stores.append(copy)

    def advance(*numbers):
        for g in numbers:
            bundle = bundles[g]
            bundle.step()
            if g >= 8:
                if bundle.stage == 7:
                    store(g, 0, UNITS[g], 17 + g)
            elif bundle.stage == 6:
                store(g, net.core * bundle.half, bundle.half, 17 + g)
            elif bundle.stage == 7:
                store(g, (1 - net.core) * bundle.half, bundle.half, 28 + g)

    stores = []
    own_lat = pltpu.make_async_copy(lat_hbm.at[0], lat.at[pl.ds(8, 16)], local.at[0])
    own_cot = pltpu.make_async_copy(cot_hbm.at[0], cot.at[pl.ds(8, 16)], local.at[1])
    for copy in [own_lat] + loads[:6] + loads[6:] + [own_cot]:
        copy.start()

    own_lat.wait()
    low = lat[pl.ds(8, 16), pl.ds(0, 16)].astype(F32)
    high = lat[pl.ds(8, 16), pl.ds(16, 16)].astype(F32)
    lat_out[0] = pack_tiles(packed(low[:, :8]))
    lat_out[1] = pack_tiles(packed(high[:, 8:]))
    lat_rows_out[0] = pack_rows(lat[pl.ds(8, 8)])
    lat_rows_out[1] = pack_rows(lat[pl.ds(16, 8)])
    net.gather()
    lat_halo = []
    for side, dc, target in ((0, -1, lat_right_in), (1, 1, lat_left_in)):
        for dr, fr, nr, tr in ((0, 0, 12, 6), (-1, 0, 6, 18), (1, 6, 6, 0)):
            lat_halo.append(
                net.start(
                    lat_out.at[side, pl.ds(fr, nr)], target.at[pl.ds(tr, nr)], net.near(dr, dc)
                )
            )
    lat_halo.append(net.start(lat_rows_out.at[0], lat_rows_in.at[1], net.near(-1, 0)))
    lat_halo.append(net.start(lat_rows_out.at[1], lat_rows_in.at[0], net.near(1, 0)))

    own_cot.wait()
    cot_rows_out[...] = pack_rows(cot[pl.ds(8, 16)])
    cot_rows = [
        net.start(cot_rows_out, cot_rows_in.at[pl.ds(8, 16)], net.near(-1, 0)),
        net.start(cot_rows_out.at[pl.ds(8, 8)], cot_rows_in.at[pl.ds(0, 8)], net.near(1, 0)),
    ]

    for copy in loads:
        copy.wait()
    a0, a1 = offsets[0, 0], offsets[0, 1]
    b0, b1 = 2 * offsets[1, 0], 2 * offsets[1, 1]
    d0, d1 = lax.rem(b0 - a0 + 8, 8), lax.rem(b1 - a1 + 8, 8)
    s0, s1 = lax.rem(b0 - d0 + 8, 16) - 8, lax.rem(b1 - d1 + 8, 16) - 8
    t0, t1 = s0 + d0, s1 + d1
    code = lax.broadcasted_iota(jnp.int32, (8, 256), 1)
    counts = jnp.zeros((8, 256), F32)
    for j in range(16):
        counts = counts + jnp.where(code == actions[0, j], 1.0, 0.0)
    condition = mm_nt(counts.astype(BF), table[...])[:1] * (1.0 / 16.0)
    f_masks16 = [head_masks(w, h, BF) for _, w, h in FINE_GROUPS]
    f_masks32 = [head_masks(w, h, F32) for _, w, h in FINE_GROUPS]
    c_masks16 = [head_masks(w, h, BF) for _, w, h in COARSE_GROUPS]
    c_masks32 = [head_masks(w, h, F32) for _, w, h in COARSE_GROUPS]
    fb = fbias[...].reshape(384, 64).T
    cb = cbias[...].reshape(768, 64).T
    fw = [fqkv[:, 192 * i : 192 * i + 192] for i in range(3)]
    cw = [cqkv[:, 384 * i : 384 * i + 384] for i in range(3)]
    fproj_t, cproj_t, hweight_t = fproj[...].T, cproj[...].T, hweight[...].T
    cw_t, mweight_t = [w.T for w in cw], mweight[...].T
    f_gain = fgain[...].reshape(1, 192)
    m_gain = mgain[...].reshape(1, 768)
    c_gain = cgain[...].reshape(1, 384)

    def two_picks(rows_out, cols_in, parity, place):
        return [
            one_hot(rows_out, cols_in, lambda x, p=p: place(x, p))
            for p in (parity * 8, 8 - parity * 8)
        ]

    for copy in lat_halo:
        copy.wait_recv()
    lat_left[...] = open_tiles(lat_left_in[...])
    lat_right[...] = open_tiles(lat_right_in[...])
    lat[pl.ds(0, 8)] = open_rows(lat_rows_in[0])
    lat[pl.ds(24, 8)] = open_rows(lat_rows_in[1])

    def lat_place(x, p):
        u = x + (s1 + 8)
        return jnp.where(u < 8, 32 + p + u, jnp.where(u < 40, u - 8, 48 + p + u - 40))

    pick = two_picks(32, 64, (8 + s0) & 1, lat_place)
    block = lat[pl.ds(8 + s0, 16)]
    rows_list = []
    for i in range(16):
        pair = (8 + s0 + i) >> 1
        source = jnp.concatenate([block[i], lat_left[pair], lat_right[pair]], axis=0)
        rows_list.append(mm(pick[i % 2], source))
    residual = to_windows(rows_list, 32) + condition
    n1 = (norm(residual)[0] * f_gain).astype(BF)
    fq, fk, fv = (mm(n1, w).astype(BF) for w in fw)
    f_probs, f_mixed = attention(8, FINE_GROUPS, fq, fk, fv, fb, f_masks16, f_masks32)
    fprobs[...] = f_probs
    attn = mm(f_mixed, fproj[...]).astype(BF)
    f_next = residual + attn.astype(F32)
    for i, row in enumerate(to_map(f_next, 16, 32)):
        ahead[i] = row.astype(BF)
    edges = [f_next[256 * wr : 256 * wr + 64].astype(BF) for wr in range(2)]
    ahead_out[...] = pack_tiles(jnp.concatenate(edges, axis=0).reshape(8, 16, 192))
    ahead_rows_out[...] = pack_rows(ahead[pl.ds(0, 8)])
    ahead_halo = [
        net.start(ahead_out, ahead_in.at[pl.ds(0, 12)], net.near(0, -1)),
        net.start(ahead_out.at[pl.ds(0, 6)], ahead_in.at[pl.ds(12, 6)], net.near(-1, -1)),
        net.start(ahead_rows_out, ahead_rows_in, net.near(-1, 0)),
    ]

    for copy in cot_rows:
        copy.wait_recv()
    cot[pl.ds(0, 8)] = open_rows(cot_rows_in[pl.ds(0, 8)])
    cot[pl.ds(24, 16)] = open_rows(cot_rows_in[pl.ds(8, 16)])
    cot_main = cot[pl.ds(8 + t0, 16)]
    cot_next_out[...] = pack_tiles(cot_main[:, :16])
    cot_prev_out[...] = pack_tiles(packed(cot_main[:, 16:].astype(F32)[:, 8:]))
    cot_halo = [
        net.start(cot_next_out, cot_next_in, net.near(0, -1)),
        net.start(cot_prev_out, cot_prev_in, net.near(0, 1)),
    ]

    def ahead_place(x, p):
        u = true_place(x) + d1
        return jnp.where(u < 32, u, u + p)

    pick = two_picks(32, 48, d0 & 1, ahead_place)
    for copy in ahead_halo:
        copy.wait_recv()
    ahead_side[...] = open_tiles(ahead_in[...])
    ahead[pl.ds(16, 8)] = open_rows(ahead_rows_in[...])
    block = ahead[pl.ds(d0, 16)]
    rows_list = []
    for i in range(16):
        source = jnp.concatenate([block[i], ahead_side[(d0 + i) >> 1]], axis=0)
        rows_list.append(mm(pick[i % 2], source))
    merged = jnp.concatenate(paired(rows_list), axis=1)
    m_unit, m_inverse = norm(merged)
    n2 = (m_unit * m_gain).astype(BF)
    c_residual = mm(n2, mweight[...]).astype(BF).astype(F32)
    c_unit, c_inverse = norm(c_residual)
    n3 = (c_unit * c_gain).astype(BF)
    cq, ck, cv = (mm(n3, w).astype(BF) for w in cw)
    c_probs, c_mixed = attention(2, COARSE_GROUPS, cq, ck, cv, cb, c_masks16, c_masks32)
    cprobs[...] = c_probs
    c_attn = mm(c_mixed, cproj[...]).astype(BF)
    c_next = (c_residual + c_attn.astype(F32)).astype(BF)

    head_out = mm(c_next, hweight[...])
    for i, row in enumerate(unpaired([head_out[:, 192 * t : 192 * t + 192] for t in range(4)])):
        head[i] = row.astype(BF)
    first = one_hot(16, 64, lambda x: (x >> 3) * 32 + folded_place(x & 7))
    edges = []
    for i in range(8):
        both = jnp.concatenate([head[2 * i], head[2 * i + 1]], axis=0)
        edges.append(mm(first, both).astype(BF))
    head_next_out[...] = pack_tiles(jnp.stack(edges))
    head_prev_out[...] = pack_tiles(head[:, pl.ds(16, 16)])
    head_halo = [
        net.start(head_prev_out, head_prev_in, net.near(0, 1)),
        net.start(head_next_out, head_next_in, net.near(0, -1)),
    ]

    for copy in cot_halo:
        copy.wait_recv()

    def cot_place(x, p):
        u = true_place(x) + (t1 + 8)
        return jnp.where(u < 8, 48 + p + u, u - 8)

    pick = two_picks(32, 64, 0, cot_place)
    cot_next, cot_prev = open_tiles(cot_next_in[...]), open_tiles(cot_prev_in[...])
    rows_list = []
    for i in range(16):
        source = jnp.concatenate([cot_main[i], cot_next[i], cot_prev[i // 2]], axis=0)
        rows_list.append(mm(pick[i % 2], source))
    grad_out = jnp.concatenate(paired(rows_list), axis=1).astype(BF)
    grad_next = mm(grad_out, hweight_t).astype(BF)
    c_mixed_grad = mm(grad_next, cproj_t).astype(BF)

    g_head = mm_tn(c_next, grad_out)
    for j in range(6):
        works[j // 3][0][pl.ds(24 * (j % 3), 24)] = units(
            g_head[:, 128 * j : 128 * j + 128].astype(BF)
        )
    g_cproj = mm_tn(c_mixed, grad_next)
    for j in range(3):
        works[2][0][pl.ds(24 * j, 24)] = units(g_cproj[:, 128 * j : 128 * j + 128].astype(BF))
    advance(0, 1, 2)

    c_packed = attention_back(
        2, COARSE_GROUPS, cq, ck, cv, cprobs[...], c_mixed_grad, c_masks16, c_masks32,
        lambda w: None,
    )
    rolled = mm(c_packed[0], cw_t[0]) + mm(c_packed[1], cw_t[1]) + mm(c_packed[2], cw_t[2])
    grad_residual = (
        grad_next.astype(F32)
        + norm_back(rolled.astype(BF).astype(F32), c_unit, c_inverse, c_gain)
    ).astype(BF)
    norm_grad = mm(grad_residual, mweight_t).astype(BF).astype(F32)
    merged_grad = norm_back(norm_grad, m_unit, m_inverse, m_gain)
    rows_list = [
        row.astype(BF)
        for row in unpaired([merged_grad[:, 192 * t : 192 * t + 192] for t in range(4)])
    ]
    last = one_hot(16, 64, lambda x: (x >> 3) * 32 + folded_place(24 + (x & 7)))
    edges = []
    for i in range(8):
        both = jnp.concatenate(rows_list[2 * i : 2 * i + 2], axis=0)
        back[8 + 2 * i], back[9 + 2 * i] = rows_list[2 * i], rows_list[2 * i + 1]
        edges.append(mm(last, both).astype(BF))
    back_out[...] = pack_tiles(jnp.stack(edges))
    back_rows_out[...] = pack_rows(jnp.stack(rows_list[8:]))
    back_halo = [
        net.start(back_out, back_in.at[pl.ds(6, 12)], net.near(0, 1)),
        net.start(back_out.at[pl.ds(6, 6)], back_in.at[pl.ds(0, 6)], net.near(1, 1)),
        net.start(back_rows_out, back_rows_in, net.near(1, 0)),
    ]
    advance(0, 1, 2)
    for t in range(3):
        g_part = mm_tn(n3, c_packed[t])
        for j in range(3):
            works[3 + t][0][pl.ds(24 * j, 24)] = units(
                g_part[:, 128 * j : 128 * j + 128].astype(BF)
            )
    advance(3, 4, 5)
    g_merge = mm_tn(n2, grad_residual)
    for t in range(2):
        for j in range(3):
            works[6 + t][0][pl.ds(24 * j, 24)] = units(
                g_merge[384 * t : 384 * t + 384, 128 * j : 128 * j + 128].astype(BF)
            )
    advance(6, 7)
    advance(3, 4, 5)
    def turn_rows():
        for copy in head_halo:
            copy.wait_recv()
        pick = two_picks(32, 64, 0, head_place)
        head_prev, head_next = open_tiles(head_prev_in[...]), open_tiles(head_next_in[...])
        for i in range(16):
            source = jnp.concatenate([head[i], head_prev[i], head_next[i // 2]], axis=0)
            head_rows[16 + i] = mm(pick[i % 2], source).astype(BF)
        head_rows_out[...] = pack_rows(head_rows[pl.ds(16, 16)])
        return [
            net.start(head_rows_out, head_rows_in.at[pl.ds(0, 16)], net.near(1, 0)),
            net.start(head_rows_out.at[pl.ds(0, 8)], head_rows_in.at[pl.ds(16, 8)], net.near(-1, 0)),
        ]

    def head_place(x, p):
        u = x + (16 - t1)
        return jnp.where(
            u < 16, 32 + folded_place(u), jnp.where(u < 48, folded_place(u - 16), u + p)
        )

    advance(6, 7)
    rows_halo = turn_rows()

    def back_place(x, p):
        u = x + (8 - d1)
        return jnp.where(u < 8, 32 + p + u, folded_place(u - 8))

    pick = two_picks(32, 48, d0 & 1, back_place)
    for copy in back_halo:
        copy.wait_recv()

    back_side[...] = open_tiles(back_in[...])
    back[pl.ds(0, 8)] = open_rows(back_rows_in[...])
    block = back[pl.ds(8 - d0, 16)]
    rows_list = []
    for i in range(16):
        source = jnp.concatenate([block[i], back_side[(8 - d0 + i) >> 1]], axis=0)
        rows_list.append(mm(pick[i % 2], source))
    f_grad = to_windows(rows_list, 32).astype(BF)
    f_mixed_grad = mm(f_grad, fproj_t).astype(BF)
    g_fproj = mm_tn(f_mixed, f_grad)

    def between(w):
        if w == 2:
            advance(0, 1, 2)
        if w == 7:
            advance(3, 4, 5, 6, 7)

    f_packed = attention_back(
        8, FINE_GROUPS, fq, fk, fv, fprobs[...], f_mixed_grad, f_masks16, f_masks32, between
    )
    g_parts = [mm_tn(n1, x) for x in f_packed]
    g_parts.append(g_fproj)
    for t in range(4):
        works[8 + t // 2][0][pl.ds(12 * (t % 2), 12)] = units(g_parts[t][:, :128].astype(BF))
    for t in (0, 2):
        tails = jnp.concatenate([g_parts[t][:, 128:], g_parts[t + 1][:, 128:]], axis=1)
        works[10][0][pl.ds(6 * t, 12)] = units(tails.astype(BF))
    advance(8, 9, 10)
    advance(3, 4, 5, 6, 7)
    advance(0, 1, 2)
    advance(8, 9, 10)
    advance(3, 4, 5, 6, 7)
    for copy in rows_halo:
        copy.wait_recv()
    head_rows[pl.ds(0, 16)] = open_rows(head_rows_in[pl.ds(0, 16)])
    head_rows[pl.ds(32, 8)] = open_rows(head_rows_in[pl.ds(16, 8)])
    pred[...] = head_rows[pl.ds(16 - t0, 16)]
    stores.append(pltpu.make_async_copy(pred, pred_out, local.at[16]))
    stores[-1].start()
    advance(8, 9, 10)
    advance(0, 1, 2)
    advance(3, 4, 5, 6, 7)
    advance(8, 9, 10)
    advance(0, 1, 2)
    advance(3, 4, 5, 6, 7)
    advance(8, 9, 10)
    advance(0, 1, 2)
    for copy in stores:
        copy.wait()
    for copy in net.copies:
        copy.wait_send()


N_COPIES = 8 + 4 + 3 + 3 + 4 + 14 * 8 + 20 * 3


def unpack(*refs):
    pred_in, *heres = refs[:12]
    pred_out, *outs = refs[12:19]
    packs, wides, held, sems = refs[19:30], refs[30:36], refs[36], refs[37]
    fq, fp, me, cq, cp, he = wides
    pass_in = pltpu.make_async_copy(pred_in, held, sems.at[17])
    pass_on = pltpu.make_async_copy(held, pred_out.at[0], sems.at[18])
    loads = [pltpu.make_async_copy(heres[g], packs[g], sems.at[g]) for g in range(11)]
    stores = [pltpu.make_async_copy(wides[i], outs[i], sems.at[11 + i]) for i in range(6)]
    for copy in loads + [pass_in]:
        copy.start()

    def take(g, at, count):
        return packs[g][pl.ds(at, count)].reshape(count * 16, 128).astype(F32)

    for t in range(2):
        loads[t].wait()
        for j in range(3):
            he[:, pl.ds(384 * t + 128 * j, 128)] = take(t, 24 * j, 24)
    stores[5].start()
    loads[2].wait()
    for j in range(3):
        cp[:, pl.ds(128 * j, 128)] = take(2, 24 * j, 24)
    stores[4].start()
    for t in range(3):
        loads[3 + t].wait()
        for j in range(3):
            cq[:, pl.ds(384 * t + 128 * j, 128)] = take(3 + t, 24 * j, 24)
    stores[3].start()
    for t in range(2):
        loads[6 + t].wait()
        for j in range(3):
            me[pl.ds(384 * t, 384), pl.ds(128 * j, 128)] = take(6 + t, 24 * j, 24)
    stores[2].start()
    pass_in.wait()
    pass_on.start()
    for g in (8, 9, 10):
        loads[g].wait()
    parts = [take(8 + t // 2, 12 * (t % 2), 12) for t in range(4)]
    tails = [take(10, 12 * t, 12) for t in range(2)]
    fq[...] = jnp.concatenate(
        [parts[0], tails[0][:, :64], parts[1], tails[0][:, 64:], parts[2], tails[1][:, :64]], axis=1
    )
    fp[...] = jnp.concatenate([parts[3], tails[1][:, 64:]], axis=1)
    stores[0].start()
    stores[1].start()
    for copy in stores + [pass_on]:
        copy.wait()


def on_device(
    latents, actions, action_table, offsets, fine_gain, fine_qkv, fine_bias, fine_proj, merge_gain,
    merge_weight, coarse_gain, coarse_qkv, coarse_bias, coarse_proj, head_weight, cotangent,
):
    hbm = pl.BlockSpec(memory_space=pltpu.HBM)
    held = (
        offsets, actions, action_table.T, fine_gain, fine_qkv, fine_bias, fine_proj, merge_gain,
        merge_weight, coarse_gain, coarse_qkv, coarse_bias, coarse_proj, head_weight,
    )
    scratch = [pltpu.SMEM(x.shape, x.dtype) for x in held[:2]]
    scratch += [pltpu.VMEM(x.shape, x.dtype) for x in held[2:]]
    scratch += [
        pltpu.VMEM(shape + (192,), BF)
        for shape in (
            (32, 32), (16, 16), (16, 16), (40, 32), (24, 32), (12, 16), (16, 32), (40, 32), (24, 32),
            (12, 16),
        )
    ]
    scratch += [
        pltpu.VMEM(shape + (128,), BF)
        for shape in (
            (2, 8, 48), (2, 8, 48), (2, 12, 16), (24, 16), (24, 16), (16, 48), (24, 48), (24, 16),
            (24, 16), (12, 16), (12, 16), (8, 48), (8, 48), (12, 16), (18, 16), (8, 48), (8, 48),
            (12, 16), (18, 16), (24, 16), (24, 16), (12, 16), (12, 16), (16, 48), (24, 48),
        )
    ]
    scratch += [
        pltpu.VMEM((8, 64, 384), F32),
        pltpu.VMEM((2, 64, 768), F32),
    ]
    wide = ((72,), (36,), (3, 9), (36,), (4, 9), (4, 9))
    narrow = ((24,), (7, 3), (4, 3), (4, 3))
    for shape in wide * 8 + narrow * 3:
        scratch.append(pltpu.VMEM(shape + (16, 128), BF))
    scratch.append(pltpu.VMEM((16, 32, 192), BF))
    scratch += [pltpu.VMEM((n, 16, 128), BF) for n in UNITS]
    scratch += [
        pltpu.SemaphoreType.DMA((N_COPIES,)),
        pltpu.SemaphoreType.DMA((N_COPIES,)),
        pltpu.SemaphoreType.DMA((36,)),
    ]
    pred, *results = pl.pallas_call(
        body,
        out_shape=[jax.ShapeDtypeStruct((16, 32, 192), BF)]
        + [jax.ShapeDtypeStruct((n, 16, 128), BF) for n in UNITS],
        in_specs=[hbm] * 16,
        out_specs=[hbm] * 12,
        scratch_shapes=scratch,
        compiler_params=pltpu.CompilerParams(
            collective_id=0, has_side_effects=True, vmem_limit_bytes=60 * 1024 * 1024
        ),
        name="block_pair",
    )(*held, latents, cotangent)
    shapes = ((192, 576), (192, 192), (768, 384), (384, 1152), (384, 384), (384, 768))
    return tuple(
        pl.pallas_call(
            unpack,
            out_shape=[jax.ShapeDtypeStruct((1, 16, 32, 192), BF)]
            + [jax.ShapeDtypeStruct(s, F32) for s in shapes],
            in_specs=[hbm] * 12,
            out_specs=[hbm] * 7,
            scratch_shapes=[pltpu.VMEM((n, 16, 128), BF) for n in UNITS]
            + [pltpu.VMEM(s, F32) for s in shapes]
            + [pltpu.VMEM((16, 32, 192), BF), pltpu.SemaphoreType.DMA((19,))],
            compiler_params=pltpu.CompilerParams(vmem_limit_bytes=60 * 1024 * 1024),
            name="unpack",
        )(pred, *results)
    )


def solution(mesh):
    split = P(None, "rows", "cols", None)
    return jax.shard_map(
        on_device,
        mesh=mesh,
        in_specs=(split,) + (P(),) * 14 + (split,),
        out_specs=(split,) + (P(),) * 6,
        check_vma=False,
    )
```
